32 devices in a mesh: dp: 4 (over y, core), fsdp: 8 (over z, x).
Axes of the slice: x: 2, y: 2, z: 4, core: 2. Of those that a mesh axis runs over, the one named last changes fastest.
Arguments:
- hidden: bfloat16 [256, 64, 768], P(('dp', 'fsdp')), may hold values from -6 to 6
- image_feats: bfloat16 [96, 257, 1408], P(('dp', 'fsdp')), may hold values from -12 to 12
- caption_counts: int32 [32, 3], P(('dp', 'fsdp')), may hold values from 1 to 5, 8 in all within a row
- text_lengths: int32 [256], P(('dp', 'fsdp')), may hold values from 1 to 32
- out_grad: bfloat16 [256, 64, 768], P(('dp', 'fsdp')), may hold values from -6 to 6
- self_query: bfloat16 [768, 768], P('fsdp'), may hold values from -0.21875 to 0.21875
- query_bias: bfloat16 [768], P('fsdp'), may hold values from -3 to 3
- self_key: bfloat16 [768, 768], P('fsdp'), may hold values from -0.21875 to 0.21875
- self_value: bfloat16 [768, 768], P('fsdp'), may hold values from -0.21875 to 0.21875
- value_bias: bfloat16 [768], P('fsdp'), may hold values from -3 to 3
- self_output: bfloat16 [768, 768], P('fsdp'), may hold values from -0.875 to 0.875
- output_bias: bfloat16 [768], P('fsdp'), may hold values from -3 to 3
- first_gain: bfloat16 [768], P('fsdp'), may hold values from 0.099609375 to 1.8984375
- first_shift: bfloat16 [768], P('fsdp'), may hold values from -3 to 3
- cross_query: bfloat16 [768, 768], P('fsdp'), may hold values from -0.21875 to 0.21875
- crossquery_bias: bfloat16 [768], P('fsdp'), may hold values from -3 to 3
- cross_key: bfloat16 [1408, 768], P('fsdp'), may hold values from -0.15625 to 0.15625
- cross_value: bfloat16 [1408, 768], P('fsdp'), may hold values from -0.15625 to 0.15625
- crossvalue_bias: bfloat16 [768], P('fsdp'), may hold values from -3 to 3
- cross_output: bfloat16 [768, 768], P('fsdp'), may hold values from -1.75 to 1.75
- crossoutput_bias: bfloat16 [768], P('fsdp'), may hold values from -3 to 3
- second_gain: bfloat16 [768], P('fsdp'), may hold values from 0.099609375 to 1.8984375
- second_shift: bfloat16 [768], P('fsdp'), may hold values from -3 to 3
- vision_gain: bfloat16 [1408], P('fsdp'), may hold values from 0.099609375 to 1.8984375
- vision_shift: bfloat16 [1408], P('fsdp'), may hold values from -3 to 3
- expand_weight: bfloat16 [768, 3072], P(None, 'fsdp'), may hold values from -0.21875 to 0.21875
- expand_bias: bfloat16 [3072], P('fsdp'), may hold values from -3 to 3
- contract_weight: bfloat16 [3072, 768], P('fsdp'), may hold values from -0.109375 to 0.109375
- contract_bias: bfloat16 [768], P('fsdp'), may hold values from -3 to 3
- third_gain: bfloat16 [768], P('fsdp'), may hold values from 0.099609375 to 1.8984375
- third_shift: bfloat16 [768], P('fsdp'), may hold values from -3 to 3
Outputs:
- layer_out: float32 [256, 64, 768], P(('dp', 'fsdp'))
- input_grad: float32 [256, 64, 768], P(('dp', 'fsdp'))
- self_query_grad: float32 [768, 768], P('fsdp')
- query_bias_grad: float32 [768], P('fsdp')
- self_key_grad: float32 [768, 768], P('fsdp')
- self_value_grad: float32 [768, 768], P('fsdp')
- value_bias_grad: float32 [768], P('fsdp')
- self_output_grad: float32 [768, 768], P('fsdp')
- output_bias_grad: float32 [768], P('fsdp')
- first_gain_grad: float32 [768], P('fsdp')
- first_shift_grad: float32 [768], P('fsdp')
- cross_query_grad: float32 [768, 768], P('fsdp')
- crossquery_bias_grad: float32 [768], P('fsdp')
- cross_key_grad: float32 [1408, 768], P('fsdp')
- cross_value_grad: float32 [1408, 768], P('fsdp')
- crossvalue_bias_grad: float32 [768], P('fsdp')
- cross_output_grad: float32 [768, 768], P('fsdp')
- crossoutput_bias_grad: float32 [768], P('fsdp')
- second_gain_grad: float32 [768], P('fsdp')
- second_shift_grad: float32 [768], P('fsdp')
- vision_gain_grad: float32 [1408], P('fsdp')
- vision_shift_grad: float32 [1408], P('fsdp')
- expand_weight_grad: float32 [768, 3072], P(None, 'fsdp')
- expand_bias_grad: float32 [3072], P('fsdp')
- contract_weight_grad: float32 [3072, 768], P('fsdp')
- contract_bias_grad: float32 [768], P('fsdp')
- third_gain_grad: float32 [768], P('fsdp')
- third_shift_grad: float32 [768], P('fsdp')
The draws below stay inside these ranges and needn't reach their ends.
Inputs may be any that keep to these rules, and one draw needn't show every extreme that they name: `caption_counts`: each row sums to 8 and its largest entry is 5; images are shown by consecutive captions of their block in order.
All inputs are finite; a program needn't handle non-finite values.
Results may differ from the reference program's by a relative error of at most 0.025.
Values may be sent and summed in bfloat16 or wider, within the bound.
A program may use at most 192 MiB of HBM per device.

```python
import math
import jax
import jax.numpy as jnp
import numpy as np
from jax import lax

D = 768
HEADS = 12
HDIM = 64
FF = 3072
FEAT = 1408
PATCH = 257
NQ = 32
NT = 32
CAP_DEV = 8
SEQ = 64
IMG_DEV = 3
GROUPS = 32
CAPTIONS = 256
IMAGES = 96


def with_ends(values, stream_key, smallest, high):
    longest = values.shape.index(max(values.shape))
    spots = []
    for shift in (0, 1):
        where = [jax.random.randint(jax.random.fold_in(stream_key, axis), (), 0, length) for axis, length in enumerate(values.shape)]
        where[longest] = (where[longest] + shift) % values.shape[longest]
        spots.append(tuple(where))
    return values.at[spots[0]].set(smallest).at[spots[1]].set(high)


def steps_of(own_key, shape, pieces, least, top_value):
    def one(dim, blocks):
        heights = jax.random.uniform(jax.random.fold_in(jax.random.fold_in(own_key, 6), dim), (blocks,), jnp.float32, least / len(pieces), top_value / len(pieces))
        return jnp.repeat(jnp.exp(heights), shape[dim] // blocks).reshape((-1,) + (1,) * (len(shape) - dim - 1))

    loudness = one(*pieces[0])
    for cut in pieces[1:]:
        loudness = loudness * one(*cut)
    return loudness


def profile(amount, total, reach, slope):
    loads = [(1 << 20) // math.isqrt(grade ** slope) + 1 for grade in range(2, amount + 1)]
    surplus, counts = total - reach - (amount - 1), [1] * (amount - 1)
    while surplus > 0:
        movable = [i for i in range(amount - 1) if counts[i] < reach]
        pool, left = sum([loads[i] for i in movable]), surplus
        for i in movable:
            more = min(reach - counts[i], max(1, left * loads[i] // pool), surplus)
            counts[i] = counts[i] + more
            surplus = surplus - more
    return np.array([reach] + counts)


def uneven(stream_key, count, total, bound, slope):
    if count == 2:
        one = jax.random.randint(stream_key, (), max(1, total - bound), min(bound, total - 1) + 1)
        return jnp.stack([one, total - one])
    tallies = jnp.asarray(profile(count, total, bound, slope), jnp.int32)
    twos = (count - 1) // 2
    donor, sink = tallies[1:1 + 2 * twos:2], tallies[2:2 + 2 * twos:2]
    margin = jnp.minimum(donor - 1, bound - sink)
    moved = jax.random.randint(jax.random.fold_in(stream_key, 1), (twos,), 0, 1 << 20) % (margin + 1)
    tallies = tallies.at[1:1 + 2 * twos:2].set(donor - moved).at[2:2 + 2 * twos:2].set(sink + moved)
    return tallies[jax.random.permutation(jax.random.fold_in(stream_key, 2), count)]


def bell_draw(rng, extent, width, most, pieces=(), kind=jnp.bfloat16):
    gain = steps_of(rng, extent, pieces, -0.22, 0.18) if pieces else 1.0
    values = jax.random.normal(rng, extent, jnp.float32) * width * gain
    return jnp.minimum(jnp.maximum(values, -most), most).astype(kind)


def setup_inputs(seed: int = 0) -> dict:
    key_of = jax.random.split(jax.random.key(seed), 32)
    return {
        "hidden": bell_draw(key_of[0], (CAPTIONS, SEQ, D), 1.0, 6.0, ((0, 32),)),
        "image_feats": bell_draw(key_of[1], (IMAGES, PATCH, FEAT), 2.0, 12.0, ((0, 32),)),
        "caption_counts": jax.vmap(lambda own: uneven(own, IMG_DEV, CAP_DEV, 5, 2))(jax.random.split(key_of[2], GROUPS)).reshape((GROUPS, IMG_DEV)).astype(jnp.int32),
        "text_lengths": with_ends(jax.random.randint(key_of[3], (CAPTIONS,), 1, NT + 1), jax.random.fold_in(key_of[3], 1), 1, NT).astype(jnp.int32),
        "out_grad": bell_draw(key_of[4], (CAPTIONS, SEQ, D), 1.0, 6.0, ((0, 32),)),
        "self_query": bell_draw(key_of[5], (D, D), D ** -0.5, 0.21875, ((0, 8),)),
        "query_bias": bell_draw(key_of[6], (D,), 0.5, 3.0, ((0, 8),)),
        "self_key": bell_draw(key_of[7], (D, D), D ** -0.5, 0.21875, ((0, 8),)),
        "self_value": bell_draw(key_of[8], (D, D), D ** -0.5, 0.21875, ((0, 8),)),
        "value_bias": bell_draw(key_of[9], (D,), 0.5, 3.0, ((0, 8),)),
        "self_output": bell_draw(key_of[10], (D, D), (D // 16) ** -0.5, 0.875, ((0, 8),)),
        "output_bias": bell_draw(key_of[11], (D,), 0.5, 3.0, ((0, 8),)),
        "first_gain": jnp.clip(1.0 + 0.18 * jax.random.normal(key_of[12], (D,), jnp.float32), 0.099609375, 1.8984375).astype(jnp.bfloat16),
        "first_shift": bell_draw(key_of[13], (D,), 0.5, 3.0, ((0, 8),)),
        "cross_query": bell_draw(key_of[14], (D, D), D ** -0.5, 0.21875, ((0, 8),)),
        "crossquery_bias": bell_draw(key_of[15], (D,), 0.5, 3.0, ((0, 8),)),
        "cross_key": bell_draw(key_of[16], (FEAT, D), FEAT ** -0.5, 0.15625, ((0, 8),)),
        "cross_value": bell_draw(key_of[17], (FEAT, D), FEAT ** -0.5, 0.15625, ((0, 8),)),
        "crossvalue_bias": bell_draw(key_of[18], (D,), 0.5, 3.0, ((0, 8),)),
        "cross_output": bell_draw(key_of[19], (D, D), (D // 64) ** -0.5, 1.75, ((0, 8),)),
        "crossoutput_bias": bell_draw(key_of[20], (D,), 0.5, 3.0, ((0, 8),)),
        "second_gain": jnp.clip(1.0 + 0.18 * jax.random.normal(key_of[21], (D,), jnp.float32), 0.099609375, 1.8984375).astype(jnp.bfloat16),
        "second_shift": bell_draw(key_of[22], (D,), 0.5, 3.0, ((0, 8),)),
        "vision_gain": jnp.clip(1.0 + 0.18 * jax.random.normal(key_of[23], (FEAT,), jnp.float32), 0.099609375, 1.8984375).astype(jnp.bfloat16),
        "vision_shift": bell_draw(key_of[24], (FEAT,), 0.5, 3.0, ((0, 8),)),
        "expand_weight": bell_draw(key_of[25], (D, FF), D ** -0.5, 0.21875, ((1, 8),)),
        "expand_bias": bell_draw(key_of[26], (FF,), 0.5, 3.0, ((0, 8),)),
        "contract_weight": bell_draw(key_of[27], (FF, D), FF ** -0.5, 0.109375, ((0, 8),)),
        "contract_bias": bell_draw(key_of[28], (D,), 0.5, 3.0, ((0, 8),)),
        "third_gain": jnp.clip(1.0 + 0.18 * jax.random.normal(key_of[29], (D,), jnp.float32), 0.099609375, 1.8984375).astype(jnp.bfloat16),
        "third_shift": bell_draw(key_of[30], (D,), 0.5, 3.0, ((0, 8),)),
    }


EPS = 1e-06
HIGH = lax.Precision.HIGHEST

@jax.custom_vjp
def low(v):
    return lax.optimization_barrier(v.astype(jnp.bfloat16)).astype(jnp.float32)

@jax.custom_vjp
def low_back(v):
    return v

def low_keep(v):
    return (low(v), None)

def low_pass(kept, grad):
    return (grad,)

def back_keep(v):
    return (v, None)

def back_low(kept, grad):
    return (low(grad),)
low.defvjp(low_keep, low_pass)
low_back.defvjp(back_keep, back_low)

def both_ways(values):
    return low(low_back(values))

def norm_rows(values, gain_row, shift_row):
    center = values - lax.optimization_barrier(jnp.mean(values, axis=-1, keepdims=True))
    spread = lax.optimization_barrier(jnp.mean(center * center, axis=-1, keepdims=True))
    return center * lax.rsqrt(spread + EPS) * gain_row + shift_row

def softmax_rows(scores):
    row_top = lax.optimization_barrier(jnp.max(scores, axis=-1, keepdims=True))
    shifted = jnp.exp(scores - row_top)
    return shifted / lax.optimization_barrier(jnp.sum(shifted, axis=-1, keepdims=True))

def gelu_exact(values):
    return jax.nn.gelu(values, approximate=False)

def project(operand, weight):
    return jnp.einsum('...k,kn->...n', operand, weight, precision=HIGH)

def heads_of(values):
    return values.reshape(values.shape[:-1] + (HEADS, HDIM))

def caption_images(counts_row):
    bounds = jnp.cumsum(counts_row, dtype=jnp.int32)
    positions = jnp.arange(CAP_DEV, dtype=jnp.int32)
    image_index = lax.optimization_barrier(jnp.sum((positions[:, None] >= bounds[None, :]).astype(jnp.int32), axis=1, dtype=jnp.int32))
    return (image_index[:, None] == jnp.arange(IMG_DEV, dtype=jnp.int32)[None, :]).astype(jnp.float32)

def key_valid(lengths_row):
    positions = jnp.arange(SEQ, dtype=jnp.int32)[None, :]
    return jnp.logical_or(positions < NQ, positions - NQ < lengths_row[:, None])

def block_forward(params, hidden, feats, onehot, valid):
    w_query, b_query, w_key, w_value, b_value, w_out, b_out, gain_one, shift_one, w_cquery, b_cquery, w_ckey, w_cvalue, b_cvalue, w_cout, b_cout, gain_two, shift_two, gain_vision, shift_vision, w_expand, b_expand, w_contract, b_contract, gain_three, shift_three = params
    scaling = HDIM ** (-0.5)
    captions = hidden.shape[0]
    query = both_ways(project(hidden, w_query) + b_query)
    key_self = both_ways(project(hidden, w_key))
    value_self = both_ways(project(hidden, w_value) + b_value)
    scores = jnp.einsum('cqhd,ckhd->chqk', heads_of(query), heads_of(key_self), precision=HIGH) * scaling
    scores = low_back(jnp.where(valid[:, None, None, :], scores, -1000000000.0))
    probs = low(softmax_rows(scores))
    mixed = both_ways(jnp.einsum('chqk,ckhd->cqhd', probs, heads_of(value_self), precision=HIGH).reshape(captions, SEQ, D))
    branch = low_back(project(mixed, w_out) + b_out)
    first = norm_rows(hidden + branch, gain_one, shift_one)
    query_rows = first[:, :NQ]
    cross_in = low(query_rows)
    cquery = both_ways(project(cross_in, w_cquery) + b_cquery)
    expanded = jnp.einsum('ci,ipf->cpf', onehot, feats, precision=HIGH)
    vision = low(norm_rows(expanded, gain_vision, shift_vision))
    ckey = both_ways(project(vision, w_ckey))
    cvalue = both_ways(project(vision, w_cvalue) + b_cvalue)
    cscores = low_back(jnp.einsum('cqhd,ckhd->chqk', heads_of(cquery), heads_of(ckey), precision=HIGH) * scaling)
    cprobs = low(softmax_rows(cscores))
    cmixed = both_ways(jnp.einsum('chqk,ckhd->cqhd', cprobs, heads_of(cvalue), precision=HIGH).reshape(captions, NQ, D))
    cbranch = low_back(project(cmixed, w_cout) + b_cout)
    second = norm_rows(query_rows + cbranch, gain_two, shift_two)
    joined = jnp.concatenate([second, first[:, NQ:]], axis=1)
    widened = low_back(project(low(joined), w_expand) + b_expand)
    active = low(gelu_exact(widened))
    narrowed = low_back(project(active, w_contract) + b_contract)
    return norm_rows(joined + narrowed, gain_three, shift_three)

def reference(hidden, image_feats, caption_counts, text_lengths, out_grad, self_query, query_bias, self_key, self_value, value_bias, self_output, output_bias, first_gain, first_shift, cross_query, crossquery_bias, cross_key, cross_value, crossvalue_bias, cross_output, crossoutput_bias, second_gain, second_shift, vision_gain, vision_shift, expand_weight, expand_bias, contract_weight, contract_bias, third_gain, third_shift):
    params = tuple((item.astype(jnp.float32) for item in (self_query, query_bias, self_key, self_value, value_bias, self_output, output_bias, first_gain, first_shift, cross_query, crossquery_bias, cross_key, cross_value, crossvalue_bias, cross_output, crossoutput_bias, second_gain, second_shift, vision_gain, vision_shift, expand_weight, expand_bias, contract_weight, contract_bias, third_gain, third_shift)))
    groups = caption_counts.shape[0]
    blocks = (hidden.astype(jnp.float32).reshape(groups, CAP_DEV, SEQ, D), image_feats.astype(jnp.float32).reshape(groups, IMG_DEV, PATCH, FEAT), caption_counts, text_lengths.reshape(groups, CAP_DEV), out_grad.astype(jnp.float32).reshape(groups, CAP_DEV, SEQ, D))

    def step(totals, block):
        hidden_block, feats_block, counts_row, lengths_row, cotangent = block
        onehot = caption_images(counts_row)
        valid = key_valid(lengths_row)

        def forward(param_set, inputs):
            return block_forward(param_set, inputs, feats_block, onehot, valid)
        result, pullback = jax.vjp(forward, params, hidden_block)
        param_grads, input_grads = pullback(cotangent)
        totals = jax.tree.map(jnp.add, totals, param_grads)
        return (totals, (result, input_grads))
    start = tuple((jnp.zeros_like(item) for item in params))
    totals, (results, input_grads) = lax.scan(step, start, blocks)
    layer_out = results.reshape(-1, SEQ, D)
    input_grad = input_grads.reshape(-1, SEQ, D)
    return (layer_out, input_grad, totals[0], totals[1], totals[2], totals[3], totals[4], totals[5], totals[6], totals[7], totals[8], totals[9], totals[10], totals[11], totals[12], totals[13], totals[14], totals[15], totals[16], totals[17], totals[18], totals[19], totals[20], totals[21], totals[22], totals[23], totals[24], totals[25])
```

```python
import functools

import jax
import jax.numpy as jnp
from jax import lax
from jax.experimental import pallas as pl
from jax.experimental.pallas import tpu as pltpu
from jax.sharding import PartitionSpec as P

D = 768
HEADS = 12
HDIM = 64
PATCH = 257
NQ = 32
SEQ = 64
EPS = 1e-06
MASKED = -1000000000.0


def norm_rows(values, gain_row, shift_row):
    center = values - jnp.mean(values, axis=-1, keepdims=True)
    spread = jnp.mean(center * center, axis=-1, keepdims=True)
    return center * lax.rsqrt(spread + EPS) * gain_row + shift_row


def softmax_rows(scores):
    row_top = jnp.max(scores, axis=-1, keepdims=True)
    shifted = jnp.exp(scores - row_top)
    return shifted / jnp.sum(shifted, axis=-1, keepdims=True)


def gelu_exact(values):
    return jax.nn.gelu(values, approximate=False)


def project(operand, weight):
    return jnp.einsum("...k,kn->...n", operand, weight, preferred_element_type=jnp.float32)


def project_back(upstream, weight):
    return jnp.einsum("...n,kn->...k", upstream, weight, preferred_element_type=jnp.float32)


def weight_grad(operand, upstream):
    flat_operand = operand.reshape(-1, operand.shape[-1])
    flat_upstream = upstream.reshape(-1, upstream.shape[-1])
    return lax.dot_general(
        flat_operand, flat_upstream, (((0,), (0,)), ((), ())), preferred_element_type=jnp.float32
    )


def bias_grad(upstream):
    return jnp.sum(upstream.reshape(-1, upstream.shape[-1]), axis=0, dtype=jnp.float32)


def heads_of(values):
    return values.reshape(values.shape[:-1] + (HEADS, HDIM))


def as_float(values):
    return values.astype(jnp.float32)


MESH = pl.DeviceIdType.MESH
COMM_VMEM = 56 * 1024 * 1024


def place():
    dp, fs = lax.axis_index("dp"), lax.axis_index("fsdp")
    return dp // 2, dp % 2, fs // 2, fs % 2


def at_device(y, c, z, x):
    return (2 * y + c, 2 * z + x)


def rows_at(start, size):
    return pl.ds(pl.multiple_of(start, 16), size)


def greet(peers):
    barrier = pltpu.get_barrier_semaphore()
    for peer in peers:
        pl.semaphore_signal(barrier, inc=1, device_id=peer, device_id_type=MESH)
    pl.semaphore_wait(barrier, len(peers))


class Piece:
    def __init__(self, array, four, size, which, start):
        self.array, self.four, self.size, self.which, self.start = array, four, size, which, start

    def shard(self, refs, y, c):
        return refs[self.array].at[self.which(y, c), rows_at(self.start(y, c), self.size)]

    def at(self, refs, y, c, z, x):
        return refs[self.array].at[self.which(y, c), z, x, rows_at(self.start(y, c), self.size)]

    def column(self, refs, y, c, x):
        return refs[self.array].at[self.which(y, c), :, x, rows_at(self.start(y, c), self.size)]

    def every(self, refs, y, c):
        return refs[self.array].at[self.which(y, c), :, :, rows_at(self.start(y, c), self.size)]


ARRAY_ROWS = ((1, 32), (4, 96), (2, 176), (2, 96), (1, 384), (1, 384))
GATHER_PIECES = (
    Piece(0, False, 16, lambda y, c: 0, lambda y, c: 16 * c),
    Piece(1, True, 96, lambda y, c: 2 * y + c, lambda y, c: 0),
    Piece(2, True, 80, lambda y, c: y, lambda y, c: 80 * c),
    Piece(2, False, 16, lambda y, c: c, lambda y, c: 160),
    Piece(3, True, 48, lambda y, c: y, lambda y, c: 48 * c),
    Piece(4, True, 48, lambda y, c: 0, lambda y, c: 48 * (2 * y + c)),
    Piece(4, False, 96, lambda y, c: 0, lambda y, c: 192 + 96 * c),
    Piece(5, True, 48, lambda y, c: 0, lambda y, c: 48 * (2 * y + c)),
    Piece(5, False, 96, lambda y, c: 0, lambda y, c: 192 + 96 * c),
)
SUM_PIECES = (
    Piece(5, True, 48, lambda y, c: 0, lambda y, c: 48 * (2 * y + c)),
    Piece(5, False, 96, lambda y, c: 0, lambda y, c: 192 + 96 * c),
    Piece(4, True, 48, lambda y, c: 0, lambda y, c: 48 * (2 * y + c)),
    Piece(4, False, 96, lambda y, c: 0, lambda y, c: 192 + 96 * c),
    Piece(3, True, 32, lambda y, c: y, lambda y, c: 32 * c),
    Piece(3, False, 32, lambda y, c: c, lambda y, c: 64),
    Piece(2, True, 48, lambda y, c: y, lambda y, c: 48 * c),
    Piece(2, False, 80, lambda y, c: c, lambda y, c: 96),
    Piece(1, True, 48, lambda y, c: 2 * y + c, lambda y, c: 0),
    Piece(1, False, 48, lambda y, c: 2 * c, lambda y, c: 48),
    Piece(1, False, 48, lambda y, c: 2 * c + 1, lambda y, c: 48),
    Piece(0, False, 16, lambda y, c: 0, lambda y, c: 16 * c),
)


def remote(src, dst, send, recv, device):
    return pltpu.make_async_remote_copy(
        src_ref=src, dst_ref=dst, send_sem=send, recv_sem=recv, device_id=device, device_id_type=MESH
    )


def gather_kernel(*refs):
    count = len(ARRAY_ROWS)
    own, full = refs[:count], refs[count : 2 * count]
    here, zs, xs, ys, cs, zs_s, xs_s, ys_s, cs_s = refs[2 * count :]
    y, c, z, x = place()
    zp = [lax.rem(z + i, 4) for i in (1, 2, 3)]
    zm = [lax.rem(z + 4 - i, 4) for i in (1, 2, 3)]
    to_z = [at_device(y, c, p, x) for p in zp]
    to_x, to_y, to_c = at_device(y, c, z, 1 - x), at_device(1 - y, c, z, x), at_device(y, 1 - c, z, x)
    greet(to_z + [to_x, to_y, to_c])
    sent = []

    def go(*spec):
        copy = remote(*spec)
        copy.start()
        sent.append(copy)

    def arrived(dst, recv, send):
        remote(dst, dst, send, recv, to_x).wait_recv()

    locals_ = []
    for k, p in enumerate(GATHER_PIECES):
        for i in range(3):
            go(p.shard(own, y, c), p.at(full, y, c, z, x), zs_s.at[k, i], zs.at[k, i], to_z[i])
        go(p.shard(own, y, c), p.at(full, y, c, z, x), xs_s.at[k, 0], xs.at[k, 0], to_x)
        for j in range(2 if p.four else 1):
            yy = y if j == 0 else 1 - y
            copy = pltpu.make_async_copy(p.shard(own, yy, c), p.at(full, yy, c, z, x), here.at[k, j])
            copy.start()
            locals_.append(copy)
    for copy in locals_:
        copy.wait()

    def stage_x(k):
        p = GATHER_PIECES[k]
        for i in range(3):
            got = p.at(full, y, c, zm[i], x)
            arrived(got, zs.at[k, i], zs_s.at[k, i])
            go(got, got, xs_s.at[k, i + 1], xs.at[k, i + 1], to_x)

    def stage_y(k):
        p = GATHER_PIECES[k]
        arrived(p.at(full, y, c, z, 1 - x), xs.at[k, 0], xs_s.at[k, 0])
        for i in range(3):
            arrived(p.at(full, y, c, zm[i], 1 - x), xs.at[k, i + 1], xs_s.at[k, i + 1])
        if p.four:
            far = p.column(full, y, c, 1 - x)
            go(far, far, ys_s.at[k, 0], ys.at[k, 0], to_y)
            for i in range(3):
                near = p.at(full, y, c, zm[i], x)
                go(near, near, ys_s.at[k, i + 1], ys.at[k, i + 1], to_y)
        mine = p.every(full, y, c)
        go(mine, mine, cs_s.at[k, 0], cs.at[k, 0], to_c)

    def stage_c(k):
        p = GATHER_PIECES[k]
        if p.four:
            arrived(p.column(full, 1 - y, c, 1 - x), ys.at[k, 0], ys_s.at[k, 0])
            for i in range(3):
                arrived(p.at(full, 1 - y, c, zm[i], x), ys.at[k, i + 1], ys_s.at[k, i + 1])
            mine = p.every(full, 1 - y, c)
            go(mine, mine, cs_s.at[k, 1], cs.at[k, 1], to_c)

    def finish(k):
        p = GATHER_PIECES[k]
        arrived(p.every(full, y, 1 - c), cs.at[k, 0], cs_s.at[k, 0])
        if p.four:
            arrived(p.every(full, 1 - y, 1 - c), cs.at[k, 1], cs_s.at[k, 1])

    total = len(GATHER_PIECES)
    for t in range(total + 3):
        for lag, stage in enumerate((stage_x, stage_y, stage_c, finish)):
            if 0 <= t - lag < total:
                stage(t - lag)
    for copy in sent:
        copy.wait_send()


def gather_all(shards):
    total = len(GATHER_PIECES)
    return pl.pallas_call(
        gather_kernel,
        out_shape=[
            jax.ShapeDtypeStruct((count, 4, 2, rows, D), jnp.bfloat16) for count, rows in ARRAY_ROWS
        ],
        in_specs=[pl.BlockSpec(memory_space=pl.ANY)] * len(ARRAY_ROWS),
        out_specs=[pl.BlockSpec(memory_space=pl.ANY)] * len(ARRAY_ROWS),
        scratch_shapes=[
            pltpu.SemaphoreType.DMA((total, 2)),
            pltpu.SemaphoreType.DMA((total, 3)),
            pltpu.SemaphoreType.DMA((total, 4)),
            pltpu.SemaphoreType.DMA((total, 4)),
            pltpu.SemaphoreType.DMA((total, 2)),
            pltpu.SemaphoreType.DMA((total, 3)),
            pltpu.SemaphoreType.DMA((total, 4)),
            pltpu.SemaphoreType.DMA((total, 4)),
            pltpu.SemaphoreType.DMA((total, 2)),
        ],
        compiler_params=pltpu.CompilerParams(collective_id=0, has_side_effects=True),
        cost_estimate=pl.CostEstimate(flops=0, bytes_accessed=100_000_000, transcendentals=0),
    )(*shards)


def add_pieces(target, other, lead):
    def step(i, carry):
        target[i] = target[i] + other[i]
        return carry

    lax.fori_loop(0, lead, step, 0)


def sum_kernel(*refs):
    count, total = len(ARRAY_ROWS), len(SUM_PIECES)
    grads, outs = refs[:count], refs[count : 2 * count]
    refs = refs[2 * count :]
    mine, from_c, from_y, from_x, from_z, last = (refs[i * total : (i + 1) * total] for i in range(6))
    here, done, cs, ys, xs, zs, fs, cs_s, ys_s, xs_s, zs_s, fs_s = refs[6 * total :]
    y, c, z, x = place()
    zp = [lax.rem(z + i, 4) for i in (1, 2, 3)]
    to_z = [at_device(y, c, p, x) for p in zp]
    to_x, to_y, to_c = at_device(y, c, z, 1 - x), at_device(1 - y, c, z, x), at_device(y, 1 - c, z, x)
    to_d = at_device(1 - y, 1 - c, z, x)
    greet(to_z + [to_x, to_y, to_c, to_d])
    sent, stored = [], []

    def go(*spec):
        copy = remote(*spec)
        copy.start()
        sent.append(copy)

    def arrived(dst, recv, send):
        remote(dst, dst, send, recv, to_x).wait_recv()

    def sides(p):
        return (y, 1 - y) if p.four else (y,)

    local = []
    for k, p in enumerate(SUM_PIECES):
        for j, yy in enumerate(sides(p)):
            copy = pltpu.make_async_copy(p.every(grads, yy, c), mine[k].at[j], here.at[k, j])
            copy.start()
            local.append((k, copy))
            go(p.every(grads, yy, 1 - c), from_c[k].at[j], cs_s.at[k, j], cs.at[k, j], to_c)

    def stage_c(k):
        p = SUM_PIECES[k]
        for kk, copy in local:
            if kk == k:
                copy.wait()
        for j in reversed(range(len(sides(p)))):
            arrived(from_c[k].at[j], cs.at[k, j], cs_s.at[k, j])
            for i in range(4):
                for l in range(2):
                    mine[k][j, i, l] = mine[k][j, i, l] + from_c[k][j, i, l]
            if j == 1:
                go(mine[k].at[1], from_y[k], ys_s.at[k], ys.at[k], to_y)

    def stage_y(k):
        p = SUM_PIECES[k]
        if p.four:
            arrived(from_y[k], ys.at[k], ys_s.at[k])
            for i in range(4):
                for l in range(2):
                    mine[k][0, i, l] = mine[k][0, i, l] + from_y[k][i, l]
        go(mine[k].at[0, :, 1 - x], from_x[k], xs_s.at[k], xs.at[k], to_x)

    def stage_x(k):
        arrived(from_x[k], xs.at[k], xs_s.at[k])
        for i in range(4):
            from_x[k][i] = from_x[k][i] + mine[k][0, i, x]
        for i in range(3):
            go(from_x[k].at[zp[i]], from_z[k].at[i], zs_s.at[k, i], zs.at[k, i], to_z[i])

    def stage_z(k):
        p = SUM_PIECES[k]
        for i in range(3):
            arrived(from_z[k].at[i], zs.at[k, i], zs_s.at[k, i])
        value = from_x[k][z].astype(jnp.float32)
        for i in range(3):
            value = value + from_z[k][i].astype(jnp.float32)
        last[k][0] = value.astype(jnp.bfloat16)
        if p.four:
            go(last[k].at[0], last[k].at[1], fs_s.at[k, 0], fs.at[k, 0], to_y)
            go(last[k].at[0], last[k].at[2], fs_s.at[k, 1], fs.at[k, 1], to_c)
            go(last[k].at[0], last[k].at[3], fs_s.at[k, 2], fs.at[k, 2], to_d)
        else:
            go(last[k].at[0], last[k].at[1], fs_s.at[k, 0], fs.at[k, 0], to_y)

    def put(k, j, slot, yy, cc):
        copy = pltpu.make_async_copy(last[k].at[slot], SUM_PIECES[k].shard(outs, yy, cc), done.at[k, j])
        copy.start()
        stored.append(copy)

    def stage_f(k):
        p = SUM_PIECES[k]
        if p.four:
            put(k, 0, 0, y, c)
            for j, (yy, cc) in enumerate(((1 - y, c), (y, 1 - c), (1 - y, 1 - c))):
                arrived(last[k].at[j + 1], fs.at[k, j], fs_s.at[k, j])
                put(k, j + 1, j + 1, yy, cc)
        else:
            arrived(last[k].at[1], fs.at[k, 0], fs_s.at[k, 0])
            last[k][2] = last[k][0] + last[k][1]
            go(last[k].at[2], last[k].at[3], fs_s.at[k, 1], fs.at[k, 1], to_c)
            put(k, 0, 2, y, c)

    def stage_g(k):
        p = SUM_PIECES[k]
        if not p.four:
            arrived(last[k].at[3], fs.at[k, 1], fs_s.at[k, 1])
            put(k, 1, 3, y, 1 - c)

    stages = (stage_c, stage_y, stage_x, stage_z, stage_f, stage_g)
    for t in range(total + len(stages) - 1):
        for lag, stage in enumerate(stages):
            if 0 <= t - lag < total:
                stage(t - lag)
    for copy in sent:
        copy.wait_send()
    for copy in stored:
        copy.wait()


def sum_all(grads):
    total = len(SUM_PIECES)
    low = jnp.bfloat16
    sides = [2 if p.four else 1 for p in SUM_PIECES]
    sizes = [p.size for p in SUM_PIECES]
    dma = pltpu.SemaphoreType.DMA
    return pl.pallas_call(
        sum_kernel,
        out_shape=[jax.ShapeDtypeStruct((count, rows, D), low) for count, rows in ARRAY_ROWS],
        in_specs=[pl.BlockSpec(memory_space=pl.ANY)] * len(ARRAY_ROWS),
        out_specs=[pl.BlockSpec(memory_space=pl.ANY)] * len(ARRAY_ROWS),
        scratch_shapes=[pltpu.VMEM((s, 4, 2, n, D), low) for s, n in zip(sides, sizes)]
        + [pltpu.VMEM((s, 4, 2, n, D), low) for s, n in zip(sides, sizes)]
        + [pltpu.VMEM((4, 2, n, D) if s == 2 else (1, 1, 16, D), low) for s, n in zip(sides, sizes)]
        + [pltpu.VMEM((4, n, D), low) for n in sizes]
        + [pltpu.VMEM((3, n, D), low) for n in sizes]
        + [pltpu.VMEM((4, n, D), low) for n in sizes]
        + [
            dma((total, 2)),
            dma((total, 4)),
            dma((total, 2)),
            dma((total,)),
            dma((total,)),
            dma((total, 3)),
            dma((total, 3)),
            dma((total, 2)),
            dma((total,)),
            dma((total,)),
            dma((total, 3)),
            dma((total, 3)),
        ],
        compiler_params=pltpu.CompilerParams(
            collective_id=1, has_side_effects=True, vmem_limit_bytes=COMM_VMEM
        ),
        cost_estimate=pl.CostEstimate(flops=0, bytes_accessed=100_000_000, transcendentals=0),
    )(*grads)


def pack_rows(vectors):
    rows = [jnp.pad(v, (0, D - v.shape[0])) for v in vectors]
    rows += [jnp.zeros((D,), rows[0].dtype)] * (32 - len(rows))
    return jnp.stack(rows)[None]


def gather_shards(fast, shards):
    if fast:
        return gather_all(shards)
    return [lax.all_gather(s, "fsdp", axis=1, tiled=False) for s in shards]


def sum_shards(fast, grads):
    if fast:
        return sum_all([g.reshape(g.shape[0], 4, 2, g.shape[2], D) for g in grads])
    owned = [lax.psum_scatter(g, "fsdp", scatter_dimension=1, tiled=False) for g in grads]
    return [lax.psum(g, "dp") for g in owned]


def local(
    fast,
    hidden,
    image_feats,
    caption_counts,
    text_lengths,
    out_grad,
    self_query,
    query_bias,
    self_key,
    self_value,
    value_bias,
    self_output,
    output_bias,
    first_gain,
    first_shift,
    cross_query,
    crossquery_bias,
    cross_key,
    cross_value,
    crossvalue_bias,
    cross_output,
    crossoutput_bias,
    second_gain,
    second_shift,
    vision_gain,
    vision_shift,
    expand_weight,
    expand_bias,
    contract_weight,
    contract_bias,
    third_gain,
    third_shift,
):
    low = jnp.bfloat16
    vectors = (
        query_bias,
        value_bias,
        output_bias,
        first_gain,
        first_shift,
        crossquery_bias,
        crossvalue_bias,
        crossoutput_bias,
        second_gain,
        second_shift,
        contract_bias,
        third_gain,
        third_shift,
        vision_gain,
        vision_shift,
        expand_bias,
    )
    full = gather_shards(
        fast,
        (
            pack_rows(vectors),
            jnp.stack([self_query, self_key, self_value, self_output]),
            jnp.stack([cross_key, cross_value]),
            jnp.stack([cross_query, cross_output]),
            expand_weight.T[None],
            contract_weight[None],
        ),
    )
    rows = full[0].reshape(-1, 32, D)
    shards = rows.shape[0]
    (
        b_query,
        b_value,
        b_out,
        gain_one,
        shift_one,
        b_cquery,
        b_cvalue,
        b_cout,
        gain_two,
        shift_two,
        b_contract,
        gain_three,
        shift_three,
        gain_vision,
        shift_vision,
        b_expand,
    ) = (as_float(rows[:, i, : v.shape[0]].reshape(-1)) for i, v in enumerate(vectors))
    w_query, w_key, w_value, w_out = full[1].reshape(4, D, D)
    feat = image_feats.shape[-1]
    w_ckey, w_cvalue = full[2].reshape(2, feat, D)
    w_cquery, w_cout = full[3].reshape(2, D, D)
    w_expand_t = full[4].reshape(-1, D)
    w_contract = full[5].reshape(-1, D)

    scaling = HDIM ** (-0.5)
    captions = hidden.shape[0]
    images = image_feats.shape[0]
    bounds = jnp.cumsum(caption_counts[0], dtype=jnp.int32)
    positions = jnp.arange(captions, dtype=jnp.int32)
    image_index = jnp.sum(
        (positions[:, None] >= bounds[None, :]).astype(jnp.int32), axis=1, dtype=jnp.int32
    )
    row_image = jnp.repeat(image_index, NQ)
    key_image = jnp.repeat(jnp.arange(images, dtype=jnp.int32), PATCH)
    shown = row_image[:, None] == key_image[None, :]
    slots = jnp.arange(SEQ, dtype=jnp.int32)[None, :]
    key_valid = jnp.logical_or(slots < NQ, slots - NQ < text_lengths[:, None])
    query_low = (project(hidden, w_query) + b_query).astype(low)
    key_low = project(hidden, w_key).astype(low)
    value_low = (project(hidden, w_value) + b_value).astype(low)
    scores = (
        jnp.einsum(
            "cqhd,ckhd->chqk",
            heads_of(query_low),
            heads_of(key_low),
            preferred_element_type=jnp.float32,
        )
        * scaling
    )
    scores = jnp.where(key_valid[:, None, None, :], scores, MASKED)
    probs, soft_back = jax.vjp(softmax_rows, scores)
    probs_low = probs.astype(low)
    mixed_low = (
        jnp.einsum(
            "chqk,ckhd->cqhd", probs_low, heads_of(value_low), preferred_element_type=jnp.float32
        )
        .reshape(captions, SEQ, D)
        .astype(low)
    )
    branch = project(mixed_low, w_out) + b_out
    first, norm_back_one = jax.vjp(norm_rows, as_float(hidden) + branch, gain_one, shift_one)
    query_rows = first[:, :NQ]
    cross_in = query_rows.astype(low)
    cquery_low = (project(cross_in, w_cquery) + b_cquery).astype(low).reshape(-1, D)
    vision_vals, vision_back = jax.vjp(
        norm_rows, as_float(image_feats.reshape(-1, feat)), gain_vision, shift_vision
    )
    vision_low = vision_vals.astype(low)
    ckey_low = project(vision_low, w_ckey).astype(low)
    cvalue_low = (project(vision_low, w_cvalue) + b_cvalue).astype(low)
    cscores = (
        jnp.einsum(
            "qhd,khd->hqk",
            heads_of(cquery_low),
            heads_of(ckey_low),
            preferred_element_type=jnp.float32,
        )
        * scaling
    )
    cscores = jnp.where(shown[None], cscores, -jnp.inf)
    cprobs, csoft_back = jax.vjp(softmax_rows, cscores)
    cprobs_low = cprobs.astype(low)
    cmixed_low = (
        jnp.einsum(
            "hqk,khd->qhd", cprobs_low, heads_of(cvalue_low), preferred_element_type=jnp.float32
        )
        .reshape(captions, NQ, D)
        .astype(low)
    )
    cbranch = project(cmixed_low, w_cout) + b_cout
    second, norm_back_two = jax.vjp(norm_rows, query_rows + cbranch, gain_two, shift_two)
    joined = jnp.concatenate([second, first[:, NQ:]], axis=1)
    joined_low = joined.astype(low)
    widened = project_back(joined_low, w_expand_t) + b_expand
    active, gelu_back = jax.vjp(gelu_exact, widened)
    active_low = active.astype(low)
    narrowed = project(active_low, w_contract) + b_contract
    layer_out, norm_back_three = jax.vjp(norm_rows, joined + narrowed, gain_three, shift_three)

    grad_three_in, grad_gain_three, grad_shift_three = norm_back_three(as_float(out_grad))
    grad_narrow = grad_three_in.astype(low)
    grad_w_contract = weight_grad(active_low, grad_narrow)
    grad_b_contract = bias_grad(grad_narrow)
    (grad_wide,) = gelu_back(project_back(grad_narrow, w_contract))
    grad_wide_low = grad_wide.astype(low)
    grad_w_expand_t = weight_grad(grad_wide_low, joined_low)
    grad_b_expand = bias_grad(grad_wide_low)
    grad_joined = grad_three_in + project(grad_wide_low, w_expand_t)
    grad_two_in, grad_gain_two, grad_shift_two = norm_back_two(grad_joined[:, :NQ])
    grad_cbranch = grad_two_in.astype(low)
    grad_w_cout = weight_grad(cmixed_low, grad_cbranch)
    grad_b_cout = bias_grad(grad_cbranch)
    grad_cmixed = heads_of(project_back(grad_cbranch, w_cout).astype(low).reshape(-1, D))
    grad_cprobs = jnp.einsum(
        "qhd,khd->hqk", grad_cmixed, heads_of(cvalue_low), preferred_element_type=jnp.float32
    )
    grad_cvalue = (
        jnp.einsum("hqk,qhd->khd", cprobs_low, grad_cmixed, preferred_element_type=jnp.float32)
        .reshape(-1, D)
        .astype(low)
    )
    (grad_cscores,) = csoft_back(grad_cprobs)
    grad_cscores_low = grad_cscores.astype(low)
    grad_cquery = (
        (
            jnp.einsum(
                "hqk,khd->qhd",
                grad_cscores_low,
                heads_of(ckey_low),
                preferred_element_type=jnp.float32,
            )
            * scaling
        )
        .reshape(captions, NQ, D)
        .astype(low)
    )
    grad_ckey = (
        (
            jnp.einsum(
                "hqk,qhd->khd",
                grad_cscores_low,
                heads_of(cquery_low),
                preferred_element_type=jnp.float32,
            )
            * scaling
        )
        .reshape(-1, D)
        .astype(low)
    )
    grad_w_cquery = weight_grad(cross_in, grad_cquery)
    grad_b_cquery = bias_grad(grad_cquery)
    key_term = weight_grad(vision_low, grad_ckey)
    value_term = weight_grad(vision_low, grad_cvalue)
    value_bias_term = bias_grad(grad_cvalue)
    rows_grad = project_back(grad_ckey, w_ckey) + project_back(grad_cvalue, w_cvalue)
    unused_feats, grad_gain_vision, grad_shift_vision = vision_back(rows_grad)
    grad_first = jnp.concatenate(
        [grad_two_in + project_back(grad_cquery, w_cquery), grad_joined[:, NQ:]], axis=1
    )
    grad_one_in, grad_gain_one, grad_shift_one = norm_back_one(grad_first)
    grad_branch = grad_one_in.astype(low)
    grad_w_out = weight_grad(mixed_low, grad_branch)
    grad_b_out = bias_grad(grad_branch)
    grad_mixed = heads_of(project_back(grad_branch, w_out).astype(low))
    grad_probs = jnp.einsum(
        "cqhd,ckhd->chqk", grad_mixed, heads_of(value_low), preferred_element_type=jnp.float32
    )
    grad_value = (
        jnp.einsum("chqk,cqhd->ckhd", probs_low, grad_mixed, preferred_element_type=jnp.float32)
        .reshape(captions, SEQ, D)
        .astype(low)
    )
    (grad_scores,) = soft_back(grad_probs)
    grad_scores_low = grad_scores.astype(low)
    grad_query = (
        (
            jnp.einsum(
                "chqk,ckhd->cqhd",
                grad_scores_low,
                heads_of(key_low),
                preferred_element_type=jnp.float32,
            )
            * scaling
        )
        .reshape(captions, SEQ, D)
        .astype(low)
    )
    grad_key = (
        (
            jnp.einsum(
                "chqk,cqhd->ckhd",
                grad_scores_low,
                heads_of(query_low),
                preferred_element_type=jnp.float32,
            )
            * scaling
        )
        .reshape(captions, SEQ, D)
        .astype(low)
    )
    grad_w_query = weight_grad(hidden, grad_query)
    grad_b_query = bias_grad(grad_query)
    grad_w_key = weight_grad(hidden, grad_key)
    grad_w_value = weight_grad(hidden, grad_value)
    grad_b_value = bias_grad(grad_value)
    input_grad = (
        grad_one_in
        + project_back(grad_query, w_query)
        + project_back(grad_key, w_key)
        + project_back(grad_value, w_value)
    )
    vector_grads = (
        grad_b_query,
        grad_b_value,
        grad_b_out,
        grad_gain_one,
        grad_shift_one,
        grad_b_cquery,
        value_bias_term,
        grad_b_cout,
        grad_gain_two,
        grad_shift_two,
        grad_b_contract,
        grad_gain_three,
        grad_shift_three,
        grad_gain_vision,
        grad_shift_vision,
        grad_b_expand,
    )
    packed = jnp.stack(
        [
            jnp.pad(v.astype(low).reshape(shards, -1), ((0, 0), (0, D - v.shape[0] // shards)))
            for v in vector_grads
        ]
        + [jnp.zeros((shards, D), low)] * (32 - len(vector_grads)),
        axis=1,
    )

    def cut(*parts):
        return jnp.stack([p.astype(low).reshape(shards, -1, D) for p in parts])

    summed = sum_shards(
        fast,
        (
            packed[None],
            cut(grad_w_query, grad_w_key, grad_w_value, grad_w_out),
            cut(key_term, value_term),
            cut(grad_w_cquery, grad_w_cout),
            cut(grad_w_expand_t),
            cut(grad_w_contract),
        ),
    )
    sums = [as_float(s) for s in summed]
    vec = [sums[0][0, i, : v.shape[0]] for i, v in enumerate(vectors)]
    return (
        layer_out,
        input_grad,
        sums[1][0],
        vec[0],
        sums[1][1],
        sums[1][2],
        vec[1],
        sums[1][3],
        vec[2],
        vec[3],
        vec[4],
        sums[3][0],
        vec[5],
        sums[2][0],
        sums[2][1],
        vec[6],
        sums[3][1],
        vec[7],
        vec[8],
        vec[9],
        vec[13],
        vec[14],
        sums[4][0].T,
        vec[15],
        sums[5][0],
        vec[10],
        vec[11],
        vec[12],
    )


def solution(mesh):
    placed = (
        P(("dp", "fsdp"), None, None),
        P(("dp", "fsdp"), None, None),
        P(("dp", "fsdp"), None),
        P(("dp", "fsdp")),
        P(("dp", "fsdp"), None, None),
        P("fsdp", None),
        P("fsdp"),
        P("fsdp", None),
        P("fsdp", None),
        P("fsdp"),
        P("fsdp", None),
        P("fsdp"),
        P("fsdp"),
        P("fsdp"),
        P("fsdp", None),
        P("fsdp"),
        P("fsdp", None),
        P("fsdp", None),
        P("fsdp"),
        P("fsdp", None),
        P("fsdp"),
        P("fsdp"),
        P("fsdp"),
        P("fsdp"),
        P("fsdp"),
        P(None, "fsdp"),
        P("fsdp"),
        P("fsdp", None),
        P("fsdp"),
        P("fsdp"),
        P("fsdp"),
    )
    fast = mesh.shape["dp"] == 4 and mesh.shape["fsdp"] == 8
    return jax.shard_map(
        functools.partial(local, fast),
        mesh=mesh,
        in_specs=placed,
        out_specs=(
            P(("dp", "fsdp"), None, None),
            P(("dp", "fsdp"), None, None),
            P("fsdp", None),
            P("fsdp"),
            P("fsdp", None),
            P("fsdp", None),
            P("fsdp"),
            P("fsdp", None),
            P("fsdp"),
            P("fsdp"),
            P("fsdp"),
            P("fsdp", None),
            P("fsdp"),
            P("fsdp", None),
            P("fsdp", None),
            P("fsdp"),
            P("fsdp", None),
            P("fsdp"),
            P("fsdp"),
            P("fsdp"),
            P("fsdp"),
            P("fsdp"),
            P(None, "fsdp"),
            P("fsdp"),
            P("fsdp", None),
            P("fsdp"),
            P("fsdp"),
            P("fsdp"),
        ),
        check_vma=False,
    )
```

```python
import functools
import typing

import jax
import jax.numpy as jnp
from jax import lax
from jax.experimental import pallas as pl
from jax.experimental.pallas import tpu as pltpu
from jax.sharding import PartitionSpec as P

D = 768
HEADS = 12
HDIM = 64
PATCH = 257
NQ = 32
SEQ = 64
EPS = 1e-06
MASKED = -1000000000.0


MESH = pl.DeviceIdType.MESH
DP, FSDP = "dp", "fsdp"
SHARD_LANES = 96


def place():
    dp, fs = lax.axis_index(DP), lax.axis_index(FSDP)
    return dp // 2, dp % 2, fs // 2, fs % 2


def at_device(y, c, z, x):
    return (2 * y + c, 2 * z + x)


def rows_at(start, size):
    return pl.ds(pl.multiple_of(start, 16), size)


def greet(peers):
    barrier = pltpu.get_barrier_semaphore()
    for peer in peers:
        pl.semaphore_signal(barrier, inc=1, device_id=peer, device_id_type=MESH)
    pl.semaphore_wait(barrier, len(peers))


class Piece:
    def __init__(self, array, four, size, which, start):
        self.array, self.four, self.size, self.which, self.start = array, four, size, which, start

    def shard(self, refs, y, c):
        return refs[self.array].at[self.which(y, c), rows_at(self.start(y, c), self.size)]

    def at(self, refs, y, c, z, x):
        return refs[self.array].at[self.which(y, c), z, x, rows_at(self.start(y, c), self.size)]

    def column(self, refs, y, c, x):
        return refs[self.array].at[self.which(y, c), :, x, rows_at(self.start(y, c), self.size)]

    def every(self, refs, y, c):
        return refs[self.array].at[self.which(y, c), :, :, rows_at(self.start(y, c), self.size)]


ARRAY_ROWS = ((1, 32), (4, 96), (2, 176), (2, 96), (1, 384), (1, 384))


def corner(array, start):
    return Piece(array, True, 48, lambda y, c: 0, lambda y, c: start + 48 * (2 * y + c))


def halved(array, start):
    return Piece(array, False, 48, lambda y, c: 0, lambda y, c: start + 48 * c)


GATHER_PIECES = (
    Piece(1, True, 32, lambda y, c: 2 * y + c, lambda y, c: 0),
    Piece(1, True, 32, lambda y, c: 2 * y + c, lambda y, c: 32),
    Piece(1, True, 32, lambda y, c: 2 * y + c, lambda y, c: 64),
    Piece(2, True, 48, lambda y, c: y, lambda y, c: 80 * c),
    Piece(2, True, 32, lambda y, c: y, lambda y, c: 80 * c + 48),
    Piece(2, False, 16, lambda y, c: c, lambda y, c: 160),
    Piece(3, True, 48, lambda y, c: y, lambda y, c: 48 * c),
    corner(4, 0),
    halved(4, 192),
    halved(4, 288),
    corner(5, 0),
    halved(5, 192),
    halved(5, 288),
)
GATHER_AHEAD = 3
GATHER_LAGS = (0, 1, 3, 4)
GATHER_SLOTS = len(GATHER_PIECES) + GATHER_LAGS[-1]


def remote(src, dst, send, recv, device):
    return pltpu.make_async_remote_copy(
        src_ref=src, dst_ref=dst, send_sem=send, recv_sem=recv, device_id=device, device_id_type=MESH
    )


class Gather:
    def __init__(self, own, full, sems):
        self.own, self.full = own, full
        self.here, self.vs, self.zs, self.xs, self.ys, self.cs = sems[:6]
        self.vs_s, self.zs_s, self.xs_s, self.ys_s, self.cs_s = sems[6:]
        y, c, z, x = self.me = place()
        self.zp = [lax.rem(z + i, 4) for i in (1, 2, 3)]
        self.zm = [lax.rem(z + 4 - i, 4) for i in (1, 2, 3)]
        self.to_z = [at_device(y, c, p, x) for p in self.zp]
        self.to_diag = [at_device(y, c, p, 1 - x) for p in self.zp]
        self.to_x, self.to_y = at_device(y, c, z, 1 - x), at_device(1 - y, c, z, x)
        self.to_c = at_device(y, 1 - c, z, x)
        self.sent, self.slot_at = [], 0
        greet(self.to_z + self.to_diag + [self.to_x, self.to_y, self.to_c])

    def go(self, *spec):
        copy = remote(*spec)
        copy.start()
        self.sent.append(copy)

    def arrived(self, dst, recv, send):
        remote(dst, dst, send, recv, self.to_x).wait_recv()

    def start(self):
        y, c, z, x = self.me
        mine = self.full[0].at[0, z, x]
        for i, device in enumerate(self.to_z + self.to_diag + [self.to_x]):
            self.go(self.own[0].at[0], mine, self.vs_s.at[i], self.vs.at[i], device)
        self.locals = [pltpu.make_async_copy(self.own[0].at[0], mine, self.here.at[0, 0])]
        for k in range(GATHER_AHEAD):
            self.send(k)
        for k, p in enumerate(GATHER_PIECES):
            for j in range(2 if p.four else 1):
                yy = y if j == 0 else 1 - y
                self.locals.append(
                    pltpu.make_async_copy(
                        p.shard(self.own, yy, c), p.at(self.full, yy, c, z, x), self.here.at[k + 1, j]
                    )
                )
        for copy in self.locals:
            copy.start()
        for copy in self.locals:
            copy.wait()

    def vectors(self):
        y, c, z, x = self.me
        places = [(m, x) for m in self.zm] + [(m, 1 - x) for m in self.zm] + [(z, 1 - x)]
        for i, (zz, xx) in enumerate(places):
            self.arrived(self.full[0].at[0, zz, xx], self.vs.at[i], self.vs_s.at[i])

    def send(self, k):
        y, c, z, x = self.me
        p = GATHER_PIECES[k]
        src, dst = p.shard(self.own, y, c), p.at(self.full, y, c, z, x)
        for i in range(3):
            self.go(src, dst, self.zs_s.at[k, i], self.zs.at[k, i], self.to_z[i])
        self.go(src, dst, self.xs_s.at[k, 0], self.xs.at[k, 0], self.to_x)

    def stage_x(self, k):
        y, c, z, x = self.me
        p = GATHER_PIECES[k]
        for i in range(3):
            got = p.at(self.full, y, c, self.zm[i], x)
            self.arrived(got, self.zs.at[k, i], self.zs_s.at[k, i])
            self.go(got, got, self.xs_s.at[k, i + 1], self.xs.at[k, i + 1], self.to_x)

    def stage_y(self, k):
        y, c, z, x = self.me
        p = GATHER_PIECES[k]
        self.arrived(p.at(self.full, y, c, z, 1 - x), self.xs.at[k, 0], self.xs_s.at[k, 0])
        for i in range(3):
            got = p.at(self.full, y, c, self.zm[i], 1 - x)
            self.arrived(got, self.xs.at[k, i + 1], self.xs_s.at[k, i + 1])
        if p.four:
            far = p.column(self.full, y, c, 1 - x)
            self.go(far, far, self.ys_s.at[k, 0], self.ys.at[k, 0], self.to_y)
            for i in range(3):
                near = p.at(self.full, y, c, self.zm[i], x)
                self.go(near, near, self.ys_s.at[k, i + 1], self.ys.at[k, i + 1], self.to_y)
        mine = p.every(self.full, y, c)
        self.go(mine, mine, self.cs_s.at[k, 0], self.cs.at[k, 0], self.to_c)

    def stage_c(self, k):
        y, c, z, x = self.me
        p = GATHER_PIECES[k]
        if p.four:
            got = p.column(self.full, 1 - y, c, 1 - x)
            self.arrived(got, self.ys.at[k, 0], self.ys_s.at[k, 0])
            for i in range(3):
                got = p.at(self.full, 1 - y, c, self.zm[i], x)
                self.arrived(got, self.ys.at[k, i + 1], self.ys_s.at[k, i + 1])
            mine = p.every(self.full, 1 - y, c)
            self.go(mine, mine, self.cs_s.at[k, 1], self.cs.at[k, 1], self.to_c)

    def finish(self, k):
        y, c, z, x = self.me
        p = GATHER_PIECES[k]
        self.arrived(p.every(self.full, y, 1 - c), self.cs.at[k, 0], self.cs_s.at[k, 0])
        if p.four:
            self.arrived(p.every(self.full, 1 - y, 1 - c), self.cs.at[k, 1], self.cs_s.at[k, 1])

    def advance(self, slots):
        total = len(GATHER_PIECES)
        while self.slot_at < min(slots, GATHER_SLOTS):
            t = self.slot_at
            if GATHER_AHEAD <= t + GATHER_AHEAD < total:
                self.send(t + GATHER_AHEAD)
            stages = (self.stage_x, self.stage_y, self.stage_c, self.finish)
            for lag, stage in zip(GATHER_LAGS, stages):
                if 0 <= t - lag < total:
                    stage(t - lag)
            self.slot_at += 1

    def need(self, k):
        self.advance(k + GATHER_LAGS[-1] + 1)

    def end(self):
        for copy in self.sent:
            copy.wait_send()


def gather_semaphores():
    total, dma = len(GATHER_PIECES), pltpu.SemaphoreType.DMA
    pairs = [dma((7,)), dma((total, 3)), dma((total, 4)), dma((total, 4)), dma((total, 2))]
    return [dma((total + 1, 2))] + pairs + pairs


LOW = jnp.bfloat16
F32 = jnp.float32
KEYS = 272
SCALE = HDIM**-0.5
NN = (((1,), (0,)), ((), ()))
NT = (((1,), (1,)), ((), ()))
TN = (((0,), (0,)), ((), ()))


def mm(a, b, dims=NN):
    return lax.dot_general(a, b, dims, preferred_element_type=F32)


def erf_of(v):
    v = jnp.clip(v, -3.832506856900711, 3.832506856900711)
    s = v * v
    top = jnp.full_like(s, 0.00022905065861350646)
    for k in (0.0034082910107109506, 0.050955695062380861, 0.18520832239976145, 1.128379143519084):
        top = top * s + k
    low = jnp.full_like(s, -1.1791602954361697e-7)
    for k in (0.000023547966471313185, 0.0010179625278914885, 0.014070470171167667, 0.11098505178285362, 0.49746925110067538, 1.0):
        low = low * s + k
    return v * top / low


def norm_parts(v):
    center = v - jnp.mean(v, axis=-1, keepdims=True)
    r = lax.rsqrt(jnp.mean(center * center, axis=-1, keepdims=True) + EPS)
    return center * r, r


def norm_back(dy, xhat, r, gain):
    gdy = gain * dy
    return r * (
        gdy
        - jnp.mean(gdy, axis=-1, keepdims=True)
        - xhat * jnp.mean(gdy * xhat, axis=-1, keepdims=True)
    )


def pair_lanes(v):
    lane = lax.broadcasted_iota(jnp.int32, v.shape, 1)
    zero = jnp.zeros_like(v)
    return jnp.concatenate([jnp.where(lane < HDIM, v, zero), jnp.where(lane < HDIM, zero, v)], axis=0)


def unpair(t):
    n = t.shape[1] // 2
    return jnp.concatenate([t[:HDIM, :n], t[HDIM:, n:]], axis=0).T


def self_mask(lengths, g):
    key = lax.broadcasted_iota(jnp.int32, (128, 256), 0)
    query = lax.broadcasted_iota(jnp.int32, (128, 256), 1) % 128
    late = key >= SEQ
    limit = jnp.where(late, lengths[2 * g + 1], lengths[2 * g]) + NQ
    slot = jnp.where(late, key - SEQ, key)
    return jnp.logical_and(late == (query >= SEQ), slot < limit)


def cross_mask(counts, rows, images):
    shape = (images * KEYS, 2 * rows)
    key = lax.broadcasted_iota(jnp.int32, shape, 0)
    caption = (lax.broadcasted_iota(jnp.int32, (1, 2 * rows), 1) % rows) // NQ
    shows = jnp.zeros_like(caption)
    total = 0
    for i in range(images):
        total = total + counts[0, i]
        shows = shows + (caption >= total).astype(jnp.int32)
    image = jnp.zeros_like(key)
    for i in range(1, images):
        image = image + (key >= i * KEYS).astype(jnp.int32)
    return jnp.logical_and(image == shows, key - image * KEYS < PATCH)


def softmax_down(s):
    e = jnp.exp(s - jnp.max(s, axis=0, keepdims=True))
    return e * (1.0 / jnp.sum(e, axis=0, keepdims=True))


VEC_ROWS = 13
(
    B_QUERY,
    B_VALUE,
    B_OUT,
    GAIN_1,
    SHIFT_1,
    B_CQUERY,
    B_CVALUE,
    B_COUT,
    GAIN_2,
    SHIFT_2,
    B_CONTRACT,
    GAIN_3,
    SHIFT_3,
) = range(VEC_ROWS)


def lanes_at(i, size=128):
    return pl.ds(pl.multiple_of(i * size, 128), size)


def forward_steps(r):
    tokens = r.x.shape[0]
    rows = tokens // 2
    half = tokens // 2
    images, feat = r.feats.shape[0], r.feats.shape[2]
    keys = images * KEYS
    pairs = D // 128

    def vec(i):
        return r.vec[i : i + 1, :]

    gain_v, shift_v = r.vec_feat[0:1, :], r.vec_feat[1:2, :]
    for image in range(images):

        def vision_step(i, carry):
            xhat, _ = norm_parts(r.feats[image, rows_at(i * 64, 64), :].astype(F32))
            to = rows_at(image * KEYS + i * 64, 64)
            r.vision[to, :] = (xhat * gain_v + shift_v).astype(LOW)
            r.xhat_v[to, :] = xhat.astype(LOW)
            return carry

        lax.fori_loop(0, PATCH // 64, vision_step, 0)
        xhat, _ = norm_parts(r.feats[image, PATCH - 1 : PATCH, :].astype(F32))
        only = lax.broadcasted_iota(jnp.int32, (16, feat), 0) == 0
        to = pl.ds(image * KEYS + PATCH - 1, 16)
        r.vision[to, :] = jnp.where(only, xhat * gain_v + shift_v, 0.0).astype(LOW)
        r.xhat_v[to, :] = jnp.where(only, xhat, 0.0).astype(LOW)
        r.step()
    r.shown[...] = jnp.where(cross_mask(r.counts, rows, images), 3e38, -3e38)
    r.save(K.vision, K.xhat_v)

    def project_to(dst, weight, bias):
        def step(i, carry):
            at = rows_at(i * half, half)
            out = mm(r.x[at, :], weight[...])
            if bias is not None:
                out = out + vec(bias)
            dst[at, :] = out.astype(LOW)
            return carry

        lax.fori_loop(0, 2, step, 0)

    def self_step(i, carry):
        lanes = lanes_at(i)
        for g in range(tokens // 128):
            at = pl.ds(g * 128, 128)
            s = mm(r.k[at, lanes], pair_lanes(r.q[at, lanes] * SCALE), NT)
            p = softmax_down(jnp.where(self_mask(r.lengths, g), s, MASKED)).astype(LOW)
            r.p_self[i, g] = p
            r.mixed[at, lanes] = unpair(mm(r.v[at, lanes], p, TN)).astype(LOW)
        return carry

    r.need(2)
    r.save_weights(1)
    project_to(r.q, r.w_self(0), B_QUERY)
    r.step()
    project_to(r.k, r.w_self(1), None)
    project_to(r.v, r.w_self(2), B_VALUE)
    r.step()
    lax.fori_loop(0, pairs // 2, self_step, 0)
    r.step()
    lax.fori_loop(pairs // 2, pairs, self_step, 0)
    r.save(K.q, K.k, K.v, K.p_self, K.mixed)
    r.step()

    def out_step(i, carry):
        at = rows_at(i * half, half)
        v = r.x[at, :].astype(F32) + (mm(r.mixed[at, :], r.w_self(3)[...]) + vec(B_OUT))
        xhat, scale = norm_parts(v)
        r.xhat1[at, :] = xhat
        r.r1[at, :] = jnp.broadcast_to(scale, (half, 128))
        r.joined[at, :] = xhat * vec(GAIN_1) + vec(SHIFT_1)
        return carry

    lax.fori_loop(0, 2, out_step, 0)
    for c in range(tokens // SEQ):
        r.cross_in[pl.ds(c * NQ, NQ), :] = r.joined[pl.ds(c * SEQ, NQ), :].astype(LOW)
    r.save(K.xhat1, K.r1, K.cross_in)
    r.need(5)
    r.save_weights(2)
    for image in range(images):
        at = pl.ds(image * KEYS, KEYS)
        r.ck[at, :] = mm(r.vision[at, :], r.w_ckey[...]).astype(LOW)
        r.cv[at, :] = (mm(r.vision[at, :], r.w_cvalue[...]) + vec(B_CVALUE)).astype(LOW)
        if image == 1:
            r.step()
    r.save(K.ck, K.cv)
    r.need(6)
    r.save_weights(3)
    r.cq[...] = (mm(r.cross_in[...], r.w_cross(0)[...]) + vec(B_CQUERY)).astype(LOW)

    def cross_step(i, carry):
        lanes = lanes_at(i)
        s = mm(r.ck[:, lanes], pair_lanes(r.cq[:, lanes] * SCALE), NT)
        p = softmax_down(jnp.minimum(s, r.shown[...])).astype(LOW)
        r.keep_cross(i, p)
        r.cmixed[:, lanes] = unpair(mm(r.cv[:, lanes], p, TN)).astype(LOW)
        return carry

    for first in range(0, pairs, 2):
        r.step()
        lax.fori_loop(first, first + 2, cross_step, 0)
    r.save(K.cq, K.cmixed)
    r.step()
    branch = mm(r.cmixed[...], r.w_cross(1)[...]) + vec(B_COUT)
    for c in range(tokens // SEQ):
        own, at = pl.ds(c * NQ, NQ), pl.ds(c * SEQ, NQ)
        xhat, scale = norm_parts(r.joined[at, :] + branch[c * NQ : (c + 1) * NQ, :])
        r.xhat2[own, :] = xhat
        r.r2[own, :] = jnp.broadcast_to(scale, (NQ, 128))
        r.joined[at, :] = xhat * vec(GAIN_2) + vec(SHIFT_2)
    r.joined_low[...] = r.joined[...].astype(LOW)
    r.save(K.xhat2, K.r2, K.joined_low)
    tile = 768
    tiles = r.active.shape[0]
    r.need(9)
    r.save_weights(4)

    def wide_step(n, carry):
        at = rows_at(n * tile, tile)
        r.before_slope(n)
        for m in range(2):
            part = pl.ds(m * half, half)
            wide = mm(r.joined_low[part, :], r.w_expand[at, :], NT) + r.vec_ff[0:1, lanes_at(n, tile)]
            cdf = 0.5 * (1.0 + erf_of(wide * 0.7071067811865476))
            slope = cdf + wide * (jnp.exp(-0.5 * wide * wide) * 0.3989422804014327)
            r.active[n, part, :] = (wide * cdf).astype(LOW)
            r.slope[n % 2, part, :] = slope.astype(LOW)
        r.after_slope(n)
        return carry

    for first in range(0, tiles, 2):
        lax.fori_loop(first, first + 2, wide_step, 0)
        r.step()
    r.need(12)
    r.save_weights(5)
    gain3, shift3, bias3 = vec(GAIN_3), vec(SHIFT_3), vec(B_CONTRACT)
    zero = jnp.zeros((1, D), F32)
    dgain, dshift = zero, zero
    for m in range(2):
        part = pl.ds(m * half, half)

        def narrow_step(n, carry):
            return carry + mm(r.active[n, part, :], r.w_contract[rows_at(n * tile, tile), :])

        r.acc[...] = lax.fori_loop(0, tiles, narrow_step, jnp.zeros((half, D), F32))

        def last_step(i, carry):
            at = rows_at(m * half + i * 64, 64)
            xhat, scale = norm_parts(r.joined[at, :] + (r.acc[rows_at(i * 64, 64), :] + bias3))
            r.layer_out[at, :] = xhat * gain3 + shift3
            dy = r.out_grad[at, :].astype(F32)
            r.dthree[at, :] = norm_back(dy, xhat, scale, gain3)
            return (
                carry[0] + jnp.sum(dy * xhat, axis=0, keepdims=True),
                carry[1] + jnp.sum(dy, axis=0, keepdims=True),
            )

        dgain, dshift = lax.fori_loop(0, half // 64, last_step, (dgain, dshift))
    r.dvec3[...] = jnp.zeros_like(r.dvec3)
    r.dvec3[0:1, :] = dgain
    r.dvec3[1:2, :] = dshift
    r.save(K.dthree, K.layer_out, K.dvec3)


def spread(size, width, taken, offset):
    row = lax.broadcasted_iota(jnp.int32, (size, width), 0)
    lane = lax.broadcasted_iota(jnp.int32, (size, width), 1)
    return jnp.logical_and(lane == row + offset, row < taken).astype(F32).astype(LOW)


def build_vectors(rows, vec, vec_feat, vec_ff):
    feat, ff = vec_feat.shape[1], vec_ff.shape[1]
    one, two, three = D // 8, feat // 8, ff // 8
    total = jnp.zeros(vec.shape, F32)
    total_feat = jnp.zeros((16, feat), F32)
    for d in range(8):
        part = rows[0, d // 2, d % 2, 0:16, :]
        total = total + mm(part[:, :128], spread(128, D, one, one * d))
        total_feat = total_feat + mm(part[:, :256], spread(256, feat, two, two * d))
        vec_ff[0:1, d * three : (d + 1) * three] = part[15:16, :three].astype(F32)
    vec[...] = total
    vec_feat[0:2, :] = total_feat[VEC_ROWS : VEC_ROWS + 2]


def column_sum(v):
    return jnp.sum(v.astype(F32), axis=0, keepdims=True)


def weight_into(target, a, b, at=0, block=256):
    width = a.shape[1]
    for start in range(0, width, block):
        size = min(block, width - start)
        target[pl.ds(at + start, size), :] = mm(a[:, start : start + size], b[...], TN).astype(LOW)


def backward_ffn(r, ready):
    tokens = r.dthree.shape[0]
    half = tokens // 2
    tile = 768
    r.wait(K.dthree, K.joined_low, WEIGHT_LOAD + 5, WEIGHT_LOAD + 4)
    r.dn[...] = r.dthree[...].astype(LOW)
    r.dvec[B_CONTRACT : B_CONTRACT + 1, :] = column_sum(r.dn[...])

    def step(n, carry):
        at = rows_at(n * tile, tile)
        slot = r.ffn_tile(n)
        total = jnp.zeros((1, tile), F32)
        for m in range(2):
            part = pl.ds(m * half, half)
            wide = (mm(r.dn[part, :], r.w_contract[at, :], NT) * r.slope[slot, part, :].astype(F32)).astype(LOW)
            r.dwide[part, :] = wide
            total = total + column_sum(wide)
        r.dvec_ff[0:1, lanes_at(n, tile)] = total
        for j in range(3):
            lanes = slice(j * 256, (j + 1) * 256)
            to = rows_at(n * tile + j * 256, 256)
            r.w_contract[to, :] = mm(r.active[slot, :, lanes], r.dn[...], TN).astype(LOW)
        for m in range(2):
            part = pl.ds(m * half, half)
            r.dthree[part, :] += mm(r.dwide[part, :], r.w_expand[at, :])
        for j in range(3):
            lanes = slice(j * 256, (j + 1) * 256)
            to = rows_at(n * tile + j * 256, 256)
            r.w_expand[to, :] = mm(r.dwide[:, lanes], r.joined_low[...], TN).astype(LOW)
        return carry

    lax.fori_loop(0, r.w_contract.shape[0] // tile, step, 0)
    ready(5, 4)


def backward_cross(r, ready):
    tokens = r.dthree.shape[0]
    rows = tokens // 2
    keys = r.ck.shape[0]
    r.wait(K.xhat2, K.r2, K.cmixed, WEIGHT_LOAD + 3)
    gain = r.vec[GAIN_2 : GAIN_2 + 1, :]
    dgain, dshift = jnp.zeros((1, D), F32), jnp.zeros((1, D), F32)
    for c in range(tokens // SEQ):
        own, at = pl.ds(c * NQ, NQ), pl.ds(c * SEQ, NQ)
        dy, xhat = r.dthree[at, :], r.xhat2[own, :]
        dgain = dgain + column_sum(dy * xhat)
        dshift = dshift + column_sum(dy)
        dtwo = norm_back(dy, xhat, r.r2[own, 0:1], gain)
        r.dthree[at, :] = dtwo
        r.dcb[own, :] = dtwo.astype(LOW)
    r.dvec[GAIN_2 : GAIN_2 + 1, :] = dgain
    r.dvec[SHIFT_2 : SHIFT_2 + 1, :] = dshift
    r.dvec[B_COUT : B_COUT + 1, :] = column_sum(r.dcb[...])
    r.dcm[...] = mm(r.dcb[...], r.w_cross(1)[...], NT).astype(LOW)
    weight_into(r.w_cross(1), r.cmixed[...], r.dcb)
    r.wait(K.ck, K.cv, K.cq)

    def step(i, carry):
        lanes = lanes_at(i)
        slot = r.cross_tile(i)
        low = r.p_cross[slot]
        p = low.astype(F32)
        up = pair_lanes(r.dcm[:, lanes])
        dp = mm(r.cv[:, lanes], up, NT)
        ds = (p * (dp - jnp.sum(p * dp, axis=0, keepdims=True))).astype(LOW)
        r.cv[:, lanes] = mm(low, up).astype(LOW)
        dq = unpair(mm(r.ck[:, lanes], ds, TN)) * SCALE
        r.ck[:, lanes] = (mm(ds, pair_lanes(r.cq[:, lanes])) * SCALE).astype(LOW)
        r.dcq[:, lanes] = dq.astype(LOW)
        return carry

    lax.fori_loop(0, D // 128, step, 0)
    r.dvec[B_CVALUE : B_CVALUE + 1, :] = column_sum(r.cv[...])
    r.dvec[B_CQUERY : B_CQUERY + 1, :] = column_sum(r.dcq[...])
    r.wait(WEIGHT_LOAD + 2, K.vision, K.xhat_v, K.cross_in)
    feat = r.vision.shape[1]
    zero = jnp.zeros((1, feat), F32)

    def vision_step(i, carry):
        at = rows_at(i * KEYS, KEYS)
        up = mm(r.ck[at, :], r.w_ckey[...], NT) + mm(r.cv[at, :], r.w_cvalue[...], NT)
        return (
            carry[0] + column_sum(up * r.xhat_v[at, :].astype(F32)),
            carry[1] + column_sum(up),
        )

    dgain, dshift = lax.fori_loop(0, keys // KEYS, vision_step, (zero, zero))
    r.dvec_feat[0:1, :] = dgain
    r.dvec_feat[1:2, :] = dshift
    for start, size in ((0, 512), (512, 512), (1024, 384)):
        columns = r.vision[:, start : start + size]
        r.w_ckey[pl.ds(start, size), :] = mm(columns, r.ck[...], TN).astype(LOW)
        r.w_cvalue[pl.ds(start, size), :] = mm(columns, r.cv[...], TN).astype(LOW)
    ready(2)
    back = mm(r.dcq[...], r.w_cross(0)[...], NT)
    for c in range(tokens // SEQ):
        at = pl.ds(c * SEQ, NQ)
        r.dthree[at, :] += back[c * NQ : (c + 1) * NQ, :]
    weight_into(r.w_cross(0), r.cross_in[...], r.dcq)
    ready(3)


def backward_self(r, ready):
    tokens = r.dthree.shape[0]
    half = tokens // 2
    r.wait(K.xhat1, K.r1, K.mixed, WEIGHT_LOAD + 1)
    gain = r.vec[GAIN_1 : GAIN_1 + 1, :]
    zero = jnp.zeros((1, D), F32)

    def norm_step(i, carry):
        at = rows_at(i * 128, 128)
        dy, xhat = r.dthree[at, :], r.xhat1[at, :]
        done = norm_back(dy, xhat, r.r1[at, 0:1], gain)
        r.dthree[at, :] = done
        low = done.astype(LOW)
        r.dn[at, :] = low
        return (
            carry[0] + column_sum(dy * xhat),
            carry[1] + column_sum(dy),
            carry[2] + column_sum(low),
        )

    dgain, dshift, dbias = lax.fori_loop(0, tokens // 128, norm_step, (zero, zero, zero))
    r.dvec[GAIN_1 : GAIN_1 + 1, :] = dgain
    r.dvec[SHIFT_1 : SHIFT_1 + 1, :] = dshift
    r.dvec[B_OUT : B_OUT + 1, :] = dbias

    for m in range(2):
        part = pl.ds(m * half, half)
        r.dm[part, :] = mm(r.dn[part, :], r.w_self(3)[...], NT).astype(LOW)
    weight_into(r.w_self(3), r.mixed[...], r.dn)
    r.wait(K.q, K.k, K.v, K.p_self)

    def step(i, carry):
        lanes = lanes_at(i)
        for g in range(tokens // 128):
            at = pl.ds(g * 128, 128)
            low = r.p_self[i, g]
            p = low.astype(F32)
            up = pair_lanes(r.dm[at, lanes])
            dp = mm(r.v[at, lanes], up, NT)
            ds = (p * (dp - jnp.sum(p * dp, axis=0, keepdims=True))).astype(LOW)
            dq = unpair(mm(r.k[at, lanes], ds, TN)) * SCALE
            dk = mm(ds, pair_lanes(r.q[at, lanes])) * SCALE
            r.v[at, lanes] = mm(low, up).astype(LOW)
            r.q[at, lanes] = dq.astype(LOW)
            r.k[at, lanes] = dk.astype(LOW)
        return carry

    lax.fori_loop(0, D // 128, step, 0)
    r.dvec[B_QUERY : B_QUERY + 1, :] = column_sum(r.q[...])
    r.dvec[B_VALUE : B_VALUE + 1, :] = column_sum(r.v[...])
    r.wait(X_LOAD)
    for m in range(2):
        part = pl.ds(m * half, half)
        r.input_grad[part, :] = (
            r.dthree[part, :]
            + mm(r.q[part, :], r.w_self(0)[...], NT)
            + mm(r.k[part, :], r.w_self(1)[...], NT)
            + mm(r.v[part, :], r.w_self(2)[...], NT)
        )
    for j, ref in enumerate((r.q, r.k, r.v)):
        weight_into(r.w_self(j), r.x[...], ref)
    ready(1)


class Refs:
    def __init__(self, **names):
        self.__dict__.update(names)


class Saved(typing.NamedTuple):
    vision: typing.Any
    xhat_v: typing.Any
    q: typing.Any
    k: typing.Any
    v: typing.Any
    p_self: typing.Any
    mixed: typing.Any
    xhat1: typing.Any
    r1: typing.Any
    cross_in: typing.Any
    ck: typing.Any
    cv: typing.Any
    cq: typing.Any
    cmixed: typing.Any
    xhat2: typing.Any
    r2: typing.Any
    joined_low: typing.Any
    dthree: typing.Any
    layer_out: typing.Any
    dvec3: typing.Any
    vec: typing.Any
    active: typing.Any
    slope: typing.Any
    p_cross: typing.Any


K = Saved(*range(len(Saved._fields)))
HELD = K.vec + 1
X_LOAD, WEIGHT_LOAD = 100, 200
VMEM_BYTES = 63 * 1024 * 1024


def saved_shapes(tokens, images, feat, ff):
    rows, keys = tokens // 2, images * KEYS
    return Saved(
        vision=((keys, feat), LOW),
        xhat_v=((keys, feat), LOW),
        q=((tokens, D), LOW),
        k=((tokens, D), LOW),
        v=((tokens, D), LOW),
        p_self=((D // 128, tokens // 128, 128, 256), LOW),
        mixed=((tokens, D), LOW),
        xhat1=((tokens, D), F32),
        r1=((tokens, 128), F32),
        cross_in=((rows, D), LOW),
        ck=((keys, D), LOW),
        cv=((keys, D), LOW),
        cq=((rows, D), LOW),
        cmixed=((rows, D), LOW),
        xhat2=((rows, D), F32),
        r2=((rows, 128), F32),
        joined_low=((tokens, D), LOW),
        dthree=((tokens, D), F32),
        layer_out=((tokens, D), F32),
        dvec3=((8, D), F32),
        vec=((16, D), F32),
        active=((ff // 768, tokens, 768), LOW),
        slope=((ff // 768, tokens, 768), LOW),
        p_cross=((D // 128, keys, 2 * rows), LOW),
    )


def full_views(full):
    def flat(ref, j):
        return ref.at[j].reshape(8 * ref.shape[3], D)

    return dict(
        w_self=lambda j: flat(full[1], j),
        w_ckey=flat(full[2], 0),
        w_cvalue=flat(full[2], 1),
        w_cross=lambda j: flat(full[3], j),
        w_expand=flat(full[4], 0),
        w_contract=flat(full[5], 0),
    )


def forward_kernel(fast, *refs):
    count = len(ARRAY_ROWS)
    (counts, lengths, x, feats, out_grad), refs = refs[:5], refs[5:]
    own, refs = refs[:count], refs[count:]
    if not fast:
        vec_in, refs = refs[:3], refs[3:]
    outs, refs = Saved(*refs[: len(K)]), refs[len(K) :]
    weights, refs = refs[: count - 1], refs[count - 1 :]
    held, refs = refs[:HELD], refs[HELD:]
    full, refs = refs[:count], refs[count:]
    vec_feat, vec_ff, joined, acc, shown, active, slope, pbuf = refs[:8]
    save_sem, weight_sem, active_sem, slope_sem, p_sem = refs[8:13]
    kept = dict(zip(Saved._fields, held))
    vec = kept[Saved._fields[K.vec]]
    pairs, tiles = outs.p_cross.shape[0], outs.slope.shape[0]
    copies = []

    def begin(copy):
        copy.start()
        copies.append(copy)

    def save(*names):
        for i in names:
            begin(pltpu.make_async_copy(held[i], outs[i], save_sem.at[i]))

    def save_weights(i):
        begin(pltpu.make_async_copy(full[i], weights[i - 1], weight_sem.at[i]))

    def p_copy(i):
        return pltpu.make_async_copy(pbuf.at[i % 2], outs.p_cross.at[i], p_sem.at[i % 2])

    def slope_copy(n):
        return pltpu.make_async_copy(slope.at[n % 2], outs.slope.at[n], slope_sem.at[n % 2])

    def active_copy(n):
        return pltpu.make_async_copy(active.at[n], outs.active.at[n], active_sem.at[n])

    def keep_cross(i, p):
        @pl.when(i >= 2)
        def _():
            p_copy(i - 2).wait()

        pbuf[i % 2] = p
        p_copy(i).start()

    def before_slope(n):
        @pl.when(n >= 2)
        def _():
            slope_copy(n - 2).wait()

    def after_slope(n):
        slope_copy(n).start()
        active_copy(n).start()

    if fast:
        gather = Gather(own, full, refs[13:])
        gather.start()
        gather.vectors()
        build_vectors(full[0], vec, vec_feat, vec_ff)
        need = gather.need

        def step():
            gather.advance(gather.slot_at + 1)
    else:
        loads = [pltpu.make_async_copy(own[i], full[i], weight_sem.at[i]) for i in range(count)]
        loads += [
            pltpu.make_async_copy(src, dst, p_sem.at[0])
            for src, dst in zip(vec_in, (vec, vec_feat, vec_ff))
        ]
        for copy in loads:
            copy.start()
            copy.wait()

        def need(k):
            pass

        def step():
            pass

    save(K.vec)
    r = Refs(
        counts=counts,
        lengths=lengths,
        x=x,
        feats=feats,
        out_grad=out_grad,
        **kept,
        **full_views(full),
        vec_feat=vec_feat,
        vec_ff=vec_ff,
        joined=joined,
        acc=acc,
        shown=shown,
        active=active,
        slope=slope,
        save=save,
        save_weights=save_weights,
        need=need,
        step=step,
        keep_cross=keep_cross,
        before_slope=before_slope,
        after_slope=after_slope,
    )
    forward_steps(r)
    for i in (pairs - 2, pairs - 1):
        p_copy(i).wait()
    for n in (tiles - 2, tiles - 1):
        slope_copy(n).wait()
    for n in range(tiles):
        active_copy(n).wait()
    for copy in copies:
        copy.wait()
    if fast:
        gather.end()


def forward_all(fast, counts, lengths, x, feats, out_grad, own, vectors):
    tokens, images, feat = x.shape[0], feats.shape[0], feats.shape[2]
    count = len(ARRAY_ROWS)
    if fast:
        full = [(k, 4, 2, rows, D) for k, rows in ARRAY_ROWS]
    else:
        full = [w.shape for w in own]
    ff = 8 * full[4][3]
    rows, keys = tokens // 2, images * KEYS
    shapes = saved_shapes(tokens, images, feat, ff)
    vmem, smem = pl.BlockSpec(memory_space=pltpu.VMEM), pl.BlockSpec(memory_space=pltpu.SMEM)
    hbm = pl.BlockSpec(memory_space=pl.ANY)
    ins = [counts, lengths, x, feats, out_grad, *own]
    if not fast:
        ins += list(vectors)
    out_shape = [jax.ShapeDtypeStruct(*shape) for shape in shapes]
    out_shape += [jax.ShapeDtypeStruct(shape, LOW) for shape in full[1:]]
    dma = pltpu.SemaphoreType.DMA
    outs = pl.pallas_call(
        functools.partial(forward_kernel, fast),
        name="forward",
        out_shape=out_shape,
        in_specs=[smem, smem] + [vmem] * 3 + [hbm] * (len(ins) - 5),
        out_specs=[hbm] * len(out_shape),
        scratch_shapes=[pltpu.VMEM(*shape) for shape in shapes[:HELD]]
        + [pltpu.VMEM(shape, LOW) for shape in full]
        + [
            pltpu.VMEM((8, feat), F32),
            pltpu.VMEM((8, ff), F32),
            pltpu.VMEM((tokens, D), F32),
            pltpu.VMEM((tokens // 2, D), F32),
            pltpu.VMEM((keys, 2 * rows), F32),
            pltpu.VMEM((ff // 768, tokens, 768), LOW),
            pltpu.VMEM((2, tokens, 768), LOW),
            pltpu.VMEM((2, keys, 2 * rows), LOW),
            dma((HELD,)),
            dma((count,)),
            dma((ff // 768,)),
            dma((2,)),
            dma((2,)),
        ]
        + (gather_semaphores() if fast else []),
        compiler_params=pltpu.CompilerParams(
            vmem_limit_bytes=VMEM_BYTES,
            **(dict(collective_id=0, has_side_effects=True) if fast else {}),
        ),
    )(*ins)
    return Saved(*outs[: len(K)]), list(outs[len(K) :])


LOADS = (K.dthree, K.joined_low, K.xhat2, K.r2, K.cmixed, K.ck, K.cv, K.cq, K.vision, K.xhat_v, K.cross_in)
LOADS += (K.xhat1, K.r1, K.mixed, K.q, K.k, K.v, K.p_self)


def backward_kernel(*refs):
    x_in, refs = refs[0], refs[1:]
    ins, refs = Saved(*refs[: len(K)]), refs[len(K) :]
    weights, refs = refs[:5], refs[5:]
    (dvec, dvec_feat, dvec_ff, input_grad), refs = refs[:4], refs[4:]
    grads, refs = refs[:5], refs[5:]
    held, refs = dict(zip(LOADS, refs)), refs[len(LOADS) :]
    full, refs = refs[:5], refs[5:]
    x, vec, dn, dwide, dm, dcb, dcm, dcq, abuf, sbuf, pbuf = refs[:11]
    load_sem, w_sem, g_sem, abuf_sem, sbuf_sem, pbuf_sem = refs[11:]
    loads = {i: pltpu.make_async_copy(ins[i], held[i], load_sem.at[i]) for i in LOADS}
    loads[K.vec] = pltpu.make_async_copy(ins.vec, vec, load_sem.at[K.vec])
    loads[X_LOAD] = pltpu.make_async_copy(x_in, x, load_sem.at[K.layer_out])
    for i in range(5):
        loads[WEIGHT_LOAD + 1 + i] = pltpu.make_async_copy(weights[i], full[i], w_sem.at[i])

    def tile_copies(n, slot):
        return (
            pltpu.make_async_copy(ins.active.at[n], abuf.at[slot], abuf_sem.at[slot]),
            pltpu.make_async_copy(ins.slope.at[n], sbuf.at[slot], sbuf_sem.at[slot]),
        )

    def pair_copy(i, slot):
        return pltpu.make_async_copy(ins.p_cross.at[i], pbuf.at[slot], pbuf_sem.at[slot])

    for i in LOADS[:2] + (K.vec, WEIGHT_LOAD + 5):
        loads[i].start()
    for copy in tile_copies(0, 0):
        copy.start()
    for i in (WEIGHT_LOAD + 4,) + LOADS[2:5] + (WEIGHT_LOAD + 3,) + LOADS[5:8]:
        loads[i].start()
    pair_copy(0, 0).start()
    for i in (WEIGHT_LOAD + 2,) + LOADS[8:14] + (WEIGHT_LOAD + 1,) + LOADS[14:] + (X_LOAD,):
        loads[i].start()

    def wait(*names):
        for i in names:
            loads[i].wait()

    def ffn_tile(n):
        @pl.when(n + 1 < ins.active.shape[0])
        def _():
            for copy in tile_copies(n + 1, (n + 1) % 2):
                copy.start()

        for copy in tile_copies(n, n % 2):
            copy.wait()
        return n % 2

    def cross_tile(i):
        @pl.when(i + 1 < ins.p_cross.shape[0])
        def _():
            pair_copy(i + 1, (i + 1) % 2).start()

        pair_copy(i, i % 2).wait()
        return i % 2

    stored = []

    def ready(*arrays):
        for i in arrays:
            copy = pltpu.make_async_copy(full[i - 1], grads[i - 1], g_sem.at[i - 1])
            copy.start()
            stored.append(copy)

    r = Refs(
        **{Saved._fields[i]: ref for i, ref in held.items()},
        **full_views((None,) + tuple(full)),
        x=x,
        vec=vec,
        dvec=dvec,
        dvec_feat=dvec_feat,
        dvec_ff=dvec_ff,
        input_grad=input_grad,
        dn=dn,
        dwide=dwide,
        dm=dm,
        dcb=dcb,
        dcm=dcm,
        dcq=dcq,
        active=abuf,
        slope=sbuf,
        p_cross=pbuf,
        wait=wait,
        ffn_tile=ffn_tile,
        cross_tile=cross_tile,
    )
    dvec[...] = jnp.zeros_like(dvec)
    dvec_feat[...] = jnp.zeros_like(dvec_feat)
    dvec_ff[...] = jnp.zeros_like(dvec_ff)
    wait(K.vec)
    backward_ffn(r, ready)
    backward_cross(r, ready)
    backward_self(r, ready)
    for copy in stored:
        copy.wait()


def backward_all(saved, weights, x):
    tokens, keys, feat = x.shape[0], saved.vision.shape[0], saved.vision.shape[1]
    rows, ff = tokens // 2, 8 * weights[3].shape[3]
    vmem, hbm = pl.BlockSpec(memory_space=pltpu.VMEM), pl.BlockSpec(memory_space=pl.ANY)
    dma = pltpu.SemaphoreType.DMA
    shapes = [jax.ShapeDtypeStruct(w.shape, LOW) for w in weights]
    outs = pl.pallas_call(
        backward_kernel,
        name="backward",
        out_shape=[
            jax.ShapeDtypeStruct((16, D), F32),
            jax.ShapeDtypeStruct((8, feat), F32),
            jax.ShapeDtypeStruct((8, ff), F32),
            jax.ShapeDtypeStruct((tokens, D), F32),
        ]
        + shapes,
        in_specs=[hbm] * (1 + len(K) + 5),
        out_specs=[vmem] * 4 + [hbm] * 5,
        scratch_shapes=[pltpu.VMEM(saved[i].shape, saved[i].dtype) for i in LOADS]
        + [pltpu.VMEM(w.shape, LOW) for w in weights]
        + [pltpu.VMEM((tokens, D), LOW), pltpu.VMEM((16, D), F32)]
        + [pltpu.VMEM((tokens, D), LOW)] * 3
        + [pltpu.VMEM((rows, D), LOW)] * 3
        + [
            pltpu.VMEM((2, tokens, 768), LOW),
            pltpu.VMEM((2, tokens, 768), LOW),
            pltpu.VMEM((2, keys, 2 * rows), LOW),
            dma((len(K),)),
            dma((5,)),
            dma((5,)),
            dma((2,)),
            dma((2,)),
            dma((2,)),
        ],
        compiler_params=pltpu.CompilerParams(vmem_limit_bytes=VMEM_BYTES),
    )(x, *saved, *weights)
    return outs[:3], outs[3], outs[4:]


COMM_VMEM = 56 * 1024 * 1024
SUM_PIECES = (
    Piece(5, True, 48, lambda y, c: 0, lambda y, c: 48 * (2 * y + c)),
    Piece(5, False, 96, lambda y, c: 0, lambda y, c: 192 + 96 * c),
    Piece(4, True, 48, lambda y, c: 0, lambda y, c: 48 * (2 * y + c)),
    Piece(4, False, 96, lambda y, c: 0, lambda y, c: 192 + 96 * c),
    Piece(3, True, 32, lambda y, c: y, lambda y, c: 32 * c),
    Piece(3, False, 32, lambda y, c: c, lambda y, c: 64),
    Piece(2, True, 48, lambda y, c: y, lambda y, c: 48 * c),
    Piece(2, False, 80, lambda y, c: c, lambda y, c: 96),
    Piece(1, True, 48, lambda y, c: 2 * y + c, lambda y, c: 0),
    Piece(1, False, 48, lambda y, c: 2 * c, lambda y, c: 48),
    Piece(1, False, 48, lambda y, c: 2 * c + 1, lambda y, c: 48),
    Piece(0, False, 16, lambda y, c: 0, lambda y, c: 16 * c),
)


def sum_kernel(*refs):
    count, total = len(ARRAY_ROWS), len(SUM_PIECES)
    grads, outs = refs[:count], refs[count : 2 * count]
    refs = refs[2 * count :]
    mine, from_c, from_y, from_x, from_z, last = (refs[i * total : (i + 1) * total] for i in range(6))
    here, done, cs, ys, xs, zs, fs, cs_s, ys_s, xs_s, zs_s, fs_s = refs[6 * total :]
    y, c, z, x = place()
    zp = [lax.rem(z + i, 4) for i in (1, 2, 3)]
    to_z = [at_device(y, c, p, x) for p in zp]
    to_x, to_y, to_c = at_device(y, c, z, 1 - x), at_device(1 - y, c, z, x), at_device(y, 1 - c, z, x)
    to_d = at_device(1 - y, 1 - c, z, x)
    greet(to_z + [to_x, to_y, to_c, to_d])
    sent, stored = [], []

    def go(*spec):
        copy = remote(*spec)
        copy.start()
        sent.append(copy)

    def arrived(dst, recv, send):
        remote(dst, dst, send, recv, to_x).wait_recv()

    def sides(p):
        return (y, 1 - y) if p.four else (y,)

    local = []
    for k, p in enumerate(SUM_PIECES):
        for j, yy in enumerate(sides(p)):
            copy = pltpu.make_async_copy(p.every(grads, yy, c), mine[k].at[j], here.at[k, j])
            copy.start()
            local.append((k, copy))
            go(p.every(grads, yy, 1 - c), from_c[k].at[j], cs_s.at[k, j], cs.at[k, j], to_c)

    def stage_c(k):
        p = SUM_PIECES[k]
        for kk, copy in local:
            if kk == k:
                copy.wait()
        for j in reversed(range(len(sides(p)))):
            arrived(from_c[k].at[j], cs.at[k, j], cs_s.at[k, j])
            for i in range(4):
                for l in range(2):
                    mine[k][j, i, l] = mine[k][j, i, l] + from_c[k][j, i, l]
            if j == 1:
                go(mine[k].at[1], from_y[k], ys_s.at[k], ys.at[k], to_y)

    def stage_y(k):
        p = SUM_PIECES[k]
        if p.four:
            arrived(from_y[k], ys.at[k], ys_s.at[k])
            for i in range(4):
                for l in range(2):
                    mine[k][0, i, l] = mine[k][0, i, l] + from_y[k][i, l]
        go(mine[k].at[0, :, 1 - x], from_x[k], xs_s.at[k], xs.at[k], to_x)

    def stage_x(k):
        arrived(from_x[k], xs.at[k], xs_s.at[k])
        for i in range(4):
            from_x[k][i] = from_x[k][i] + mine[k][0, i, x]
        for i in range(3):
            go(from_x[k].at[zp[i]], from_z[k].at[i], zs_s.at[k, i], zs.at[k, i], to_z[i])

    def stage_z(k):
        p = SUM_PIECES[k]
        for i in range(3):
            arrived(from_z[k].at[i], zs.at[k, i], zs_s.at[k, i])
        value = from_x[k][z].astype(jnp.float32)
        for i in range(3):
            value = value + from_z[k][i].astype(jnp.float32)
        last[k][0] = value.astype(jnp.bfloat16)
        if p.four:
            go(last[k].at[0], last[k].at[1], fs_s.at[k, 0], fs.at[k, 0], to_y)
            go(last[k].at[0], last[k].at[2], fs_s.at[k, 1], fs.at[k, 1], to_c)
            go(last[k].at[0], last[k].at[3], fs_s.at[k, 2], fs.at[k, 2], to_d)
        else:
            go(last[k].at[0], last[k].at[1], fs_s.at[k, 0], fs.at[k, 0], to_y)

    def put(k, j, slot, yy, cc):
        copy = pltpu.make_async_copy(last[k].at[slot], SUM_PIECES[k].shard(outs, yy, cc), done.at[k, j])
        copy.start()
        stored.append(copy)

    def stage_f(k):
        p = SUM_PIECES[k]
        if p.four:
            put(k, 0, 0, y, c)
            for j, (yy, cc) in enumerate(((1 - y, c), (y, 1 - c), (1 - y, 1 - c))):
                arrived(last[k].at[j + 1], fs.at[k, j], fs_s.at[k, j])
                put(k, j + 1, j + 1, yy, cc)
        else:
            arrived(last[k].at[1], fs.at[k, 0], fs_s.at[k, 0])
            last[k][2] = last[k][0] + last[k][1]
            go(last[k].at[2], last[k].at[3], fs_s.at[k, 1], fs.at[k, 1], to_c)
            put(k, 0, 2, y, c)

    def stage_g(k):
        p = SUM_PIECES[k]
        if not p.four:
            arrived(last[k].at[3], fs.at[k, 1], fs_s.at[k, 1])
            put(k, 1, 3, y, 1 - c)

    stages = (stage_c, stage_y, stage_x, stage_z, stage_f, stage_g)
    for t in range(total + len(stages) - 1):
        for lag, stage in enumerate(stages):
            if 0 <= t - lag < total:
                stage(t - lag)
    for copy in sent:
        copy.wait_send()
    for copy in stored:
        copy.wait()


def sum_all(grads):
    total = len(SUM_PIECES)
    low = jnp.bfloat16
    sides = [2 if p.four else 1 for p in SUM_PIECES]
    sizes = [p.size for p in SUM_PIECES]
    dma = pltpu.SemaphoreType.DMA
    return pl.pallas_call(
        sum_kernel,
        out_shape=[jax.ShapeDtypeStruct((count, rows, D), low) for count, rows in ARRAY_ROWS],
        in_specs=[pl.BlockSpec(memory_space=pl.ANY)] * len(ARRAY_ROWS),
        out_specs=[pl.BlockSpec(memory_space=pl.ANY)] * len(ARRAY_ROWS),
        scratch_shapes=[pltpu.VMEM((s, 4, 2, n, D), low) for s, n in zip(sides, sizes)]
        + [pltpu.VMEM((s, 4, 2, n, D), low) for s, n in zip(sides, sizes)]
        + [pltpu.VMEM((4, 2, n, D) if s == 2 else (1, 1, 16, D), low) for s, n in zip(sides, sizes)]
        + [pltpu.VMEM((4, n, D), low) for n in sizes]
        + [pltpu.VMEM((3, n, D), low) for n in sizes]
        + [pltpu.VMEM((4, n, D), low) for n in sizes]
        + [
            dma((total, 2)),
            dma((total, 4)),
            dma((total, 2)),
            dma((total,)),
            dma((total,)),
            dma((total, 3)),
            dma((total, 3)),
            dma((total, 2)),
            dma((total,)),
            dma((total,)),
            dma((total, 3)),
            dma((total, 3)),
        ],
        compiler_params=pltpu.CompilerParams(
            collective_id=1, has_side_effects=True, vmem_limit_bytes=COMM_VMEM
        ),
        cost_estimate=pl.CostEstimate(flops=0, bytes_accessed=100_000_000, transcendentals=0),
    )(*grads)


def pack_rows(vectors):
    rows = [jnp.pad(v, (0, D - v.shape[0])) for v in vectors]
    rows += [jnp.zeros((D,), rows[0].dtype)] * (32 - len(rows))
    return jnp.stack(rows)[None]


def sum_shards(fast, grads):
    if fast:
        return sum_all([g.reshape(g.shape[0], 4, 2, g.shape[2], D) for g in grads])
    owned = [lax.psum_scatter(g, FSDP, scatter_dimension=1, tiled=False) for g in grads]
    return [lax.psum(g, DP) for g in owned]


def local(
    fast,
    hidden,
    image_feats,
    caption_counts,
    text_lengths,
    out_grad,
    self_query,
    query_bias,
    self_key,
    self_value,
    value_bias,
    self_output,
    output_bias,
    first_gain,
    first_shift,
    cross_query,
    crossquery_bias,
    cross_key,
    cross_value,
    crossvalue_bias,
    cross_output,
    crossoutput_bias,
    second_gain,
    second_shift,
    vision_gain,
    vision_shift,
    expand_weight,
    expand_bias,
    contract_weight,
    contract_bias,
    third_gain,
    third_shift,
):
    low = jnp.bfloat16
    vectors = (
        query_bias,
        value_bias,
        output_bias,
        first_gain,
        first_shift,
        crossquery_bias,
        crossvalue_bias,
        crossoutput_bias,
        second_gain,
        second_shift,
        contract_bias,
        third_gain,
        third_shift,
        vision_gain,
        vision_shift,
        expand_bias,
    )
    own = (
        pack_rows(vectors),
        jnp.stack([self_query, self_key, self_value, self_output]),
        jnp.stack([cross_key, cross_value]),
        jnp.stack([cross_query, cross_output]),
        expand_weight.T[None],
        contract_weight[None],
    )
    feat = image_feats.shape[-1]
    shards = D // self_query.shape[0]
    whole = ()
    if not fast:
        full = [lax.all_gather(s, FSDP, axis=1, tiled=False) for s in own]
        rows = full[0][0]
        each = [rows[:, i, : v.shape[0]].reshape(-1).astype(F32) for i, v in enumerate(vectors)]
        own = [f.reshape(f.shape[0], 4, 2, -1, D) for f in full]
        whole = (
            jnp.stack(each[:VEC_ROWS] + [jnp.zeros((D,), F32)] * (16 - VEC_ROWS)),
            jnp.stack(each[VEC_ROWS : VEC_ROWS + 2] + [jnp.zeros((feat,), F32)] * 6),
            jnp.broadcast_to(each[-1][None], (8, each[-1].shape[0])),
        )
    x = hidden.reshape(-1, D)
    saved, weights = forward_all(
        fast,
        caption_counts,
        text_lengths,
        x,
        image_feats,
        out_grad.reshape(-1, D),
        own,
        whole,
    )
    (dvec, dvec_feat, dvec_ff), input_grad, grads = backward_all(saved, weights, x)
    layer_out = saved.layer_out.reshape(hidden.shape)
    input_grad = input_grad.reshape(hidden.shape)
    vector_grads = [dvec[i] for i in range(VEC_ROWS)]
    vector_grads[GAIN_3], vector_grads[SHIFT_3] = saved.dvec3[0], saved.dvec3[1]
    vector_grads += [dvec_feat[0], dvec_feat[1], dvec_ff[0]]
    packed = jnp.stack(
        [
            jnp.pad(v.astype(low).reshape(shards, -1), ((0, 0), (0, D - v.shape[0] // shards)))
            for v in vector_grads
        ]
        + [jnp.zeros((shards, D), low)] * (32 - len(vector_grads)),
        axis=1,
    )

    summed = sum_shards(
        fast, (packed[None],) + tuple(g.reshape(g.shape[0], shards, -1, D) for g in grads)
    )
    sums = [s.astype(F32) for s in summed]
    small = [sums[0][0, i, : v.shape[0]] for i, v in enumerate(vectors)]
    return (
        layer_out,
        input_grad,
        sums[1][0],
        small[0],
        sums[1][1],
        sums[1][2],
        small[1],
        sums[1][3],
        small[2],
        small[3],
        small[4],
        sums[3][0],
        small[5],
        sums[2][0],
        sums[2][1],
        small[6],
        sums[3][1],
        small[7],
        small[8],
        small[9],
        small[13],
        small[14],
        sums[4][0].T,
        small[15],
        sums[5][0],
        small[10],
        small[11],
        small[12],
    )


def solution(mesh):
    fast = mesh.shape[DP] == 4 and mesh.shape[FSDP] == 8
    tokens, pair = P((DP, FSDP), None, None), P((DP, FSDP), None)
    by_row, by_column, flat = P(FSDP, None), P(None, FSDP), P(FSDP)
    params = (
        (by_row, flat, by_row, by_row, flat, by_row, flat, flat, flat)
        + (by_row, flat, by_row, by_row, flat, by_row, flat)
        + (flat,) * 4
        + (by_column, flat, by_row, flat, flat, flat)
    )
    return jax.shard_map(
        functools.partial(local, fast),
        mesh=mesh,
        in_specs=(tokens, tokens, pair, P((DP, FSDP)), tokens) + params,
        out_specs=(tokens, tokens) + params,
        check_vma=False,
    )
```

```python
import functools
import typing

import jax
import jax.numpy as jnp
from jax import lax
from jax.experimental import pallas as pl
from jax.experimental.pallas import tpu as pltpu
from jax.sharding import PartitionSpec as P

D = 768
HEADS = 12
HDIM = 64
PATCH = 257
NQ = 32
SEQ = 64
EPS = 1e-06
MASKED = -1000000000.0


MESH = pl.DeviceIdType.MESH
DP, FSDP = "dp", "fsdp"
SHARD_LANES = 96


def place():
    dp, fs = lax.axis_index(DP), lax.axis_index(FSDP)
    return dp // 2, dp % 2, fs // 2, fs % 2


def at_device(y, c, z, x):
    return (2 * y + c, 2 * z + x)


def rows_at(start, size):
    return pl.ds(pl.multiple_of(start, 16), size)


def greet(peers):
    barrier = pltpu.get_barrier_semaphore()
    for peer in peers:
        pl.semaphore_signal(barrier, inc=1, device_id=peer, device_id_type=MESH)
    pl.semaphore_wait(barrier, len(peers))


class Piece:
    def __init__(self, array, four, size, which, start):
        self.array, self.four, self.size, self.which, self.start = array, four, size, which, start

    def shard(self, refs, y, c):
        return refs[self.array].at[self.which(y, c), rows_at(self.start(y, c), self.size)]

    def at(self, refs, y, c, z, x):
        return refs[self.array].at[self.which(y, c), z, x, rows_at(self.start(y, c), self.size)]

    def column(self, refs, y, c, x):
        return refs[self.array].at[self.which(y, c), :, x, rows_at(self.start(y, c), self.size)]

    def every(self, refs, y, c):
        return refs[self.array].at[self.which(y, c), :, :, rows_at(self.start(y, c), self.size)]


ARRAY_ROWS = ((1, 32), (4, 96), (2, 176), (2, 96), (1, 384), (1, 384))


def corner(array, start):
    return Piece(array, True, 48, lambda y, c: 0, lambda y, c: start + 48 * (2 * y + c))


def halved(array, start):
    return Piece(array, False, 48, lambda y, c: 0, lambda y, c: start + 48 * c)


GATHER_PIECES = (
    Piece(1, True, 32, lambda y, c: 2 * y + c, lambda y, c: 0),
    Piece(1, True, 32, lambda y, c: 2 * y + c, lambda y, c: 32),
    Piece(1, True, 32, lambda y, c: 2 * y + c, lambda y, c: 64),
    Piece(2, True, 48, lambda y, c: y, lambda y, c: 80 * c),
    Piece(2, True, 32, lambda y, c: y, lambda y, c: 80 * c + 48),
    Piece(2, False, 16, lambda y, c: c, lambda y, c: 160),
    Piece(3, True, 48, lambda y, c: y, lambda y, c: 48 * c),
    corner(4, 0),
    halved(4, 192),
    halved(4, 288),
    corner(5, 0),
    halved(5, 192),
    halved(5, 288),
)
GATHER_AHEAD = 3
GATHER_LAGS = (0, 1, 3, 4)
GATHER_SLOTS = len(GATHER_PIECES) + GATHER_LAGS[-1]


def remote(src, dst, send, recv, device):
    return pltpu.make_async_remote_copy(
        src_ref=src, dst_ref=dst, send_sem=send, recv_sem=recv, device_id=device, device_id_type=MESH
    )


class Gather:
    def __init__(self, own, full, sems):
        self.own, self.full = own, full
        self.here, self.vs, self.zs, self.xs, self.ys, self.cs = sems[:6]
        self.vs_s, self.zs_s, self.xs_s, self.ys_s, self.cs_s = sems[6:]
        y, c, z, x = self.me = place()
        self.zp = [lax.rem(z + i, 4) for i in (1, 2, 3)]
        self.zm = [lax.rem(z + 4 - i, 4) for i in (1, 2, 3)]
        self.to_z = [at_device(y, c, p, x) for p in self.zp]
        self.to_diag = [at_device(y, c, p, 1 - x) for p in self.zp]
        self.to_x, self.to_y = at_device(y, c, z, 1 - x), at_device(1 - y, c, z, x)
        self.to_c = at_device(y, 1 - c, z, x)
        self.sent, self.slot_at = [], 0
        greet(self.to_z + self.to_diag + [self.to_x, self.to_y, self.to_c])

    def go(self, *spec):
        copy = remote(*spec)
        copy.start()
        self.sent.append(copy)

    def arrived(self, dst, recv, send):
        remote(dst, dst, send, recv, self.to_x).wait_recv()

    def start(self):
        y, c, z, x = self.me
        mine = self.full[0].at[0, z, x]
        for i, device in enumerate(self.to_z + self.to_diag + [self.to_x]):
            self.go(self.own[0].at[0], mine, self.vs_s.at[i], self.vs.at[i], device)
        self.locals = [pltpu.make_async_copy(self.own[0].at[0], mine, self.here.at[0, 0])]
        for k in range(GATHER_AHEAD):
            self.send(k)
        for k, p in enumerate(GATHER_PIECES):
            for j in range(2 if p.four else 1):
                yy = y if j == 0 else 1 - y
                self.locals.append(
                    pltpu.make_async_copy(
                        p.shard(self.own, yy, c), p.at(self.full, yy, c, z, x), self.here.at[k + 1, j]
                    )
                )
        for copy in self.locals:
            copy.start()
        for copy in self.locals:
            copy.wait()

    def vectors(self):
        y, c, z, x = self.me
        places = [(m, x) for m in self.zm] + [(m, 1 - x) for m in self.zm] + [(z, 1 - x)]
        for i, (zz, xx) in enumerate(places):
            self.arrived(self.full[0].at[0, zz, xx], self.vs.at[i], self.vs_s.at[i])

    def send(self, k):
        y, c, z, x = self.me
        p = GATHER_PIECES[k]
        src, dst = p.shard(self.own, y, c), p.at(self.full, y, c, z, x)
        for i in range(3):
            self.go(src, dst, self.zs_s.at[k, i], self.zs.at[k, i], self.to_z[i])
        self.go(src, dst, self.xs_s.at[k, 0], self.xs.at[k, 0], self.to_x)

    def stage_x(self, k):
        y, c, z, x = self.me
        p = GATHER_PIECES[k]
        for i in range(3):
            got = p.at(self.full, y, c, self.zm[i], x)
            self.arrived(got, self.zs.at[k, i], self.zs_s.at[k, i])
            self.go(got, got, self.xs_s.at[k, i + 1], self.xs.at[k, i + 1], self.to_x)

    def stage_y(self, k):
        y, c, z, x = self.me
        p = GATHER_PIECES[k]
        self.arrived(p.at(self.full, y, c, z, 1 - x), self.xs.at[k, 0], self.xs_s.at[k, 0])
        for i in range(3):
            got = p.at(self.full, y, c, self.zm[i], 1 - x)
            self.arrived(got, self.xs.at[k, i + 1], self.xs_s.at[k, i + 1])
        if p.four:
            far = p.column(self.full, y, c, 1 - x)
            self.go(far, far, self.ys_s.at[k, 0], self.ys.at[k, 0], self.to_y)
            for i in range(3):
                near = p.at(self.full, y, c, self.zm[i], x)
                self.go(near, near, self.ys_s.at[k, i + 1], self.ys.at[k, i + 1], self.to_y)
        mine = p.every(self.full, y, c)
        self.go(mine, mine, self.cs_s.at[k, 0], self.cs.at[k, 0], self.to_c)

    def stage_c(self, k):
        y, c, z, x = self.me
        p = GATHER_PIECES[k]
        if p.four:
            got = p.column(self.full, 1 - y, c, 1 - x)
            self.arrived(got, self.ys.at[k, 0], self.ys_s.at[k, 0])
            for i in range(3):
                got = p.at(self.full, 1 - y, c, self.zm[i], x)
                self.arrived(got, self.ys.at[k, i + 1], self.ys_s.at[k, i + 1])
            mine = p.every(self.full, 1 - y, c)
            self.go(mine, mine, self.cs_s.at[k, 1], self.cs.at[k, 1], self.to_c)

    def finish(self, k):
        y, c, z, x = self.me
        p = GATHER_PIECES[k]
        self.arrived(p.every(self.full, y, 1 - c), self.cs.at[k, 0], self.cs_s.at[k, 0])
        if p.four:
            self.arrived(p.every(self.full, 1 - y, 1 - c), self.cs.at[k, 1], self.cs_s.at[k, 1])

    def advance(self, slots):
        total = len(GATHER_PIECES)
        while self.slot_at < min(slots, GATHER_SLOTS):
            t = self.slot_at
            if GATHER_AHEAD <= t + GATHER_AHEAD < total:
                self.send(t + GATHER_AHEAD)
            stages = (self.stage_x, self.stage_y, self.stage_c, self.finish)
            for lag, stage in zip(GATHER_LAGS, stages):
                if 0 <= t - lag < total:
                    stage(t - lag)
            self.slot_at += 1

    def need(self, k):
        self.advance(k + GATHER_LAGS[-1] + 1)

    def end(self):
        for copy in self.sent:
            copy.wait_send()


def gather_semaphores():
    total, dma = len(GATHER_PIECES), pltpu.SemaphoreType.DMA
    pairs = [dma((7,)), dma((total, 3)), dma((total, 4)), dma((total, 4)), dma((total, 2))]
    return [dma((total + 1, 2))] + pairs + pairs


LOW = jnp.bfloat16
F32 = jnp.float32
KEYS = 272
SCALE = HDIM**-0.5
NN = (((1,), (0,)), ((), ()))
NT = (((1,), (1,)), ((), ()))
TN = (((0,), (0,)), ((), ()))


def mm(a, b, dims=NN):
    return lax.dot_general(a, b, dims, preferred_element_type=F32)


def erf_of(v):
    v = jnp.clip(v, -3.832506856900711, 3.832506856900711)
    s = v * v
    top = jnp.full_like(s, 0.00022905065861350646)
    for k in (0.0034082910107109506, 0.050955695062380861, 0.18520832239976145, 1.128379143519084):
        top = top * s + k
    low = jnp.full_like(s, -1.1791602954361697e-7)
    for k in (0.000023547966471313185, 0.0010179625278914885, 0.014070470171167667, 0.11098505178285362, 0.49746925110067538, 1.0):
        low = low * s + k
    return v * top / low


def norm_parts(v):
    center = v - jnp.mean(v, axis=-1, keepdims=True)
    r = lax.rsqrt(jnp.mean(center * center, axis=-1, keepdims=True) + EPS)
    return center * r, r


def norm_back(dy, xhat, r, gain):
    gdy = gain * dy
    return r * (
        gdy
        - jnp.mean(gdy, axis=-1, keepdims=True)
        - xhat * jnp.mean(gdy * xhat, axis=-1, keepdims=True)
    )


def pair_lanes(v):
    lane = lax.broadcasted_iota(jnp.int32, v.shape, 1)
    zero = jnp.zeros_like(v)
    return jnp.concatenate([jnp.where(lane < HDIM, v, zero), jnp.where(lane < HDIM, zero, v)], axis=0)


def unpair(t):
    n = t.shape[1] // 2
    return jnp.concatenate([t[:HDIM, :n], t[HDIM:, n:]], axis=0).T


def self_mask(lengths, g):
    key = lax.broadcasted_iota(jnp.int32, (128, 256), 0)
    query = lax.broadcasted_iota(jnp.int32, (128, 256), 1) % 128
    late = key >= SEQ
    limit = jnp.where(late, lengths[2 * g + 1], lengths[2 * g]) + NQ
    slot = jnp.where(late, key - SEQ, key)
    return jnp.logical_and(late == (query >= SEQ), slot < limit)


def cross_mask(counts, rows, images):
    shape = (images * KEYS, 2 * rows)
    key = lax.broadcasted_iota(jnp.int32, shape, 0)
    caption = (lax.broadcasted_iota(jnp.int32, (1, 2 * rows), 1) % rows) // NQ
    shows = jnp.zeros_like(caption)
    total = 0
    for i in range(images):
        total = total + counts[0, i]
        shows = shows + (caption >= total).astype(jnp.int32)
    image = jnp.zeros_like(key)
    for i in range(1, images):
        image = image + (key >= i * KEYS).astype(jnp.int32)
    return jnp.logical_and(image == shows, key - image * KEYS < PATCH)


def softmax_down(s):
    e = jnp.exp(s - jnp.max(s, axis=0, keepdims=True))
    return e * (1.0 / jnp.sum(e, axis=0, keepdims=True))


VEC_ROWS = 13
(
    B_QUERY,
    B_VALUE,
    B_OUT,
    GAIN_1,
    SHIFT_1,
    B_CQUERY,
    B_CVALUE,
    B_COUT,
    GAIN_2,
    SHIFT_2,
    B_CONTRACT,
    GAIN_3,
    SHIFT_3,
) = range(VEC_ROWS)


def lanes_at(i, size=128):
    return pl.ds(pl.multiple_of(i * size, 128), size)


def forward_steps(r):
    tokens = r.x.shape[0]
    rows = tokens // 2
    half = tokens // 2
    images, feat = r.feats.shape[0], r.feats.shape[2]
    keys = images * KEYS
    pairs = D // 128

    def vec(i):
        return r.vec[i : i + 1, :]

    gain_v, shift_v = r.vec_feat[0:1, :], r.vec_feat[1:2, :]
    for image in range(images):

        def vision_step(i, carry):
            xhat, _ = norm_parts(r.feats[image, rows_at(i * 64, 64), :].astype(F32))
            to = rows_at(image * KEYS + i * 64, 64)
            r.vision[to, :] = (xhat * gain_v + shift_v).astype(LOW)
            r.xhat_v[to, :] = xhat.astype(LOW)
            return carry

        lax.fori_loop(0, PATCH // 64, vision_step, 0)
        xhat, _ = norm_parts(r.feats[image, PATCH - 1 : PATCH, :].astype(F32))
        only = lax.broadcasted_iota(jnp.int32, (16, feat), 0) == 0
        to = pl.ds(image * KEYS + PATCH - 1, 16)
        r.vision[to, :] = jnp.where(only, xhat * gain_v + shift_v, 0.0).astype(LOW)
        r.xhat_v[to, :] = jnp.where(only, xhat, 0.0).astype(LOW)
        r.step()
    r.shown[...] = jnp.where(cross_mask(r.counts, rows, images), 3e38, -3e38)
    r.save(K.vision, K.xhat_v)

    def project_to(dst, weight, bias):
        def step(i, carry):
            at = rows_at(i * half, half)
            out = mm(r.x[at, :], weight[...])
            if bias is not None:
                out = out + vec(bias)
            dst[at, :] = out.astype(LOW)
            return carry

        lax.fori_loop(0, 2, step, 0)

    def self_step(i, carry):
        lanes = lanes_at(i)
        for g in range(tokens // 128):
            at = pl.ds(g * 128, 128)
            s = mm(r.k[at, lanes], pair_lanes(r.q[at, lanes] * SCALE), NT)
            p = softmax_down(jnp.where(self_mask(r.lengths, g), s, MASKED)).astype(LOW)
            r.p_self[i, g] = p
            r.mixed[at, lanes] = unpair(mm(r.v[at, lanes], p, TN)).astype(LOW)
        return carry

    r.need(2)
    r.save_weights(1)
    project_to(r.q, r.w_self(0), B_QUERY)
    r.step()
    project_to(r.k, r.w_self(1), None)
    project_to(r.v, r.w_self(2), B_VALUE)
    r.step()
    lax.fori_loop(0, pairs // 2, self_step, 0)
    r.step()
    lax.fori_loop(pairs // 2, pairs, self_step, 0)
    r.save(K.q, K.k, K.v, K.p_self, K.mixed)
    r.step()

    def out_step(i, carry):
        at = rows_at(i * half, half)
        v = r.x[at, :].astype(F32) + (mm(r.mixed[at, :], r.w_self(3)[...]) + vec(B_OUT))
        xhat, scale = norm_parts(v)
        r.xhat1[at, :] = xhat
        r.r1[at, :] = jnp.broadcast_to(scale, (half, 128))
        r.joined[at, :] = xhat * vec(GAIN_1) + vec(SHIFT_1)
        return carry

    lax.fori_loop(0, 2, out_step, 0)
    for c in range(tokens // SEQ):
        r.cross_in[pl.ds(c * NQ, NQ), :] = r.joined[pl.ds(c * SEQ, NQ), :].astype(LOW)
    r.save(K.xhat1, K.r1, K.cross_in)
    r.need(5)
    r.save_weights(2)
    for image in range(images):
        at = pl.ds(image * KEYS, KEYS)
        r.ck[at, :] = mm(r.vision[at, :], r.w_ckey[...]).astype(LOW)
        r.cv[at, :] = (mm(r.vision[at, :], r.w_cvalue[...]) + vec(B_CVALUE)).astype(LOW)
        if image == 1:
            r.step()
    r.save(K.ck, K.cv)
    r.need(6)
    r.save_weights(3)
    r.cq[...] = (mm(r.cross_in[...], r.w_cross(0)[...]) + vec(B_CQUERY)).astype(LOW)

    def cross_step(i, carry):
        lanes = lanes_at(i)
        s = mm(r.ck[:, lanes], pair_lanes(r.cq[:, lanes] * SCALE), NT)
        p = softmax_down(jnp.minimum(s, r.shown[...])).astype(LOW)
        r.keep_cross(i, p)
        r.cmixed[:, lanes] = unpair(mm(r.cv[:, lanes], p, TN)).astype(LOW)
        return carry

    for first in range(0, pairs, 2):
        r.step()
        lax.fori_loop(first, first + 2, cross_step, 0)
    r.save(K.cq, K.cmixed)
    r.step()
    branch = mm(r.cmixed[...], r.w_cross(1)[...]) + vec(B_COUT)
    for c in range(tokens // SEQ):
        own, at = pl.ds(c * NQ, NQ), pl.ds(c * SEQ, NQ)
        xhat, scale = norm_parts(r.joined[at, :] + branch[c * NQ : (c + 1) * NQ, :])
        r.xhat2[own, :] = xhat
        r.r2[own, :] = jnp.broadcast_to(scale, (NQ, 128))
        r.joined[at, :] = xhat * vec(GAIN_2) + vec(SHIFT_2)
    r.joined_low[...] = r.joined[...].astype(LOW)
    r.save(K.xhat2, K.r2, K.joined_low)
    tile = 768
    tiles = r.active.shape[0]
    r.need(9)
    r.save_weights(4)

    def wide_step(n, carry):
        at = rows_at(n * tile, tile)
        r.before_slope(n)
        for m in range(2):
            part = pl.ds(m * half, half)
            wide = mm(r.joined_low[part, :], r.w_expand[at, :], NT) + r.vec_ff[0:1, lanes_at(n, tile)]
            cdf = 0.5 * (1.0 + erf_of(wide * 0.7071067811865476))
            slope = cdf + wide * (jnp.exp(-0.5 * wide * wide) * 0.3989422804014327)
            r.active[n, part, :] = (wide * cdf).astype(LOW)
            r.slope[n % 2, part, :] = slope.astype(LOW)
        r.after_slope(n)
        return carry

    for first in range(0, tiles, 2):
        lax.fori_loop(first, first + 2, wide_step, 0)
        r.step()
    r.need(12)
    r.save_weights(5)
    gain3, shift3, bias3 = vec(GAIN_3), vec(SHIFT_3), vec(B_CONTRACT)
    zero = jnp.zeros((1, D), F32)
    dgain, dshift = zero, zero
    for m in range(2):
        part = pl.ds(m * half, half)

        def narrow_step(n, carry):
            return carry + mm(r.active[n, part, :], r.w_contract[rows_at(n * tile, tile), :])

        r.acc[...] = lax.fori_loop(0, tiles, narrow_step, jnp.zeros((half, D), F32))

        def last_step(i, carry):
            at = rows_at(m * half + i * 64, 64)
            xhat, scale = norm_parts(r.joined[at, :] + (r.acc[rows_at(i * 64, 64), :] + bias3))
            r.layer_out[at, :] = xhat * gain3 + shift3
            dy = r.out_grad[at, :].astype(F32)
            r.dthree[at, :] = norm_back(dy, xhat, scale, gain3)
            return (
                carry[0] + jnp.sum(dy * xhat, axis=0, keepdims=True),
                carry[1] + jnp.sum(dy, axis=0, keepdims=True),
            )

        dgain, dshift = lax.fori_loop(0, half // 64, last_step, (dgain, dshift))
    r.dvec3[...] = jnp.zeros_like(r.dvec3)
    r.dvec3[0:1, :] = dgain
    r.dvec3[1:2, :] = dshift
    r.save(K.dthree, K.layer_out, K.dvec3)


def spread(size, width, taken, offset):
    row = lax.broadcasted_iota(jnp.int32, (size, width), 0)
    lane = lax.broadcasted_iota(jnp.int32, (size, width), 1)
    return jnp.logical_and(lane == row + offset, row < taken).astype(F32).astype(LOW)


def build_vectors(rows, vec, vec_feat, vec_ff):
    feat, ff = vec_feat.shape[1], vec_ff.shape[1]
    one, two, three = D // 8, feat // 8, ff // 8
    total = jnp.zeros(vec.shape, F32)
    total_feat = jnp.zeros((16, feat), F32)
    for d in range(8):
        part = rows[0, d // 2, d % 2, 0:16, :]
        total = total + mm(part[:, :128], spread(128, D, one, one * d))
        total_feat = total_feat + mm(part[:, :256], spread(256, feat, two, two * d))
        vec_ff[0:1, d * three : (d + 1) * three] = part[15:16, :three].astype(F32)
    vec[...] = total
    vec_feat[0:2, :] = total_feat[VEC_ROWS : VEC_ROWS + 2]


def column_sum(v):
    return jnp.sum(v.astype(F32), axis=0, keepdims=True)


def weight_into(target, a, b, at=0, block=256):
    width = a.shape[1]
    for start in range(0, width, block):
        size = min(block, width - start)
        target[pl.ds(at + start, size), :] = mm(a[:, start : start + size], b[...], TN).astype(LOW)


def backward_ffn(r):
    tokens = r.dthree.shape[0]
    half = tokens // 2
    tile = 768
    tiles = r.w_contract.shape[0] // tile
    r.wait(K.dthree, WEIGHT_LOAD + 5)
    r.dn[...] = r.dthree[...].astype(LOW)
    r.dvec[B_CONTRACT : B_CONTRACT + 1, :] = column_sum(r.dn[...])

    def contract_step(n, carry):
        slot = r.ffn_tile(n)
        total = jnp.zeros((1, tile), F32)
        at = rows_at(n * tile, tile)
        for m in range(2):
            part = pl.ds(m * half, half)
            up = mm(r.dn[part, :], r.w_contract[at, :], NT)
            wide = (up * r.slope[slot, part, :].astype(F32)).astype(LOW)
            r.dwide[n, part, :] = wide
            total = total + column_sum(wide)
        r.dvec_ff[0:1, lanes_at(n, tile)] = total
        for j in range(3):
            lanes = slice(j * 256, (j + 1) * 256)
            to = rows_at(n * tile + j * 256, 256)
            r.w_contract[to, :] = mm(r.active[slot, :, lanes], r.dn[...], TN).astype(LOW)
        return carry

    lax.fori_loop(0, tiles, contract_step, 0)
    r.begin(3, 5)
    r.wait(K.joined_low, WEIGHT_LOAD + 4)

    def expand_step(n, carry):
        at = rows_at(n * tile, tile)
        for m in range(2):
            part = pl.ds(m * half, half)
            r.dthree[part, :] += mm(r.dwide[n, part, :], r.w_expand[at, :])
        for j in range(3):
            lanes = slice(j * 256, (j + 1) * 256)
            to = rows_at(n * tile + j * 256, 256)
            r.w_expand[to, :] = mm(r.dwide[n, :, lanes], r.joined_low[...], TN).astype(LOW)
        return carry

    for first in range(tiles):
        lax.fori_loop(first, first + 1, expand_step, 0)
        r.step()
    r.begin(3, 4)


def backward_cross(r):
    tokens = r.dthree.shape[0]
    rows = tokens // 2
    keys = r.ck.shape[0]
    r.wait(K.xhat2, K.r2, K.cmixed, WEIGHT_LOAD + 3)
    gain = r.vec[GAIN_2 : GAIN_2 + 1, :]
    dgain, dshift = jnp.zeros((1, D), F32), jnp.zeros((1, D), F32)
    for c in range(tokens // SEQ):
        own, at = pl.ds(c * NQ, NQ), pl.ds(c * SEQ, NQ)
        dy, xhat = r.dthree[at, :], r.xhat2[own, :]
        dgain = dgain + column_sum(dy * xhat)
        dshift = dshift + column_sum(dy)
        dtwo = norm_back(dy, xhat, r.r2[own, 0:1], gain)
        r.dthree[at, :] = dtwo
        r.dcb[own, :] = dtwo.astype(LOW)
    r.dvec[GAIN_2 : GAIN_2 + 1, :] = dgain
    r.dvec[SHIFT_2 : SHIFT_2 + 1, :] = dshift
    r.dvec[B_COUT : B_COUT + 1, :] = column_sum(r.dcb[...])
    r.dcm[...] = mm(r.dcb[...], r.w_cross(1)[...], NT).astype(LOW)
    weight_into(r.w_cross(1), r.cmixed[...], r.dcb)
    r.step()
    r.wait(K.ck, K.cv, K.cq)

    def step(i, carry):
        lanes = lanes_at(i)
        slot = r.cross_tile(i)
        low = r.p_cross[slot]
        p = low.astype(F32)
        up = pair_lanes(r.dcm[:, lanes])
        dp = mm(r.cv[:, lanes], up, NT)
        ds = (p * (dp - jnp.sum(p * dp, axis=0, keepdims=True))).astype(LOW)
        r.cv[:, lanes] = mm(low, up).astype(LOW)
        dq = unpair(mm(r.ck[:, lanes], ds, TN)) * SCALE
        r.ck[:, lanes] = (mm(ds, pair_lanes(r.cq[:, lanes])) * SCALE).astype(LOW)
        r.dcq[:, lanes] = dq.astype(LOW)
        return carry

    for first in range(0, D // 128, 2):
        lax.fori_loop(first, first + 2, step, 0)
        r.step()
    r.dvec[B_CVALUE : B_CVALUE + 1, :] = column_sum(r.cv[...])
    r.dvec[B_CQUERY : B_CQUERY + 1, :] = column_sum(r.dcq[...])
    r.wait(WEIGHT_LOAD + 2, K.vision, K.xhat_v, K.cross_in)
    feat = r.vision.shape[1]
    zero = jnp.zeros((1, feat), F32)

    def vision_step(i, carry):
        at = rows_at(i * KEYS, KEYS)
        up = mm(r.ck[at, :], r.w_ckey[...], NT) + mm(r.cv[at, :], r.w_cvalue[...], NT)
        return (
            carry[0] + column_sum(up * r.xhat_v[at, :].astype(F32)),
            carry[1] + column_sum(up),
        )

    carry = (zero, zero)
    for image in range(keys // KEYS):
        carry = vision_step(image, carry)
        if image == 1:
            r.step()
    dgain, dshift = carry
    r.dvec_feat[VEC_ROWS : VEC_ROWS + 1, :] = dgain
    r.dvec_feat[VEC_ROWS + 1 : VEC_ROWS + 2, :] = dshift
    r.step()
    for start, size in ((0, 512), (512, 512), (1024, 384)):
        columns = r.vision[:, start : start + size]
        r.w_ckey[pl.ds(start, size), :] = mm(columns, r.ck[...], TN).astype(LOW)
        r.w_cvalue[pl.ds(start, size), :] = mm(columns, r.cv[...], TN).astype(LOW)
        r.step()
    r.begin(2, 2)
    back = mm(r.dcq[...], r.w_cross(0)[...], NT)
    for c in range(tokens // SEQ):
        at = pl.ds(c * SEQ, NQ)
        r.dthree[at, :] += back[c * NQ : (c + 1) * NQ, :]
    weight_into(r.w_cross(0), r.cross_in[...], r.dcq)
    r.begin(2, 3)
    r.step()


def backward_self(r):
    tokens = r.dthree.shape[0]
    half = tokens // 2
    r.wait(K.xhat1, K.r1, K.mixed, WEIGHT_LOAD + 1)
    gain = r.vec[GAIN_1 : GAIN_1 + 1, :]
    zero = jnp.zeros((1, D), F32)

    def norm_step(i, carry):
        at = rows_at(i * 128, 128)
        dy, xhat = r.dthree[at, :], r.xhat1[at, :]
        done = norm_back(dy, xhat, r.r1[at, 0:1], gain)
        r.dthree[at, :] = done
        low = done.astype(LOW)
        r.dn[at, :] = low
        return (
            carry[0] + column_sum(dy * xhat),
            carry[1] + column_sum(dy),
            carry[2] + column_sum(low),
        )

    dgain, dshift, dbias = lax.fori_loop(0, tokens // 128, norm_step, (zero, zero, zero))
    r.dvec[GAIN_1 : GAIN_1 + 1, :] = dgain
    r.dvec[SHIFT_1 : SHIFT_1 + 1, :] = dshift
    r.dvec[B_OUT : B_OUT + 1, :] = dbias
    for m in range(2):
        part = pl.ds(m * half, half)
        r.dm[part, :] = mm(r.dn[part, :], r.w_self(3)[...], NT).astype(LOW)
    weight_into(r.w_self(3), r.mixed[...], r.dn)
    r.begin(1)
    r.step()
    r.wait(K.q, K.k, K.v, K.p_self)

    def step(i, carry):
        lanes = lanes_at(i)
        for g in range(tokens // 128):
            at = pl.ds(g * 128, 128)
            low = r.p_self[i, g]
            p = low.astype(F32)
            up = pair_lanes(r.dm[at, lanes])
            dp = mm(r.v[at, lanes], up, NT)
            ds = (p * (dp - jnp.sum(p * dp, axis=0, keepdims=True))).astype(LOW)
            dq = unpair(mm(r.k[at, lanes], ds, TN)) * SCALE
            dk = mm(ds, pair_lanes(r.q[at, lanes])) * SCALE
            r.v[at, lanes] = mm(low, up).astype(LOW)
            r.q[at, lanes] = dq.astype(LOW)
            r.k[at, lanes] = dk.astype(LOW)
        return carry

    for first in range(0, D // 128, 2):
        lax.fori_loop(first, first + 2, step, 0)
        r.step()
    r.dvec[B_QUERY : B_QUERY + 1, :] = column_sum(r.q[...])
    r.dvec[B_VALUE : B_VALUE + 1, :] = column_sum(r.v[...])
    r.wait(X_LOAD)
    for j, ref in enumerate((r.q, r.k, r.v)):
        for m in range(2):
            part = pl.ds(m * half, half)
            r.dthree[part, :] += mm(ref[part, :], r.w_self(j)[...], NT)
        weight_into(r.w_self(j), r.x[...], ref)
        if j == 1:
            r.begin(1)
        r.step()
    r.begin(1, 1)


SUM_PARTS = (
    (corner(5, 0), 0),
    (halved(5, 192), 2),
    (halved(5, 288), 3),
    (corner(4, 0), 1),
    (halved(4, 192), 4),
    (halved(4, 288), 5),
    (Piece(2, True, 48, lambda y, c: y, lambda y, c: 48 * c), 0),
    (Piece(2, False, 80, lambda y, c: c, lambda y, c: 96), 6),
    (Piece(3, True, 32, lambda y, c: y, lambda y, c: 32 * c), 7),
    (Piece(3, False, 32, lambda y, c: c, lambda y, c: 64), 8),
    (Piece(1, False, 48, lambda y, c: 3, lambda y, c: 48 * c), 2),
    (Piece(1, True, 48, lambda y, c: y, lambda y, c: 48 * c), 1),
    (Piece(1, False, 48, lambda y, c: 2, lambda y, c: 48 * c), 3),
    (Piece(0, False, 16, lambda y, c: 0, lambda y, c: 16 * c), 9),
)
SUM_PIECES = tuple(p for p, _ in SUM_PARTS)
LANDING = tuple(b for _, b in SUM_PARTS)
BUFFERS = max(LANDING) + 1
SUM_LAGS = (0, 2, 4, 6, 8, 9)


def next_user(k):
    for later in range(k + 1, len(LANDING)):
        if LANDING[later] == LANDING[k]:
            return later
    return None


def reuses(k):
    return LANDING[k] in LANDING[:k]


class Reduce:
    def __init__(self, grads, outs, refs):
        total = len(SUM_PIECES)
        self.grads, self.outs = grads, outs
        self.from_c, self.from_y, self.from_x, self.from_z = (
            refs[i * BUFFERS : (i + 1) * BUFFERS] for i in range(4)
        )
        refs = refs[4 * BUFFERS :]
        self.last, refs = refs[:total], refs[total:]
        self.done, self.credit, self.cs, self.ys, self.xs, self.zs, self.fs = refs[:7]
        self.cs_s, self.ys_s, self.xs_s, self.zs_s, self.fs_s = refs[7:]
        y, c, z, x = self.me = place()
        self.zp = [lax.rem(z + i, 4) for i in (1, 2, 3)]
        self.to_z = [at_device(y, c, p, x) for p in self.zp]
        self.back_z = [at_device(y, c, lax.rem(z + 4 - i, 4), x) for i in (1, 2, 3)]
        self.to_x, self.to_y = at_device(y, c, z, 1 - x), at_device(1 - y, c, z, x)
        self.to_c, self.to_d = at_device(y, 1 - c, z, x), at_device(1 - y, 1 - c, z, x)
        self.sent, self.stored, self.slot_at, self.begun = [], [], 0, 0
        self.z_sends = {}
        greet(self.to_z + [self.to_x, self.to_y, self.to_c, self.to_d])

    def go(self, *spec):
        copy = remote(*spec)
        copy.start()
        self.sent.append(copy)
        return copy

    def arrived(self, dst, recv, send):
        remote(dst, dst, send, recv, self.to_x).wait_recv()

    def sides(self, k):
        y = self.me[0]
        return (y, 1 - y) if SUM_PIECES[k].four else (y,)

    def owe(self, k, i, device):
        later = next_user(k)
        if later is not None:
            pl.semaphore_signal(
                self.credit.at[later, i], inc=1, device_id=device, device_id_type=MESH
            )

    def ask(self, k, i):
        if reuses(k):
            pl.semaphore_wait(self.credit.at[k, i], 1)

    def begin(self, count):
        c = self.me[1]
        for k in range(self.begun, self.begun + count):
            p = SUM_PIECES[k]
            self.ask(k, 0)
            for j, yy in enumerate(self.sides(k)):
                land = self.from_c[LANDING[k]].at[j]
                self.go(p.every(self.grads, yy, 1 - c), land, self.cs_s.at[k, j], self.cs.at[k, j], self.to_c)
        self.begun += count

    def stage_c(self, k):
        y, c, z, x = self.me
        p, buf = SUM_PIECES[k], self.from_c[LANDING[k]]
        sides = self.sides(k)
        for j in reversed(range(len(sides))):
            self.arrived(buf.at[j], self.cs.at[k, j], self.cs_s.at[k, j])
            for i in range(4):
                for l in range(2):
                    mine = p.at(self.grads, sides[j], c, i, l)
                    mine[...] = mine[...] + buf[j, i, l]
            if j == 1:
                self.ask(k, 1)
                mine = p.every(self.grads, sides[1], c)
                self.go(mine, self.from_y[LANDING[k]], self.ys_s.at[k], self.ys.at[k], self.to_y)
        self.owe(k, 0, self.to_c)

    def stage_y(self, k):
        y, c, z, x = self.me
        p = SUM_PIECES[k]
        if p.four:
            buf = self.from_y[LANDING[k]]
            self.arrived(buf, self.ys.at[k], self.ys_s.at[k])
            for i in range(4):
                for l in range(2):
                    mine = p.at(self.grads, y, c, i, l)
                    mine[...] = mine[...] + buf[i, l]
            self.owe(k, 1, self.to_y)
        self.ask(k, 2)
        far = p.column(self.grads, y, c, 1 - x)
        self.go(far, self.from_x[LANDING[k]], self.xs_s.at[k], self.xs.at[k], self.to_x)

    def stage_x(self, k):
        y, c, z, x = self.me
        p, buf = SUM_PIECES[k], self.from_x[LANDING[k]]
        self.arrived(buf, self.xs.at[k], self.xs_s.at[k])
        for i in range(4):
            buf[i] = buf[i] + p.at(self.grads, y, c, i, x)[...]
        land = self.from_z[LANDING[k]]
        self.z_sends[k] = []
        for i in range(3):
            self.ask(k, 3 + i)
            copy = remote(buf.at[self.zp[i]], land.at[i], self.zs_s.at[k, i], self.zs.at[k, i], self.to_z[i])
            copy.start()
            self.z_sends[k].append(copy)

    def stage_z(self, k):
        y, c, z, x = self.me
        p, buf, land, last = SUM_PIECES[k], self.from_x[LANDING[k]], self.from_z[LANDING[k]], self.last[k]
        for i in range(3):
            self.arrived(land.at[i], self.zs.at[k, i], self.zs_s.at[k, i])
        value = buf[z].astype(F32)
        for i in range(3):
            value = value + land[i].astype(F32)
        last[0] = value.astype(LOW)
        if p.four:
            out = p.shard(self.outs, y, c)
            for j, device in enumerate((self.to_y, self.to_c, self.to_d)):
                self.go(last.at[0], out, self.fs_s.at[k, j], self.fs.at[k, j], device)
            self.put(k, 0)
        else:
            self.go(last.at[0], last.at[1], self.fs_s.at[k, 0], self.fs.at[k, 0], self.to_y)
        for copy in self.z_sends[k]:
            copy.wait_send()
        self.owe(k, 2, self.to_x)
        for i in range(3):
            self.owe(k, 3 + i, self.back_z[i])

    def put(self, k, slot):
        y, c, z, x = self.me
        out = SUM_PIECES[k].shard(self.outs, y, c)
        copy = pltpu.make_async_copy(self.last[k].at[slot], out, self.done.at[k])
        copy.start()
        self.stored.append(copy)

    def stage_f(self, k):
        y, c, z, x = self.me
        p, last = SUM_PIECES[k], self.last[k]
        if not p.four:
            self.arrived(last.at[1], self.fs.at[k, 0], self.fs_s.at[k, 0])
            last[2] = last[0] + last[1]
            out = p.shard(self.outs, y, c)
            self.go(last.at[2], out, self.fs_s.at[k, 1], self.fs.at[k, 1], self.to_c)
            self.put(k, 2)

    def stage_g(self, k):
        y, c, z, x = self.me
        p = SUM_PIECES[k]
        if p.four:
            places = ((1 - y, c), (y, 1 - c), (1 - y, 1 - c))
            for j, (yy, cc) in enumerate(places):
                self.arrived(p.shard(self.outs, yy, cc), self.fs.at[k, j], self.fs_s.at[k, j])
        else:
            self.arrived(p.shard(self.outs, y, 1 - c), self.fs.at[k, 1], self.fs_s.at[k, 1])

    def advance(self, slots):
        total = len(SUM_PIECES)
        stages = (self.stage_c, self.stage_y, self.stage_x, self.stage_z, self.stage_f, self.stage_g)
        while self.slot_at < slots:
            if self.slot_at >= self.begun < total:
                return
            for lag, stage in zip(SUM_LAGS, stages):
                if 0 <= self.slot_at - lag < total:
                    stage(self.slot_at - lag)
            self.slot_at += 1

    def step(self):
        self.advance(self.slot_at + 1)

    def end(self):
        self.advance(len(SUM_PIECES) + SUM_LAGS[-1])
        for copy in self.sent:
            copy.wait_send()
        for copy in self.stored:
            copy.wait()


def reduce_scratch():
    total, dma = len(SUM_PIECES), pltpu.SemaphoreType.DMA
    first = [SUM_PIECES[LANDING.index(b)] for b in range(BUFFERS)]
    pairs = [dma((total, 2)), dma((total,)), dma((total,)), dma((total, 3)), dma((total, 3))]
    return (
        [pltpu.VMEM((2 if p.four else 1, 4, 2, p.size, D), LOW) for p in first]
        + [pltpu.VMEM((4, 2, p.size, D) if p.four else (1, 1, 16, 128), LOW) for p in first]
        + [pltpu.VMEM((4, p.size, D), LOW) for p in first]
        + [pltpu.VMEM((3, p.size, D), LOW) for p in first]
        + [pltpu.VMEM((1 if p.four else 3, p.size, D), LOW) for p in SUM_PIECES]
        + [dma((total,)), pltpu.SemaphoreType.REGULAR((total, 6))]
        + pairs
        + pairs
    )


def pack_vectors(rows, dvec, dvec_feat, dvec_ff):
    feat, ff = dvec_feat.shape[1], dvec_ff.shape[1]
    one, two, three = D // 8, feat // 8, ff // 8
    low, low_feat = dvec[...].astype(LOW), dvec_feat[...].astype(LOW)
    row = lax.broadcasted_iota(jnp.int32, (16, three), 0)
    for d in range(8):
        small = mm(low, spread(128, D, one, one * d), NT)
        wide = mm(low_feat, spread(256, feat, two, two * d), NT)
        block = jnp.concatenate([small + wide[:, :128], wide[:, 128:], jnp.zeros((16, three - 256), F32)], axis=1)
        block = jnp.where(row == 15, dvec_ff[0:1, d * three : (d + 1) * three], block)
        rows[0, d // 2, d % 2, 0:16, :three] = block.astype(LOW)
        rows[0, d // 2, d % 2, 0:16, three:] = jnp.zeros((16, D - three), LOW)
        rows[0, d // 2, d % 2, 16:32, :] = jnp.zeros((16, D), LOW)


class Refs:
    def __init__(self, **names):
        self.__dict__.update(names)


class Saved(typing.NamedTuple):
    vision: typing.Any
    xhat_v: typing.Any
    q: typing.Any
    k: typing.Any
    v: typing.Any
    p_self: typing.Any
    mixed: typing.Any
    xhat1: typing.Any
    r1: typing.Any
    cross_in: typing.Any
    ck: typing.Any
    cv: typing.Any
    cq: typing.Any
    cmixed: typing.Any
    xhat2: typing.Any
    r2: typing.Any
    joined_low: typing.Any
    dthree: typing.Any
    layer_out: typing.Any
    dvec3: typing.Any
    vec: typing.Any
    active: typing.Any
    slope: typing.Any
    p_cross: typing.Any


K = Saved(*range(len(Saved._fields)))
HELD = K.vec + 1
X_LOAD, WEIGHT_LOAD = 100, 200
VMEM_BYTES = 63 * 1024 * 1024


def saved_shapes(tokens, images, feat, ff):
    rows, keys = tokens // 2, images * KEYS
    return Saved(
        vision=((keys, feat), LOW),
        xhat_v=((keys, feat), LOW),
        q=((tokens, D), LOW),
        k=((tokens, D), LOW),
        v=((tokens, D), LOW),
        p_self=((D // 128, tokens // 128, 128, 256), LOW),
        mixed=((tokens, D), LOW),
        xhat1=((tokens, D), F32),
        r1=((tokens, 128), F32),
        cross_in=((rows, D), LOW),
        ck=((keys, D), LOW),
        cv=((keys, D), LOW),
        cq=((rows, D), LOW),
        cmixed=((rows, D), LOW),
        xhat2=((rows, D), F32),
        r2=((rows, 128), F32),
        joined_low=((tokens, D), LOW),
        dthree=((tokens, D), F32),
        layer_out=((tokens, D), F32),
        dvec3=((8, D), F32),
        vec=((16, D), F32),
        active=((ff // 768, tokens, 768), LOW),
        slope=((ff // 768, tokens, 768), LOW),
        p_cross=((D // 128, keys, 2 * rows), LOW),
    )


def full_views(full):
    def flat(ref, j):
        return ref.at[j].reshape(8 * ref.shape[3], D)

    return dict(
        w_self=lambda j: flat(full[1], j),
        w_ckey=flat(full[2], 0),
        w_cvalue=flat(full[2], 1),
        w_cross=lambda j: flat(full[3], j),
        w_expand=flat(full[4], 0),
        w_contract=flat(full[5], 0),
    )


def forward_kernel(fast, *refs):
    count = len(ARRAY_ROWS)
    (counts, lengths, x, feats, out_grad), refs = refs[:5], refs[5:]
    own, refs = refs[:count], refs[count:]
    if not fast:
        vec_in, refs = refs[:3], refs[3:]
    outs, refs = Saved(*refs[: len(K)]), refs[len(K) :]
    weights, refs = refs[: count - 1], refs[count - 1 :]
    held, refs = refs[:HELD], refs[HELD:]
    full, refs = refs[:count], refs[count:]
    vec_feat, vec_ff, joined, acc, shown, active, slope, pbuf = refs[:8]
    save_sem, weight_sem, active_sem, slope_sem, p_sem = refs[8:13]
    kept = dict(zip(Saved._fields, held))
    vec = kept[Saved._fields[K.vec]]
    pairs, tiles = outs.p_cross.shape[0], outs.slope.shape[0]
    copies = []

    def begin(copy):
        copy.start()
        copies.append(copy)

    def save(*names):
        for i in names:
            begin(pltpu.make_async_copy(held[i], outs[i], save_sem.at[i]))

    def save_weights(i):
        begin(pltpu.make_async_copy(full[i], weights[i - 1], weight_sem.at[i]))

    def p_copy(i):
        return pltpu.make_async_copy(pbuf.at[i % 2], outs.p_cross.at[i], p_sem.at[i % 2])

    def slope_copy(n):
        return pltpu.make_async_copy(slope.at[n % 2], outs.slope.at[n], slope_sem.at[n % 2])

    def active_copy(n):
        return pltpu.make_async_copy(active.at[n], outs.active.at[n], active_sem.at[n])

    def keep_cross(i, p):
        @pl.when(i >= 2)
        def _():
            p_copy(i - 2).wait()

        pbuf[i % 2] = p
        p_copy(i).start()

    def before_slope(n):
        @pl.when(n >= 2)
        def _():
            slope_copy(n - 2).wait()

    def after_slope(n):
        slope_copy(n).start()
        active_copy(n).start()

    if fast:
        gather = Gather(own, full, refs[13:])
        gather.start()
        gather.vectors()
        build_vectors(full[0], vec, vec_feat, vec_ff)
        need = gather.need

        def step():
            gather.advance(gather.slot_at + 1)
    else:
        loads = [pltpu.make_async_copy(own[i], full[i], weight_sem.at[i]) for i in range(count)]
        loads += [
            pltpu.make_async_copy(src, dst, p_sem.at[0])
            for src, dst in zip(vec_in, (vec, vec_feat, vec_ff))
        ]
        for copy in loads:
            copy.start()
            copy.wait()

        def need(k):
            pass

        def step():
            pass

    save(K.vec)
    r = Refs(
        counts=counts,
        lengths=lengths,
        x=x,
        feats=feats,
        out_grad=out_grad,
        **kept,
        **full_views(full),
        vec_feat=vec_feat,
        vec_ff=vec_ff,
        joined=joined,
        acc=acc,
        shown=shown,
        active=active,
        slope=slope,
        save=save,
        save_weights=save_weights,
        need=need,
        step=step,
        keep_cross=keep_cross,
        before_slope=before_slope,
        after_slope=after_slope,
    )
    forward_steps(r)
    for i in (pairs - 2, pairs - 1):
        p_copy(i).wait()
    for n in (tiles - 2, tiles - 1):
        slope_copy(n).wait()
    for n in range(tiles):
        active_copy(n).wait()
    for copy in copies:
        copy.wait()
    if fast:
        gather.end()


def forward_all(fast, counts, lengths, x, feats, out_grad, own, vectors):
    tokens, images, feat = x.shape[0], feats.shape[0], feats.shape[2]
    count = len(ARRAY_ROWS)
    if fast:
        full = [(k, 4, 2, rows, D) for k, rows in ARRAY_ROWS]
    else:
        full = [w.shape for w in own]
    ff = 8 * full[4][3]
    rows, keys = tokens // 2, images * KEYS
    shapes = saved_shapes(tokens, images, feat, ff)
    vmem, smem = pl.BlockSpec(memory_space=pltpu.VMEM), pl.BlockSpec(memory_space=pltpu.SMEM)
    hbm = pl.BlockSpec(memory_space=pl.ANY)
    ins = [counts, lengths, x, feats, out_grad, *own]
    if not fast:
        ins += list(vectors)
    out_shape = [jax.ShapeDtypeStruct(*shape) for shape in shapes]
    out_shape += [jax.ShapeDtypeStruct(shape, LOW) for shape in full[1:]]
    dma = pltpu.SemaphoreType.DMA
    outs = pl.pallas_call(
        functools.partial(forward_kernel, fast),
        name="forward",
        out_shape=out_shape,
        in_specs=[smem, smem] + [vmem] * 3 + [hbm] * (len(ins) - 5),
        out_specs=[hbm] * len(out_shape),
        scratch_shapes=[pltpu.VMEM(*shape) for shape in shapes[:HELD]]
        + [pltpu.VMEM(shape, LOW) for shape in full]
        + [
            pltpu.VMEM((8, feat), F32),
            pltpu.VMEM((8, ff), F32),
            pltpu.VMEM((tokens, D), F32),
            pltpu.VMEM((tokens // 2, D), F32),
            pltpu.VMEM((keys, 2 * rows), F32),
            pltpu.VMEM((ff // 768, tokens, 768), LOW),
            pltpu.VMEM((2, tokens, 768), LOW),
            pltpu.VMEM((2, keys, 2 * rows), LOW),
            dma((HELD,)),
            dma((count,)),
            dma((ff // 768,)),
            dma((2,)),
            dma((2,)),
        ]
        + (gather_semaphores() if fast else []),
        compiler_params=pltpu.CompilerParams(
            vmem_limit_bytes=VMEM_BYTES,
            **(dict(collective_id=0, has_side_effects=True) if fast else {}),
        ),
    )(*ins)
    return Saved(*outs[: len(K)]), list(outs[len(K) :])


LOADS = (K.dthree, K.joined_low, K.xhat2, K.r2, K.cmixed, K.ck, K.cv, K.cq, K.vision, K.xhat_v, K.cross_in)
LOADS += (K.xhat1, K.r1, K.p_self, K.vec, K.dvec3)
LATE = (K.mixed, K.q, K.k, K.v)


def backward_kernel(fast, *refs):
    count = len(ARRAY_ROWS)
    x_in, refs = refs[0], refs[1:]
    ins, refs = Saved(*refs[: len(K)]), refs[len(K) :]
    weights, refs = (None,) + tuple(refs[: count - 1]), refs[count - 1 :]
    input_grad, refs = refs[0], refs[1:]
    if fast:
        outs, refs = refs[:count], refs[count:]
    else:
        vec_outs, outs, refs = refs[:3], (None,) + tuple(refs[3 : count + 2]), refs[count + 2 :]
    held, refs = dict(zip(LOADS, refs)), refs[len(LOADS) :]
    full, refs = refs[:count], refs[count:]
    dvec, dvec_feat, dvec_ff, dn, dwide, abuf, sbuf, pbuf = refs[:8]
    load_sem, w_sem, g_sem, abuf_sem, sbuf_sem, pbuf_sem = refs[8:14]
    x, dm = abuf.at[0], abuf.at[1]
    half = dn.shape[0] // 2
    dcb, dcm, dcq = sbuf.at[0, pl.ds(0, half)], sbuf.at[0, pl.ds(half, half)], sbuf.at[1, pl.ds(0, half)]
    for i, name in enumerate(LATE):
        held[name] = dwide.at[i]
    loads = {i: pltpu.make_async_copy(ins[i], held[i], load_sem.at[i]) for i in LOADS + LATE}
    loads[X_LOAD] = pltpu.make_async_copy(x_in, x, load_sem.at[K.layer_out])
    for i in range(1, count):
        loads[WEIGHT_LOAD + i] = pltpu.make_async_copy(weights[i], full[i], w_sem.at[i])

    def tile_copies(n, slot):
        return (
            pltpu.make_async_copy(ins.active.at[n], abuf.at[slot], abuf_sem.at[slot]),
            pltpu.make_async_copy(ins.slope.at[n], sbuf.at[slot], sbuf_sem.at[slot]),
        )

    def pair_copy(i, slot):
        return pltpu.make_async_copy(ins.p_cross.at[i], pbuf.at[slot], pbuf_sem.at[slot])

    for i in (K.dthree, WEIGHT_LOAD + 5):
        loads[i].start()
    for copy in tile_copies(0, 0):
        copy.start()
    for i in (K.joined_low, WEIGHT_LOAD + 4) + LOADS[2:5] + (WEIGHT_LOAD + 3,) + LOADS[5:8]:
        loads[i].start()
    pair_copy(0, 0).start()
    for i in (WEIGHT_LOAD + 2,) + LOADS[8:] + (WEIGHT_LOAD + 1,):
        loads[i].start()

    def wait(*names):
        for i in names:
            loads[i].wait()

    def ffn_tile(n):
        @pl.when(n + 1 < ins.active.shape[0])
        def _():
            for copy in tile_copies(n + 1, (n + 1) % 2):
                copy.start()

        for copy in tile_copies(n, n % 2):
            copy.wait()
        return n % 2

    def cross_tile(i):
        @pl.when(i + 1 < ins.p_cross.shape[0])
        def _():
            pair_copy(i + 1, (i + 1) % 2).start()

        pair_copy(i, i % 2).wait()
        return i % 2

    stored = []

    def keep(src, dst, sem):
        copy = pltpu.make_async_copy(src, dst, sem)
        copy.start()
        stored.append(copy)

    if fast:
        reduce = Reduce(full, outs, refs[14:])
        step = reduce.step

        def begin(parts, *arrays):
            reduce.begin(parts)
    else:

        def step():
            pass

        def begin(parts, *arrays):
            for i in arrays:
                keep(full[i], outs[i], g_sem.at[i])

    r = Refs(
        **{Saved._fields[i]: ref for i, ref in held.items()},
        **full_views(full),
        x=x,
        dvec=dvec,
        dvec_feat=dvec_feat,
        dvec_ff=dvec_ff,
        dn=dn,
        dwide=dwide,
        dm=dm,
        dcb=dcb,
        dcm=dcm,
        dcq=dcq,
        active=abuf,
        slope=sbuf,
        p_cross=pbuf,
        wait=wait,
        begin=begin,
        step=step,
        ffn_tile=ffn_tile,
        cross_tile=cross_tile,
    )
    dvec[...] = jnp.zeros_like(dvec)
    dvec_feat[...] = jnp.zeros_like(dvec_feat)
    wait(K.vec, K.dvec3)
    dvec[GAIN_3 : GAIN_3 + 2, :] = held[K.dvec3][0:2, :]
    backward_ffn(r)
    for i in LATE + (X_LOAD,):
        loads[i].start()
    backward_cross(r)
    backward_self(r)
    keep(held[K.dthree], input_grad, g_sem.at[0])
    if fast:
        pack_vectors(full[0], dvec, dvec_feat, dvec_ff)
        reduce.begin(1)
        reduce.end()
    else:
        for src, dst, i in zip((dvec, dvec_feat, dvec_ff), vec_outs, LATE):
            keep(src, dst, load_sem.at[i])
    for copy in stored:
        copy.wait()


def backward_all(fast, saved, weights, x):
    tokens, keys, feat = x.shape[0], saved.vision.shape[0], saved.vision.shape[1]
    count = len(ARRAY_ROWS)
    rows, ff = tokens // 2, 8 * weights[3].shape[3]
    hbm = pl.BlockSpec(memory_space=pl.ANY)
    dma = pltpu.SemaphoreType.DMA
    small = [(16, D), (16, feat), (8, ff)]
    out_shape = [jax.ShapeDtypeStruct((tokens, D), F32)]
    if fast:
        out_shape += [jax.ShapeDtypeStruct((k, n, D), LOW) for k, n in ARRAY_ROWS]
    else:
        out_shape += [jax.ShapeDtypeStruct(s, F32) for s in small]
        out_shape += [jax.ShapeDtypeStruct(w.shape, LOW) for w in weights]
    outs = pl.pallas_call(
        functools.partial(backward_kernel, fast),
        name="backward",
        out_shape=out_shape,
        in_specs=[hbm] * (len(K) + count),
        out_specs=[hbm] * len(out_shape),
        scratch_shapes=[pltpu.VMEM(saved[i].shape, saved[i].dtype) for i in LOADS]
        + [pltpu.VMEM((1, 4, 2, 32, D), LOW)]
        + [pltpu.VMEM(w.shape, LOW) for w in weights]
        + [pltpu.VMEM(s, F32) for s in small]
        + [pltpu.VMEM((tokens, D), LOW), pltpu.VMEM((ff // 768, tokens, 768), LOW)]
        + [
            pltpu.VMEM((2, tokens, 768), LOW),
            pltpu.VMEM((2, tokens, 768), LOW),
            pltpu.VMEM((2, keys, 2 * rows), LOW),
            dma((len(K),)),
            dma((count,)),
            dma((count,)),
            dma((2,)),
            dma((2,)),
            dma((2,)),
        ]
        + (reduce_scratch() if fast else []),
        compiler_params=pltpu.CompilerParams(
            vmem_limit_bytes=VMEM_BYTES,
            **(dict(collective_id=1, has_side_effects=True) if fast else {}),
        ),
    )(x, *saved, *weights)
    return outs[0], list(outs[1:])


def pack_rows(vectors):
    rows = [jnp.pad(v, (0, D - v.shape[0])) for v in vectors]
    rows += [jnp.zeros((D,), rows[0].dtype)] * (32 - len(rows))
    return jnp.stack(rows)[None]


def local(
    fast,
    hidden,
    image_feats,
    caption_counts,
    text_lengths,
    out_grad,
    self_query,
    query_bias,
    self_key,
    self_value,
    value_bias,
    self_output,
    output_bias,
    first_gain,
    first_shift,
    cross_query,
    crossquery_bias,
    cross_key,
    cross_value,
    crossvalue_bias,
    cross_output,
    crossoutput_bias,
    second_gain,
    second_shift,
    vision_gain,
    vision_shift,
    expand_weight,
    expand_bias,
    contract_weight,
    contract_bias,
    third_gain,
    third_shift,
):
    low = jnp.bfloat16
    vectors = (
        query_bias,
        value_bias,
        output_bias,
        first_gain,
        first_shift,
        crossquery_bias,
        crossvalue_bias,
        crossoutput_bias,
        second_gain,
        second_shift,
        contract_bias,
        third_gain,
        third_shift,
        vision_gain,
        vision_shift,
        expand_bias,
    )
    own = (
        pack_rows(vectors),
        jnp.stack([self_query, self_key, self_value, self_output]),
        jnp.stack([cross_key, cross_value]),
        jnp.stack([cross_query, cross_output]),
        expand_weight.T[None],
        contract_weight[None],
    )
    feat = image_feats.shape[-1]
    shards = D // self_query.shape[0]
    whole = ()
    if not fast:
        full = [lax.all_gather(s, FSDP, axis=1, tiled=False) for s in own]
        rows = full[0][0]
        each = [rows[:, i, : v.shape[0]].reshape(-1).astype(F32) for i, v in enumerate(vectors)]
        own = [f.reshape(f.shape[0], 4, 2, -1, D) for f in full]
        whole = (
            jnp.stack(each[:VEC_ROWS] + [jnp.zeros((D,), F32)] * (16 - VEC_ROWS)),
            jnp.stack(each[VEC_ROWS : VEC_ROWS + 2] + [jnp.zeros((feat,), F32)] * 6),
            jnp.broadcast_to(each[-1][None], (8, each[-1].shape[0])),
        )
    x = hidden.reshape(-1, D)
    saved, weights = forward_all(
        fast,
        caption_counts,
        text_lengths,
        x,
        image_feats,
        out_grad.reshape(-1, D),
        own,
        whole,
    )
    input_grad, summed = backward_all(fast, saved, weights, x)
    layer_out = saved.layer_out.reshape(hidden.shape)
    input_grad = input_grad.reshape(hidden.shape)
    if not fast:
        dvec, dvec_feat, dvec_ff = summed[:3]
        pieces = [dvec[i] for i in range(VEC_ROWS)]
        pieces += [dvec_feat[VEC_ROWS], dvec_feat[VEC_ROWS + 1], dvec_ff[0]]
        pieces = [v.astype(LOW).reshape(shards, -1) for v in pieces]
        pieces = [jnp.pad(v, ((0, 0), (0, D - v.shape[1]))) for v in pieces]
        packed = jnp.stack(pieces + [jnp.zeros((shards, D), LOW)] * (32 - len(pieces)), axis=1)
        grads = [packed[None]] + [g.reshape(g.shape[0], shards, -1, D) for g in summed[3:]]
        summed = [lax.psum_scatter(g, FSDP, scatter_dimension=1, tiled=False) for g in grads]
        summed = [lax.psum(g, DP) for g in summed]
    sums = [s.astype(F32) for s in summed]
    small = [sums[0][0, i, : v.shape[0]] for i, v in enumerate(vectors)]
    return (
        layer_out,
        input_grad,
        sums[1][0],
        small[0],
        sums[1][1],
        sums[1][2],
        small[1],
        sums[1][3],
        small[2],
        small[3],
        small[4],
        sums[3][0],
        small[5],
        sums[2][0],
        sums[2][1],
        small[6],
        sums[3][1],
        small[7],
        small[8],
        small[9],
        small[13],
        small[14],
        sums[4][0].T,
        small[15],
        sums[5][0],
        small[10],
        small[11],
        small[12],
    )


def solution(mesh):
    fast = mesh.shape[DP] == 4 and mesh.shape[FSDP] == 8
    tokens, pair = P((DP, FSDP), None, None), P((DP, FSDP), None)
    by_row, by_column, flat = P(FSDP, None), P(None, FSDP), P(FSDP)
    params = (
        (by_row, flat, by_row, by_row, flat, by_row, flat, flat, flat)
        + (by_row, flat, by_row, by_row, flat, by_row, flat)
        + (flat,) * 4
        + (by_column, flat, by_row, flat, flat, flat)
    )
    return jax.shard_map(
        functools.partial(local, fast),
        mesh=mesh,
        in_specs=(tokens, tokens, pair, P((DP, FSDP)), tokens) + params,
        out_specs=(tokens, tokens) + params,
        check_vma=False,
    )
```

```python
import functools
import typing

import jax
import jax.numpy as jnp
from jax import lax
from jax.experimental import pallas as pl
from jax.experimental.pallas import tpu as pltpu
from jax.sharding import PartitionSpec as P

D = 768
HEADS = 12
HDIM = 64
PATCH = 257
NQ = 32
SEQ = 64
EPS = 1e-06
MASKED = -1000000000.0


MESH = pl.DeviceIdType.MESH
DP, FSDP = "dp", "fsdp"
SHARD_LANES = 96


def place():
    dp, fs = lax.axis_index(DP), lax.axis_index(FSDP)
    return dp // 2, dp % 2, fs // 2, fs % 2


def at_device(y, c, z, x):
    return (2 * y + c, 2 * z + x)


def rows_at(start, size):
    return pl.ds(pl.multiple_of(start, 16), size)


def greet(peers):
    barrier = pltpu.get_barrier_semaphore()
    for peer in peers:
        pl.semaphore_signal(barrier, inc=1, device_id=peer, device_id_type=MESH)
    pl.semaphore_wait(barrier, len(peers))


class Piece:
    def __init__(self, array, four, size, which, start):
        self.array, self.four, self.size, self.which, self.start = array, four, size, which, start

    def shard(self, refs, y, c):
        return refs[self.array].at[self.which(y, c), rows_at(self.start(y, c), self.size)]

    def at(self, refs, y, c, z, x):
        return refs[self.array].at[self.which(y, c), z, x, rows_at(self.start(y, c), self.size)]

    def column(self, refs, y, c, x):
        return refs[self.array].at[self.which(y, c), :, x, rows_at(self.start(y, c), self.size)]

    def every(self, refs, y, c):
        return refs[self.array].at[self.which(y, c), :, :, rows_at(self.start(y, c), self.size)]


ARRAY_ROWS = ((1, 32), (4, 96), (2, 176), (2, 96), (1, 384), (1, 384))


def corner(array, start):
    return Piece(array, True, 48, lambda y, c: 0, lambda y, c: start + 48 * (2 * y + c))


def halved(array, start):
    return Piece(array, False, 48, lambda y, c: 0, lambda y, c: start + 48 * c)


GATHER_PIECES = (
    Piece(1, True, 32, lambda y, c: 2 * y + c, lambda y, c: 0),
    Piece(1, True, 32, lambda y, c: 2 * y + c, lambda y, c: 32),
    Piece(1, True, 32, lambda y, c: 2 * y + c, lambda y, c: 64),
    Piece(2, True, 48, lambda y, c: y, lambda y, c: 80 * c),
    Piece(2, True, 32, lambda y, c: y, lambda y, c: 80 * c + 48),
    Piece(2, False, 16, lambda y, c: c, lambda y, c: 160),
    Piece(3, True, 48, lambda y, c: y, lambda y, c: 48 * c),
    corner(4, 0),
    halved(4, 192),
    halved(4, 288),
    corner(5, 0),
    halved(5, 192),
    halved(5, 288),
)
GATHER_AHEAD = 3
GATHER_LAGS = (0, 1, 3, 4)
GATHER_SLOTS = len(GATHER_PIECES) + GATHER_LAGS[-1]


def remote(src, dst, send, recv, device):
    return pltpu.make_async_remote_copy(
        src_ref=src, dst_ref=dst, send_sem=send, recv_sem=recv, device_id=device, device_id_type=MESH
    )


class Gather:
    def __init__(self, full, sems):
        self.full = full
        self.here, self.vs, self.zs, self.xs, self.ys, self.cs = sems[:6]
        self.vs_s, self.zs_s, self.xs_s, self.ys_s, self.cs_s = sems[6:]
        y, c, z, x = self.me = place()
        self.zp = [lax.rem(z + i, 4) for i in (1, 2, 3)]
        self.zm = [lax.rem(z + 4 - i, 4) for i in (1, 2, 3)]
        self.to_z = [at_device(y, c, p, x) for p in self.zp]
        self.to_diag = [at_device(y, c, p, 1 - x) for p in self.zp]
        self.to_x, self.to_y = at_device(y, c, z, 1 - x), at_device(1 - y, c, z, x)
        self.to_c = at_device(y, 1 - c, z, x)
        self.sent, self.slot_at = [], 0
        greet(self.to_z + self.to_diag + [self.to_x, self.to_y, self.to_c])

    def go(self, *spec):
        copy = remote(*spec)
        copy.start()
        self.sent.append(copy)

    def arrived(self, dst, recv, send):
        remote(dst, dst, send, recv, self.to_x).wait_recv()

    def start(self, raw, staged, wide, sem):
        y, c, z, x = self.me
        self.own = (raw[0],) + tuple(staged) + (raw[10],)
        places = [(1, 0), (1, 1), (1, 2), (1, 3), (2, 0), (2, 1), (3, 0), (3, 1)]
        loads = [
            pltpu.make_async_copy(raw[1 + i], self.own[array].at[j], sem.at[i])
            for i, (array, j) in enumerate(places)
        ]
        loads.append(pltpu.make_async_copy(raw[9], wide, sem.at[8]))
        for copy in loads:
            copy.start()
        mine = self.full[0].at[0, z, x]
        for i, device in enumerate(self.to_z + self.to_diag + [self.to_x]):
            self.go(self.own[0].at[0], mine, self.vs_s.at[i], self.vs.at[i], device)
        for copy in loads[:4]:
            copy.wait()
        for k in range(GATHER_AHEAD):
            self.send(k)
        for copy in loads[4:]:
            copy.wait()
        self.own[4][0] = wide[...].T
        self.locals = [pltpu.make_async_copy(self.own[0].at[0], mine, self.here.at[0, 0])]
        for k, p in enumerate(GATHER_PIECES):
            for j in range(2 if p.four else 1):
                yy = y if j == 0 else 1 - y
                self.locals.append(
                    pltpu.make_async_copy(
                        p.shard(self.own, yy, c), p.at(self.full, yy, c, z, x), self.here.at[k + 1, j]
                    )
                )
        for copy in self.locals:
            copy.start()
        for copy in self.locals:
            copy.wait()

    def vectors(self):
        y, c, z, x = self.me
        places = [(m, x) for m in self.zm] + [(m, 1 - x) for m in self.zm] + [(z, 1 - x)]
        for i, (zz, xx) in enumerate(places):
            self.arrived(self.full[0].at[0, zz, xx], self.vs.at[i], self.vs_s.at[i])

    def send(self, k):
        y, c, z, x = self.me
        p = GATHER_PIECES[k]
        src, dst = p.shard(self.own, y, c), p.at(self.full, y, c, z, x)
        for i in range(3):
            self.go(src, dst, self.zs_s.at[k, i], self.zs.at[k, i], self.to_z[i])
        self.go(src, dst, self.xs_s.at[k, 0], self.xs.at[k, 0], self.to_x)

    def stage_x(self, k):
        y, c, z, x = self.me
        p = GATHER_PIECES[k]
        for i in range(3):
            got = p.at(self.full, y, c, self.zm[i], x)
            self.arrived(got, self.zs.at[k, i], self.zs_s.at[k, i])
            self.go(got, got, self.xs_s.at[k, i + 1], self.xs.at[k, i + 1], self.to_x)

    def stage_y(self, k):
        y, c, z, x = self.me
        p = GATHER_PIECES[k]
        self.arrived(p.at(self.full, y, c, z, 1 - x), self.xs.at[k, 0], self.xs_s.at[k, 0])
        for i in range(3):
            got = p.at(self.full, y, c, self.zm[i], 1 - x)
            self.arrived(got, self.xs.at[k, i + 1], self.xs_s.at[k, i + 1])
        if p.four:
            far = p.column(self.full, y, c, 1 - x)
            self.go(far, far, self.ys_s.at[k, 0], self.ys.at[k, 0], self.to_y)
            for i in range(3):
                near = p.at(self.full, y, c, self.zm[i], x)
                self.go(near, near, self.ys_s.at[k, i + 1], self.ys.at[k, i + 1], self.to_y)
        mine = p.every(self.full, y, c)
        self.go(mine, mine, self.cs_s.at[k, 0], self.cs.at[k, 0], self.to_c)

    def stage_c(self, k):
        y, c, z, x = self.me
        p = GATHER_PIECES[k]
        if p.four:
            got = p.column(self.full, 1 - y, c, 1 - x)
            self.arrived(got, self.ys.at[k, 0], self.ys_s.at[k, 0])
            for i in range(3):
                got = p.at(self.full, 1 - y, c, self.zm[i], x)
                self.arrived(got, self.ys.at[k, i + 1], self.ys_s.at[k, i + 1])
            mine = p.every(self.full, 1 - y, c)
            self.go(mine, mine, self.cs_s.at[k, 1], self.cs.at[k, 1], self.to_c)

    def finish(self, k):
        y, c, z, x = self.me
        p = GATHER_PIECES[k]
        self.arrived(p.every(self.full, y, 1 - c), self.cs.at[k, 0], self.cs_s.at[k, 0])
        if p.four:
            self.arrived(p.every(self.full, 1 - y, 1 - c), self.cs.at[k, 1], self.cs_s.at[k, 1])

    def advance(self, slots):
        total = len(GATHER_PIECES)
        while self.slot_at < min(slots, GATHER_SLOTS):
            t = self.slot_at
            if GATHER_AHEAD <= t + GATHER_AHEAD < total:
                self.send(t + GATHER_AHEAD)
            stages = (self.stage_x, self.stage_y, self.stage_c, self.finish)
            for lag, stage in zip(GATHER_LAGS, stages):
                if 0 <= t - lag < total:
                    stage(t - lag)
            self.slot_at += 1

    def need(self, k):
        self.advance(k + GATHER_LAGS[-1] + 1)

    def end(self):
        for copy in self.sent:
            copy.wait_send()


def gather_semaphores():
    total, dma = len(GATHER_PIECES), pltpu.SemaphoreType.DMA
    pairs = [dma((7,)), dma((total, 3)), dma((total, 4)), dma((total, 4)), dma((total, 2))]
    return [dma((total + 1, 2))] + pairs + pairs


LOW = jnp.bfloat16
F32 = jnp.float32
KEYS = 272
SCALE = HDIM**-0.5
NN = (((1,), (0,)), ((), ()))
NT = (((1,), (1,)), ((), ()))
TN = (((0,), (0,)), ((), ()))


def mm(a, b, dims=NN):
    return lax.dot_general(a, b, dims, preferred_element_type=F32)


def erf_of(v):
    v = jnp.clip(v, -3.832506856900711, 3.832506856900711)
    s = v * v
    top = jnp.full_like(s, 0.00022905065861350646)
    for k in (0.0034082910107109506, 0.050955695062380861, 0.18520832239976145, 1.128379143519084):
        top = top * s + k
    low = jnp.full_like(s, -1.1791602954361697e-7)
    for k in (0.000023547966471313185, 0.0010179625278914885, 0.014070470171167667, 0.11098505178285362, 0.49746925110067538, 1.0):
        low = low * s + k
    return v * top / low


def norm_parts(v):
    center = v - jnp.mean(v, axis=-1, keepdims=True)
    r = lax.rsqrt(jnp.mean(center * center, axis=-1, keepdims=True) + EPS)
    return center * r, r


def norm_back(dy, xhat, r, gain):
    gdy = gain * dy
    return r * (
        gdy
        - jnp.mean(gdy, axis=-1, keepdims=True)
        - xhat * jnp.mean(gdy * xhat, axis=-1, keepdims=True)
    )


def pair_lanes(v):
    lane = lax.broadcasted_iota(jnp.int32, v.shape, 1)
    zero = jnp.zeros_like(v)
    return jnp.concatenate([jnp.where(lane < HDIM, v, zero), jnp.where(lane < HDIM, zero, v)], axis=0)


def unpair(t):
    n = t.shape[1] // 2
    return jnp.concatenate([t[:HDIM, :n], t[HDIM:, n:]], axis=0).T


def self_mask(lengths, g):
    key = lax.broadcasted_iota(jnp.int32, (128, 256), 0)
    query = lax.broadcasted_iota(jnp.int32, (128, 256), 1) % 128
    late = key >= SEQ
    limit = jnp.where(late, lengths[2 * g + 1], lengths[2 * g]) + NQ
    slot = jnp.where(late, key - SEQ, key)
    return jnp.logical_and(late == (query >= SEQ), slot < limit)


def cross_mask(counts, rows, images):
    shape = (images * KEYS, 2 * rows)
    key = lax.broadcasted_iota(jnp.int32, shape, 0)
    caption = (lax.broadcasted_iota(jnp.int32, (1, 2 * rows), 1) % rows) // NQ
    shows = jnp.zeros_like(caption)
    total = 0
    for i in range(images):
        total = total + counts[0, i]
        shows = shows + (caption >= total).astype(jnp.int32)
    image = jnp.zeros_like(key)
    for i in range(1, images):
        image = image + (key >= i * KEYS).astype(jnp.int32)
    return jnp.logical_and(image == shows, key - image * KEYS < PATCH)


def softmax_down(s):
    e = jnp.exp(s - jnp.max(s, axis=0, keepdims=True))
    return e * (1.0 / jnp.sum(e, axis=0, keepdims=True))


VEC_ROWS = 13
(
    B_QUERY,
    B_VALUE,
    B_OUT,
    GAIN_1,
    SHIFT_1,
    B_CQUERY,
    B_CVALUE,
    B_COUT,
    GAIN_2,
    SHIFT_2,
    B_CONTRACT,
    GAIN_3,
    SHIFT_3,
) = range(VEC_ROWS)


def lanes_at(i, size=128):
    return pl.ds(pl.multiple_of(i * size, 128), size)


def forward_steps(r):
    tokens = r.x.shape[0]
    rows = tokens // 2
    half = tokens // 2
    images, feat = r.feats.shape[0], r.feats.shape[2]
    keys = images * KEYS
    pairs = D // 128

    def vec(i):
        return r.vec[i : i + 1, :]

    gain_v, shift_v = r.vec_feat[0:1, :], r.vec_feat[1:2, :]
    for image in range(images):

        def vision_step(i, carry):
            xhat, _ = norm_parts(r.feats[image, rows_at(i * 64, 64), :].astype(F32))
            to = rows_at(image * KEYS + i * 64, 64)
            r.vision[to, :] = (xhat * gain_v + shift_v).astype(LOW)
            r.xhat_v[to, :] = xhat.astype(LOW)
            return carry

        lax.fori_loop(0, PATCH // 64, vision_step, 0)
        xhat, _ = norm_parts(r.feats[image, PATCH - 1 : PATCH, :].astype(F32))
        only = lax.broadcasted_iota(jnp.int32, (16, feat), 0) == 0
        to = pl.ds(image * KEYS + PATCH - 1, 16)
        r.vision[to, :] = jnp.where(only, xhat * gain_v + shift_v, 0.0).astype(LOW)
        r.xhat_v[to, :] = jnp.where(only, xhat, 0.0).astype(LOW)
        r.step()
    r.shown[...] = jnp.where(cross_mask(r.counts, rows, images), 3e38, -3e38)
    r.save(K.vision, K.xhat_v)

    def project_to(dst, weight, bias):
        def step(i, carry):
            at = rows_at(i * half, half)
            out = mm(r.x[at, :], weight[...])
            if bias is not None:
                out = out + vec(bias)
            dst[at, :] = out.astype(LOW)
            return carry

        lax.fori_loop(0, 2, step, 0)

    def self_step(i, carry):
        lanes = lanes_at(i)
        for g in range(tokens // 128):
            at = pl.ds(g * 128, 128)
            s = mm(r.k[at, lanes], pair_lanes(r.q[at, lanes] * SCALE), NT)
            p = softmax_down(jnp.where(self_mask(r.lengths, g), s, MASKED)).astype(LOW)
            r.p_self[i, g] = p
            r.mixed[at, lanes] = unpair(mm(r.v[at, lanes], p, TN)).astype(LOW)
        return carry

    r.need(2)
    r.save_weights(1)
    project_to(r.q, r.w_self(0), B_QUERY)
    r.step()
    project_to(r.k, r.w_self(1), None)
    project_to(r.v, r.w_self(2), B_VALUE)
    r.step()
    lax.fori_loop(0, pairs // 2, self_step, 0)
    r.step()
    lax.fori_loop(pairs // 2, pairs, self_step, 0)
    r.save(K.q, K.k, K.v, K.p_self, K.mixed)
    r.step()

    def out_step(i, carry):
        at = rows_at(i * half, half)
        v = r.x[at, :].astype(F32) + (mm(r.mixed[at, :], r.w_self(3)[...]) + vec(B_OUT))
        xhat, scale = norm_parts(v)
        r.xhat1[at, :] = xhat
        r.r1[at, :] = jnp.broadcast_to(scale, (half, 128))
        r.joined[at, :] = xhat * vec(GAIN_1) + vec(SHIFT_1)
        return carry

    lax.fori_loop(0, 2, out_step, 0)
    for c in range(tokens // SEQ):
        r.cross_in[pl.ds(c * NQ, NQ), :] = r.joined[pl.ds(c * SEQ, NQ), :].astype(LOW)
    r.save(K.xhat1, K.r1, K.cross_in)
    r.need(5)
    r.save_weights(2)
    for image in range(images):
        at = pl.ds(image * KEYS, KEYS)
        r.ck[at, :] = mm(r.vision[at, :], r.w_ckey[...]).astype(LOW)
        r.cv[at, :] = (mm(r.vision[at, :], r.w_cvalue[...]) + vec(B_CVALUE)).astype(LOW)
        if image == 1:
            r.step()
    r.save(K.ck, K.cv)
    r.need(6)
    r.save_weights(3)
    r.cq[...] = (mm(r.cross_in[...], r.w_cross(0)[...]) + vec(B_CQUERY)).astype(LOW)

    def cross_step(i, carry):
        lanes = lanes_at(i)
        s = mm(r.ck[:, lanes], pair_lanes(r.cq[:, lanes] * SCALE), NT)
        p = softmax_down(jnp.minimum(s, r.shown[...])).astype(LOW)
        r.keep_cross(i, p)
        r.cmixed[:, lanes] = unpair(mm(r.cv[:, lanes], p, TN)).astype(LOW)
        return carry

    for first in range(0, pairs, 2):
        r.step()
        lax.fori_loop(first, first + 2, cross_step, 0)
    r.save(K.cq, K.cmixed)
    r.step()
    branch = mm(r.cmixed[...], r.w_cross(1)[...]) + vec(B_COUT)
    for c in range(tokens // SEQ):
        own, at = pl.ds(c * NQ, NQ), pl.ds(c * SEQ, NQ)
        xhat, scale = norm_parts(r.joined[at, :] + branch[c * NQ : (c + 1) * NQ, :])
        r.xhat2[own, :] = xhat
        r.r2[own, :] = jnp.broadcast_to(scale, (NQ, 128))
        r.joined[at, :] = xhat * vec(GAIN_2) + vec(SHIFT_2)
    r.joined_low[...] = r.joined[...].astype(LOW)
    r.save(K.xhat2, K.r2, K.joined_low)
    tile = 768
    tiles = r.active.shape[0]
    r.need(9)
    r.save_weights(4)

    def wide_step(n, carry):
        at = rows_at(n * tile, tile)
        r.before_slope(n)
        for m in range(2):
            part = pl.ds(m * half, half)
            wide = mm(r.joined_low[part, :], r.w_expand[at, :], NT) + r.vec_ff[0:1, lanes_at(n, tile)]
            cdf = 0.5 * (1.0 + erf_of(wide * 0.7071067811865476))
            slope = cdf + wide * (jnp.exp(-0.5 * wide * wide) * 0.3989422804014327)
            r.active[n, part, :] = (wide * cdf).astype(LOW)
            r.slope[n % 2, part, :] = slope.astype(LOW)
        r.after_slope(n)
        return carry

    for first in range(0, tiles, 2):
        lax.fori_loop(first, first + 2, wide_step, 0)
        r.step()
    r.need(12)
    r.save_weights(5)
    gain3, shift3, bias3 = vec(GAIN_3), vec(SHIFT_3), vec(B_CONTRACT)
    zero = jnp.zeros((1, D), F32)
    dgain, dshift = zero, zero
    for m in range(2):
        part = pl.ds(m * half, half)

        def narrow_step(n, carry):
            return carry + mm(r.active[n, part, :], r.w_contract[rows_at(n * tile, tile), :])

        r.acc[...] = lax.fori_loop(0, tiles, narrow_step, jnp.zeros((half, D), F32))

        def last_step(i, carry):
            at = rows_at(m * half + i * 64, 64)
            xhat, scale = norm_parts(r.joined[at, :] + (r.acc[rows_at(i * 64, 64), :] + bias3))
            r.layer_out[at, :] = xhat * gain3 + shift3
            dy = r.out_grad[at, :].astype(F32)
            r.dthree[at, :] = norm_back(dy, xhat, scale, gain3)
            return (
                carry[0] + jnp.sum(dy * xhat, axis=0, keepdims=True),
                carry[1] + jnp.sum(dy, axis=0, keepdims=True),
            )

        dgain, dshift = lax.fori_loop(0, half // 64, last_step, (dgain, dshift))
    r.dvec3[...] = jnp.zeros_like(r.dvec3)
    r.dvec3[0:1, :] = dgain
    r.dvec3[1:2, :] = dshift
    r.save(K.dthree, K.layer_out, K.dvec3)


def spread(size, width, taken, offset):
    row = lax.broadcasted_iota(jnp.int32, (size, width), 0)
    lane = lax.broadcasted_iota(jnp.int32, (size, width), 1)
    return jnp.logical_and(lane == row + offset, row < taken).astype(F32).astype(LOW)


def build_vectors(rows, vec, vec_feat, vec_ff):
    feat, ff = vec_feat.shape[1], vec_ff.shape[1]
    one, two, three = D // 8, feat // 8, ff // 8
    total = jnp.zeros(vec.shape, F32)
    total_feat = jnp.zeros((16, feat), F32)
    for d in range(8):
        part = rows[0, d // 2, d % 2, 0:16, :]
        total = total + mm(part[:, :128], spread(128, D, one, one * d))
        total_feat = total_feat + mm(part[:, :256], spread(256, feat, two, two * d))
        vec_ff[0:1, d * three : (d + 1) * three] = part[15:16, :three].astype(F32)
    vec[...] = total
    vec_feat[0:2, :] = total_feat[VEC_ROWS : VEC_ROWS + 2]


def column_sum(v):
    return jnp.sum(v.astype(F32), axis=0, keepdims=True)


def weight_into(target, a, b, at=0, block=256):
    width = a.shape[1]
    for start in range(0, width, block):
        size = min(block, width - start)
        target[pl.ds(at + start, size), :] = mm(a[:, start : start + size], b[...], TN).astype(LOW)


def backward_ffn(r):
    tokens = r.dthree.shape[0]
    half = tokens // 2
    tile = 768
    tiles = r.w_contract.shape[0] // tile
    r.wait(K.dthree, WEIGHT_LOAD + 5)
    r.dn[...] = r.dthree[...].astype(LOW)
    r.dvec[B_CONTRACT : B_CONTRACT + 1, :] = column_sum(r.dn[...])

    def contract_step(n, carry):
        slot = r.ffn_tile(n)
        total = jnp.zeros((1, tile), F32)
        at = rows_at(n * tile, tile)
        for m in range(2):
            part = pl.ds(m * half, half)
            up = mm(r.dn[part, :], r.w_contract[at, :], NT)
            wide = (up * r.slope[slot, part, :].astype(F32)).astype(LOW)
            r.dwide[n, part, :] = wide
            total = total + column_sum(wide)
        r.dvec_ff[0:1, lanes_at(n, tile)] = total
        for j in range(3):
            lanes = slice(j * 256, (j + 1) * 256)
            to = rows_at(n * tile + j * 256, 256)
            r.w_contract[to, :] = mm(r.active[slot, :, lanes], r.dn[...], TN).astype(LOW)
        return carry

    lax.fori_loop(0, tiles, contract_step, 0)
    r.begin(3, 5)
    r.wait(K.joined_low, WEIGHT_LOAD + 4)

    def expand_step(n, carry):
        at = rows_at(n * tile, tile)
        for m in range(2):
            part = pl.ds(m * half, half)
            r.dthree[part, :] += mm(r.dwide[n, part, :], r.w_expand[at, :])
        for j in range(3):
            lanes = slice(j * 256, (j + 1) * 256)
            to = rows_at(n * tile + j * 256, 256)
            r.w_expand[to, :] = mm(r.dwide[n, :, lanes], r.joined_low[...], TN).astype(LOW)
        return carry

    for first in range(tiles):
        lax.fori_loop(first, first + 1, expand_step, 0)
        r.step()
    r.begin(3, 4)


def backward_cross(r):
    tokens = r.dthree.shape[0]
    rows = tokens // 2
    keys = r.ck.shape[0]
    r.wait(K.xhat2, K.r2, K.cmixed, WEIGHT_LOAD + 3)
    gain = r.vec[GAIN_2 : GAIN_2 + 1, :]
    dgain, dshift = jnp.zeros((1, D), F32), jnp.zeros((1, D), F32)
    for c in range(tokens // SEQ):
        own, at = pl.ds(c * NQ, NQ), pl.ds(c * SEQ, NQ)
        dy, xhat = r.dthree[at, :], r.xhat2[own, :]
        dgain = dgain + column_sum(dy * xhat)
        dshift = dshift + column_sum(dy)
        dtwo = norm_back(dy, xhat, r.r2[own, 0:1], gain)
        r.dthree[at, :] = dtwo
        r.dcb[own, :] = dtwo.astype(LOW)
    r.dvec[GAIN_2 : GAIN_2 + 1, :] = dgain
    r.dvec[SHIFT_2 : SHIFT_2 + 1, :] = dshift
    r.dvec[B_COUT : B_COUT + 1, :] = column_sum(r.dcb[...])
    r.dcm[...] = mm(r.dcb[...], r.w_cross(1)[...], NT).astype(LOW)
    weight_into(r.w_cross(1), r.cmixed[...], r.dcb)
    r.step()
    r.wait(K.ck, K.cv, K.cq)

    def step(i, carry):
        lanes = lanes_at(i)
        slot = r.cross_tile(i)
        low = r.p_cross[slot]
        p = low.astype(F32)
        up = pair_lanes(r.dcm[:, lanes])
        dp = mm(r.cv[:, lanes], up, NT)
        ds = (p * (dp - jnp.sum(p * dp, axis=0, keepdims=True))).astype(LOW)
        r.cv[:, lanes] = mm(low, up).astype(LOW)
        dq = unpair(mm(r.ck[:, lanes], ds, TN)) * SCALE
        r.ck[:, lanes] = (mm(ds, pair_lanes(r.cq[:, lanes])) * SCALE).astype(LOW)
        r.dcq[:, lanes] = dq.astype(LOW)
        return carry

    for first in range(0, D // 128, 2):
        lax.fori_loop(first, first + 2, step, 0)
        r.step()
    r.dvec[B_CVALUE : B_CVALUE + 1, :] = column_sum(r.cv[...])
    r.dvec[B_CQUERY : B_CQUERY + 1, :] = column_sum(r.dcq[...])
    r.wait(WEIGHT_LOAD + 2, K.vision, K.xhat_v, K.cross_in)
    feat = r.vision.shape[1]
    zero = jnp.zeros((1, feat), F32)

    def vision_step(i, carry):
        at = rows_at(i * KEYS, KEYS)
        up = mm(r.ck[at, :], r.w_ckey[...], NT) + mm(r.cv[at, :], r.w_cvalue[...], NT)
        return (
            carry[0] + column_sum(up * r.xhat_v[at, :].astype(F32)),
            carry[1] + column_sum(up),
        )

    carry = (zero, zero)
    for image in range(keys // KEYS):
        carry = vision_step(image, carry)
        if image == 1:
            r.step()
    dgain, dshift = carry
    r.dvec_feat[VEC_ROWS : VEC_ROWS + 1, :] = dgain
    r.dvec_feat[VEC_ROWS + 1 : VEC_ROWS + 2, :] = dshift
    r.step()
    for start, size in ((0, 512), (512, 512), (1024, 384)):
        columns = r.vision[:, start : start + size]
        r.w_ckey[pl.ds(start, size), :] = mm(columns, r.ck[...], TN).astype(LOW)
        r.w_cvalue[pl.ds(start, size), :] = mm(columns, r.cv[...], TN).astype(LOW)
        r.step()
    r.begin(2, 2)
    back = mm(r.dcq[...], r.w_cross(0)[...], NT)
    for c in range(tokens // SEQ):
        at = pl.ds(c * SEQ, NQ)
        r.dthree[at, :] += back[c * NQ : (c + 1) * NQ, :]
    weight_into(r.w_cross(0), r.cross_in[...], r.dcq)
    r.begin(2, 3)
    r.step()


def backward_self(r):
    tokens = r.dthree.shape[0]
    half = tokens // 2
    r.wait(K.xhat1, K.r1, K.mixed, WEIGHT_LOAD + 1)
    gain = r.vec[GAIN_1 : GAIN_1 + 1, :]
    zero = jnp.zeros((1, D), F32)

    def norm_step(i, carry):
        at = rows_at(i * 128, 128)
        dy, xhat = r.dthree[at, :], r.xhat1[at, :]
        done = norm_back(dy, xhat, r.r1[at, 0:1], gain)
        r.dthree[at, :] = done
        low = done.astype(LOW)
        r.dn[at, :] = low
        return (
            carry[0] + column_sum(dy * xhat),
            carry[1] + column_sum(dy),
            carry[2] + column_sum(low),
        )

    dgain, dshift, dbias = lax.fori_loop(0, tokens // 128, norm_step, (zero, zero, zero))
    r.dvec[GAIN_1 : GAIN_1 + 1, :] = dgain
    r.dvec[SHIFT_1 : SHIFT_1 + 1, :] = dshift
    r.dvec[B_OUT : B_OUT + 1, :] = dbias
    for m in range(2):
        part = pl.ds(m * half, half)
        r.dm[part, :] = mm(r.dn[part, :], r.w_self(3)[...], NT).astype(LOW)
    weight_into(r.w_self(3), r.mixed[...], r.dn)
    r.begin(1)
    r.step()
    r.wait(K.q, K.k, K.v, K.p_self)

    def step(i, carry):
        lanes = lanes_at(i)
        for g in range(tokens // 128):
            at = pl.ds(g * 128, 128)
            low = r.p_self[i, g]
            p = low.astype(F32)
            up = pair_lanes(r.dm[at, lanes])
            dp = mm(r.v[at, lanes], up, NT)
            ds = (p * (dp - jnp.sum(p * dp, axis=0, keepdims=True))).astype(LOW)
            dq = unpair(mm(r.k[at, lanes], ds, TN)) * SCALE
            dk = mm(ds, pair_lanes(r.q[at, lanes])) * SCALE
            r.v[at, lanes] = mm(low, up).astype(LOW)
            r.q[at, lanes] = dq.astype(LOW)
            r.k[at, lanes] = dk.astype(LOW)
        return carry

    for first in range(0, D // 128, 2):
        lax.fori_loop(first, first + 2, step, 0)
        r.step()
    r.dvec[B_QUERY : B_QUERY + 1, :] = column_sum(r.q[...])
    r.dvec[B_VALUE : B_VALUE + 1, :] = column_sum(r.v[...])
    r.wait(X_LOAD)
    for j, ref in enumerate((r.q, r.k, r.v)):
        for m in range(2):
            part = pl.ds(m * half, half)
            r.dthree[part, :] += mm(ref[part, :], r.w_self(j)[...], NT)
        weight_into(r.w_self(j), r.x[...], ref)
        if j == 1:
            r.begin(1)
        r.step()
    r.begin(1, 1)


SUM_PARTS = (
    (corner(5, 0), 0),
    (halved(5, 192), 2),
    (halved(5, 288), 3),
    (corner(4, 0), 1),
    (halved(4, 192), 4),
    (halved(4, 288), 5),
    (Piece(2, True, 48, lambda y, c: y, lambda y, c: 48 * c), 0),
    (Piece(2, False, 80, lambda y, c: c, lambda y, c: 96), 6),
    (Piece(3, True, 32, lambda y, c: y, lambda y, c: 32 * c), 7),
    (Piece(3, False, 32, lambda y, c: c, lambda y, c: 64), 8),
    (Piece(1, False, 48, lambda y, c: 3, lambda y, c: 48 * c), 2),
    (Piece(1, True, 48, lambda y, c: y, lambda y, c: 48 * c), 1),
    (Piece(1, False, 48, lambda y, c: 2, lambda y, c: 48 * c), 3),
    (Piece(0, False, 16, lambda y, c: 0, lambda y, c: 16 * c), 9),
)
SUM_PIECES = tuple(p for p, _ in SUM_PARTS)
LANDING = tuple(b for _, b in SUM_PARTS)
BUFFERS = max(LANDING) + 1
SUM_LAGS = (0, 2, 4, 6, 8, 9)


def next_user(k):
    for later in range(k + 1, len(LANDING)):
        if LANDING[later] == LANDING[k]:
            return later
    return None


def reuses(k):
    return LANDING[k] in LANDING[:k]


class Reduce:
    def __init__(self, grads, outs, refs):
        total = len(SUM_PIECES)
        self.grads, self.outs = grads, outs
        self.from_c, self.from_y, self.from_x, self.from_z = (
            refs[i * BUFFERS : (i + 1) * BUFFERS] for i in range(4)
        )
        refs = refs[4 * BUFFERS :]
        self.last, refs = refs[:total], refs[total:]
        self.done, self.credit, self.cs, self.ys, self.xs, self.zs, self.fs = refs[:7]
        self.cs_s, self.ys_s, self.xs_s, self.zs_s, self.fs_s = refs[7:]
        y, c, z, x = self.me = place()
        self.zp = [lax.rem(z + i, 4) for i in (1, 2, 3)]
        self.to_z = [at_device(y, c, p, x) for p in self.zp]
        self.back_z = [at_device(y, c, lax.rem(z + 4 - i, 4), x) for i in (1, 2, 3)]
        self.to_x, self.to_y = at_device(y, c, z, 1 - x), at_device(1 - y, c, z, x)
        self.to_c, self.to_d = at_device(y, 1 - c, z, x), at_device(1 - y, 1 - c, z, x)
        self.sent, self.stored, self.slot_at, self.begun = [], [], 0, 0
        self.z_sends = {}
        greet(self.to_z + [self.to_x, self.to_y, self.to_c, self.to_d])

    def go(self, *spec):
        copy = remote(*spec)
        copy.start()
        self.sent.append(copy)
        return copy

    def arrived(self, dst, recv, send):
        remote(dst, dst, send, recv, self.to_x).wait_recv()

    def sides(self, k):
        y = self.me[0]
        return (y, 1 - y) if SUM_PIECES[k].four else (y,)

    def owe(self, k, i, device):
        later = next_user(k)
        if later is not None:
            pl.semaphore_signal(
                self.credit.at[later, i], inc=1, device_id=device, device_id_type=MESH
            )

    def ask(self, k, i):
        if reuses(k):
            pl.semaphore_wait(self.credit.at[k, i], 1)

    def begin(self, count):
        c = self.me[1]
        for k in range(self.begun, self.begun + count):
            p = SUM_PIECES[k]
            self.ask(k, 0)
            for j, yy in enumerate(self.sides(k)):
                land = self.from_c[LANDING[k]].at[j]
                self.go(p.every(self.grads, yy, 1 - c), land, self.cs_s.at[k, j], self.cs.at[k, j], self.to_c)
        self.begun += count

    def stage_c(self, k):
        y, c, z, x = self.me
        p, buf = SUM_PIECES[k], self.from_c[LANDING[k]]
        sides = self.sides(k)
        for j in reversed(range(len(sides))):
            self.arrived(buf.at[j], self.cs.at[k, j], self.cs_s.at[k, j])
            for i in range(4):
                for l in range(2):
                    mine = p.at(self.grads, sides[j], c, i, l)
                    mine[...] = mine[...] + buf[j, i, l]
            if j == 1:
                self.ask(k, 1)
                mine = p.every(self.grads, sides[1], c)
                self.go(mine, self.from_y[LANDING[k]], self.ys_s.at[k], self.ys.at[k], self.to_y)
        self.owe(k, 0, self.to_c)

    def stage_y(self, k):
        y, c, z, x = self.me
        p = SUM_PIECES[k]
        if p.four:
            buf = self.from_y[LANDING[k]]
            self.arrived(buf, self.ys.at[k], self.ys_s.at[k])
            for i in range(4):
                for l in range(2):
                    mine = p.at(self.grads, y, c, i, l)
                    mine[...] = mine[...] + buf[i, l]
            self.owe(k, 1, self.to_y)
        self.ask(k, 2)
        far = p.column(self.grads, y, c, 1 - x)
        self.go(far, self.from_x[LANDING[k]], self.xs_s.at[k], self.xs.at[k], self.to_x)

    def stage_x(self, k):
        y, c, z, x = self.me
        p, buf = SUM_PIECES[k], self.from_x[LANDING[k]]
        self.arrived(buf, self.xs.at[k], self.xs_s.at[k])
        for i in range(4):
            buf[i] = buf[i] + p.at(self.grads, y, c, i, x)[...]
        land = self.from_z[LANDING[k]]
        self.z_sends[k] = []
        for i in range(3):
            self.ask(k, 3 + i)
            copy = remote(buf.at[self.zp[i]], land.at[i], self.zs_s.at[k, i], self.zs.at[k, i], self.to_z[i])
            copy.start()
            self.z_sends[k].append(copy)

    def stage_z(self, k):
        y, c, z, x = self.me
        p, buf, land, last = SUM_PIECES[k], self.from_x[LANDING[k]], self.from_z[LANDING[k]], self.last[k]
        for i in range(3):
            self.arrived(land.at[i], self.zs.at[k, i], self.zs_s.at[k, i])
        value = buf[z].astype(F32)
        for i in range(3):
            value = value + land[i].astype(F32)
        last[0] = value.astype(LOW)
        if p.four:
            out = p.shard(self.outs, y, c)
            for j, device in enumerate((self.to_y, self.to_c, self.to_d)):
                self.go(last.at[0], out, self.fs_s.at[k, j], self.fs.at[k, j], device)
            self.put(k, 0)
        else:
            self.go(last.at[0], last.at[1], self.fs_s.at[k, 0], self.fs.at[k, 0], self.to_y)
        for copy in self.z_sends[k]:
            copy.wait_send()
        self.owe(k, 2, self.to_x)
        for i in range(3):
            self.owe(k, 3 + i, self.back_z[i])

    def put(self, k, slot):
        y, c, z, x = self.me
        out = SUM_PIECES[k].shard(self.outs, y, c)
        copy = pltpu.make_async_copy(self.last[k].at[slot], out, self.done.at[k])
        copy.start()
        self.stored.append(copy)

    def stage_f(self, k):
        y, c, z, x = self.me
        p, last = SUM_PIECES[k], self.last[k]
        if not p.four:
            self.arrived(last.at[1], self.fs.at[k, 0], self.fs_s.at[k, 0])
            last[2] = last[0] + last[1]
            out = p.shard(self.outs, y, c)
            self.go(last.at[2], out, self.fs_s.at[k, 1], self.fs.at[k, 1], self.to_c)
            self.put(k, 2)

    def stage_g(self, k):
        y, c, z, x = self.me
        p = SUM_PIECES[k]
        if p.four:
            places = ((1 - y, c), (y, 1 - c), (1 - y, 1 - c))
            for j, (yy, cc) in enumerate(places):
                self.arrived(p.shard(self.outs, yy, cc), self.fs.at[k, j], self.fs_s.at[k, j])
        else:
            self.arrived(p.shard(self.outs, y, 1 - c), self.fs.at[k, 1], self.fs_s.at[k, 1])

    def advance(self, slots):
        total = len(SUM_PIECES)
        stages = (self.stage_c, self.stage_y, self.stage_x, self.stage_z, self.stage_f, self.stage_g)
        while self.slot_at < slots:
            if self.slot_at >= self.begun < total:
                return
            for lag, stage in zip(SUM_LAGS, stages):
                if 0 <= self.slot_at - lag < total:
                    stage(self.slot_at - lag)
            self.slot_at += 1

    def step(self):
        self.advance(self.slot_at + 1)

    def end(self):
        self.advance(len(SUM_PIECES) + SUM_LAGS[-1])
        for copy in self.sent:
            copy.wait_send()
        for copy in self.stored:
            copy.wait()


def reduce_scratch():
    total, dma = len(SUM_PIECES), pltpu.SemaphoreType.DMA
    first = [SUM_PIECES[LANDING.index(b)] for b in range(BUFFERS)]
    pairs = [dma((total, 2)), dma((total,)), dma((total,)), dma((total, 3)), dma((total, 3))]
    return (
        [pltpu.VMEM((2 if p.four else 1, 4, 2, p.size, D), LOW) for p in first]
        + [pltpu.VMEM((4, 2, p.size, D) if p.four else (1, 1, 16, 128), LOW) for p in first]
        + [pltpu.VMEM((4, p.size, D), LOW) for p in first]
        + [pltpu.VMEM((3, p.size, D), LOW) for p in first]
        + [pltpu.VMEM((1 if p.four else 3, p.size, D), LOW) for p in SUM_PIECES]
        + [dma((total,)), pltpu.SemaphoreType.REGULAR((total, 6))]
        + pairs
        + pairs
    )


def pack_vectors(rows, dvec, dvec_feat, dvec_ff):
    feat, ff = dvec_feat.shape[1], dvec_ff.shape[1]
    one, two, three = D // 8, feat // 8, ff // 8
    low, low_feat = dvec[...].astype(LOW), dvec_feat[...].astype(LOW)
    row = lax.broadcasted_iota(jnp.int32, (16, three), 0)
    for d in range(8):
        small = mm(low, spread(128, D, one, one * d), NT)
        wide = mm(low_feat, spread(256, feat, two, two * d), NT)
        block = jnp.concatenate([small + wide[:, :128], wide[:, 128:], jnp.zeros((16, three - 256), F32)], axis=1)
        block = jnp.where(row == 15, dvec_ff[0:1, d * three : (d + 1) * three], block)
        rows[0, d // 2, d % 2, 0:16, :three] = block.astype(LOW)
        rows[0, d // 2, d % 2, 0:16, three:] = jnp.zeros((16, D - three), LOW)
        rows[0, d // 2, d % 2, 16:32, :] = jnp.zeros((16, D), LOW)


class Refs:
    def __init__(self, **names):
        self.__dict__.update(names)


class Saved(typing.NamedTuple):
    vision: typing.Any
    xhat_v: typing.Any
    q: typing.Any
    k: typing.Any
    v: typing.Any
    p_self: typing.Any
    mixed: typing.Any
    xhat1: typing.Any
    r1: typing.Any
    cross_in: typing.Any
    ck: typing.Any
    cv: typing.Any
    cq: typing.Any
    cmixed: typing.Any
    xhat2: typing.Any
    r2: typing.Any
    joined_low: typing.Any
    dthree: typing.Any
    layer_out: typing.Any
    dvec3: typing.Any
    vec: typing.Any
    active: typing.Any
    slope: typing.Any
    p_cross: typing.Any


K = Saved(*range(len(Saved._fields)))
HELD = K.vec + 1
X_LOAD, WEIGHT_LOAD = 100, 200
RAW = 11
VMEM_BYTES = 63 * 1024 * 1024


def saved_shapes(tokens, images, feat, ff):
    rows, keys = tokens // 2, images * KEYS
    return Saved(
        vision=((keys, feat), LOW),
        xhat_v=((keys, feat), LOW),
        q=((tokens, D), LOW),
        k=((tokens, D), LOW),
        v=((tokens, D), LOW),
        p_self=((D // 128, tokens // 128, 128, 256), LOW),
        mixed=((tokens, D), LOW),
        xhat1=((tokens, D), F32),
        r1=((tokens, 128), F32),
        cross_in=((rows, D), LOW),
        ck=((keys, D), LOW),
        cv=((keys, D), LOW),
        cq=((rows, D), LOW),
        cmixed=((rows, D), LOW),
        xhat2=((rows, D), F32),
        r2=((rows, 128), F32),
        joined_low=((tokens, D), LOW),
        dthree=((tokens, D), F32),
        layer_out=((tokens, D), F32),
        dvec3=((8, D), F32),
        vec=((16, D), F32),
        active=((ff // 768, tokens, 768), LOW),
        slope=((ff // 768, tokens, 768), LOW),
        p_cross=((D // 128, keys, 2 * rows), LOW),
    )


def full_views(full):
    def flat(ref, j):
        return ref.at[j].reshape(8 * ref.shape[3], D)

    return dict(
        w_self=lambda j: flat(full[1], j),
        w_ckey=flat(full[2], 0),
        w_cvalue=flat(full[2], 1),
        w_cross=lambda j: flat(full[3], j),
        w_expand=flat(full[4], 0),
        w_contract=flat(full[5], 0),
    )


def forward_kernel(fast, *refs):
    count = len(ARRAY_ROWS)
    (counts, lengths, x, feats, out_grad), refs = refs[:5], refs[5:]
    inputs = RAW if fast else count
    own, refs = refs[:inputs], refs[inputs:]
    if not fast:
        vec_in, refs = refs[:3], refs[3:]
    outs, refs = Saved(*refs[: len(K)]), refs[len(K) :]
    weights, refs = refs[: count - 1], refs[count - 1 :]
    held, refs = refs[:HELD], refs[HELD:]
    full, refs = refs[:count], refs[count:]
    vec_feat, vec_ff, joined, acc, shown, active, slope, pbuf = refs[:8]
    save_sem, weight_sem, active_sem, slope_sem, p_sem = refs[8:13]
    kept = dict(zip(Saved._fields, held))
    vec = kept[Saved._fields[K.vec]]
    pairs, tiles = outs.p_cross.shape[0], outs.slope.shape[0]
    copies = []

    def begin(copy):
        copy.start()
        copies.append(copy)

    def save(*names):
        for i in names:
            begin(pltpu.make_async_copy(held[i], outs[i], save_sem.at[i]))

    def save_weights(i):
        begin(pltpu.make_async_copy(full[i], weights[i - 1], weight_sem.at[i]))

    def p_copy(i):
        return pltpu.make_async_copy(pbuf.at[i % 2], outs.p_cross.at[i], p_sem.at[i % 2])

    def slope_copy(n):
        return pltpu.make_async_copy(slope.at[n % 2], outs.slope.at[n], slope_sem.at[n % 2])

    def active_copy(n):
        return pltpu.make_async_copy(active.at[n], outs.active.at[n], active_sem.at[n])

    def keep_cross(i, p):
        @pl.when(i >= 2)
        def _():
            p_copy(i - 2).wait()

        pbuf[i % 2] = p
        p_copy(i).start()

    def before_slope(n):
        @pl.when(n >= 2)
        def _():
            slope_copy(n - 2).wait()

    def after_slope(n):
        slope_copy(n).start()
        active_copy(n).start()

    if fast:
        staged, wide, stage_sem, sems = refs[13:17], refs[17], refs[18], refs[19:]
        gather = Gather(full, sems)
        gather.start(own, staged, wide, stage_sem)
        gather.vectors()
        build_vectors(full[0], vec, vec_feat, vec_ff)
        need = gather.need

        def step():
            gather.advance(gather.slot_at + 1)
    else:
        loads = [pltpu.make_async_copy(own[i], full[i], weight_sem.at[i]) for i in range(count)]
        loads += [
            pltpu.make_async_copy(src, dst, p_sem.at[0])
            for src, dst in zip(vec_in, (vec, vec_feat, vec_ff))
        ]
        for copy in loads:
            copy.start()
            copy.wait()

        def need(k):
            pass

        def step():
            pass

    save(K.vec)
    r = Refs(
        counts=counts,
        lengths=lengths,
        x=x,
        feats=feats,
        out_grad=out_grad,
        **kept,
        **full_views(full),
        vec_feat=vec_feat,
        vec_ff=vec_ff,
        joined=joined,
        acc=acc,
        shown=shown,
        active=active,
        slope=slope,
        save=save,
        save_weights=save_weights,
        need=need,
        step=step,
        keep_cross=keep_cross,
        before_slope=before_slope,
        after_slope=after_slope,
    )
    forward_steps(r)
    for i in (pairs - 2, pairs - 1):
        p_copy(i).wait()
    for n in (tiles - 2, tiles - 1):
        slope_copy(n).wait()
    for n in range(tiles):
        active_copy(n).wait()
    for copy in copies:
        copy.wait()
    if fast:
        gather.end()


def stage_scratch(ff):
    shapes = [(k, rows, D) for k, rows in ARRAY_ROWS[1:5]]
    return [pltpu.VMEM(s, LOW) for s in shapes + [(D, ff // 8)]] + [pltpu.SemaphoreType.DMA((9,))]


def forward_all(fast, counts, lengths, x, feats, out_grad, own, vectors):
    tokens, images, feat = x.shape[0], feats.shape[0], feats.shape[2]
    count = len(ARRAY_ROWS)
    if fast:
        full = [(k, 4, 2, rows, D) for k, rows in ARRAY_ROWS]
    else:
        full = [w.shape for w in own]
    ff = 8 * full[4][3]
    rows, keys = tokens // 2, images * KEYS
    shapes = saved_shapes(tokens, images, feat, ff)
    vmem, smem = pl.BlockSpec(memory_space=pltpu.VMEM), pl.BlockSpec(memory_space=pltpu.SMEM)
    hbm = pl.BlockSpec(memory_space=pl.ANY)
    ins = [counts, lengths, x, feats, out_grad, *own]
    if not fast:
        ins += list(vectors)
    out_shape = [jax.ShapeDtypeStruct(*shape) for shape in shapes]
    out_shape += [jax.ShapeDtypeStruct(shape, LOW) for shape in full[1:]]
    dma = pltpu.SemaphoreType.DMA
    outs = pl.pallas_call(
        functools.partial(forward_kernel, fast),
        name="forward",
        out_shape=out_shape,
        in_specs=[smem, smem] + [vmem] * 3 + [hbm] * (len(ins) - 5),
        out_specs=[hbm] * len(out_shape),
        scratch_shapes=[pltpu.VMEM(*shape) for shape in shapes[:HELD]]
        + [pltpu.VMEM(shape, LOW) for shape in full]
        + [
            pltpu.VMEM((8, feat), F32),
            pltpu.VMEM((8, ff), F32),
            pltpu.VMEM((tokens, D), F32),
            pltpu.VMEM((tokens // 2, D), F32),
            pltpu.VMEM((keys, 2 * rows), F32),
            pltpu.VMEM((ff // 768, tokens, 768), LOW),
            pltpu.VMEM((2, tokens, 768), LOW),
            pltpu.VMEM((2, keys, 2 * rows), LOW),
            dma((HELD,)),
            dma((count,)),
            dma((ff // 768,)),
            dma((2,)),
            dma((2,)),
        ]
        + (stage_scratch(ff) + gather_semaphores() if fast else []),
        compiler_params=pltpu.CompilerParams(
            vmem_limit_bytes=VMEM_BYTES,
            **(dict(collective_id=0, has_side_effects=True) if fast else {}),
        ),
    )(*ins)
    return Saved(*outs[: len(K)]), list(outs[len(K) :])


LOADS = (K.dthree, K.joined_low, K.xhat2, K.r2, K.cmixed, K.ck, K.cv, K.cq, K.vision, K.xhat_v, K.cross_in)
LOADS += (K.xhat1, K.r1, K.p_self, K.vec, K.dvec3)
LATE = (K.mixed, K.q, K.k, K.v)


def backward_kernel(fast, *refs):
    count = len(ARRAY_ROWS)
    x_in, refs = refs[0], refs[1:]
    ins, refs = Saved(*refs[: len(K)]), refs[len(K) :]
    weights, refs = (None,) + tuple(refs[: count - 1]), refs[count - 1 :]
    input_grad, refs = refs[0], refs[1:]
    if fast:
        outs, refs = refs[:count], refs[count:]
    else:
        vec_outs, outs, refs = refs[:3], (None,) + tuple(refs[3 : count + 2]), refs[count + 2 :]
    held, refs = dict(zip(LOADS, refs)), refs[len(LOADS) :]
    full, refs = refs[:count], refs[count:]
    dvec, dvec_feat, dvec_ff, dn, dwide, abuf, sbuf, pbuf = refs[:8]
    load_sem, w_sem, g_sem, abuf_sem, sbuf_sem, pbuf_sem = refs[8:14]
    x, dm = abuf.at[0], abuf.at[1]
    half = dn.shape[0] // 2
    dcb, dcm, dcq = sbuf.at[0, pl.ds(0, half)], sbuf.at[0, pl.ds(half, half)], sbuf.at[1, pl.ds(0, half)]
    for i, name in enumerate(LATE):
        held[name] = dwide.at[i]
    loads = {i: pltpu.make_async_copy(ins[i], held[i], load_sem.at[i]) for i in LOADS + LATE}
    loads[X_LOAD] = pltpu.make_async_copy(x_in, x, load_sem.at[K.layer_out])
    for i in range(1, count):
        loads[WEIGHT_LOAD + i] = pltpu.make_async_copy(weights[i], full[i], w_sem.at[i])

    def tile_copies(n, slot):
        return (
            pltpu.make_async_copy(ins.active.at[n], abuf.at[slot], abuf_sem.at[slot]),
            pltpu.make_async_copy(ins.slope.at[n], sbuf.at[slot], sbuf_sem.at[slot]),
        )

    def pair_copy(i, slot):
        return pltpu.make_async_copy(ins.p_cross.at[i], pbuf.at[slot], pbuf_sem.at[slot])

    for i in (K.dthree, WEIGHT_LOAD + 5):
        loads[i].start()
    for copy in tile_copies(0, 0):
        copy.start()
    for i in (K.joined_low, WEIGHT_LOAD + 4) + LOADS[2:5] + (WEIGHT_LOAD + 3,) + LOADS[5:8]:
        loads[i].start()
    pair_copy(0, 0).start()
    for i in (WEIGHT_LOAD + 2,) + LOADS[8:] + (WEIGHT_LOAD + 1,):
        loads[i].start()

    def wait(*names):
        for i in names:
            loads[i].wait()

    def ffn_tile(n):
        @pl.when(n + 1 < ins.active.shape[0])
        def _():
            for copy in tile_copies(n + 1, (n + 1) % 2):
                copy.start()

        for copy in tile_copies(n, n % 2):
            copy.wait()
        return n % 2

    def cross_tile(i):
        @pl.when(i + 1 < ins.p_cross.shape[0])
        def _():
            pair_copy(i + 1, (i + 1) % 2).start()

        pair_copy(i, i % 2).wait()
        return i % 2

    stored = []

    def keep(src, dst, sem):
        copy = pltpu.make_async_copy(src, dst, sem)
        copy.start()
        stored.append(copy)

    if fast:
        reduce = Reduce(full, outs, refs[14:])
        step = reduce.step

        def begin(parts, *arrays):
            reduce.begin(parts)
    else:

        def step():
            pass

        def begin(parts, *arrays):
            for i in arrays:
                keep(full[i], outs[i], g_sem.at[i])

    r = Refs(
        **{Saved._fields[i]: ref for i, ref in held.items()},
        **full_views(full),
        x=x,
        dvec=dvec,
        dvec_feat=dvec_feat,
        dvec_ff=dvec_ff,
        dn=dn,
        dwide=dwide,
        dm=dm,
        dcb=dcb,
        dcm=dcm,
        dcq=dcq,
        active=abuf,
        slope=sbuf,
        p_cross=pbuf,
        wait=wait,
        begin=begin,
        step=step,
        ffn_tile=ffn_tile,
        cross_tile=cross_tile,
    )
    dvec[...] = jnp.zeros_like(dvec)
    dvec_feat[...] = jnp.zeros_like(dvec_feat)
    wait(K.vec, K.dvec3)
    dvec[GAIN_3 : GAIN_3 + 2, :] = held[K.dvec3][0:2, :]
    backward_ffn(r)
    for i in LATE + (X_LOAD,):
        loads[i].start()
    backward_cross(r)
    backward_self(r)
    keep(held[K.dthree], input_grad, g_sem.at[0])
    if fast:
        pack_vectors(full[0], dvec, dvec_feat, dvec_ff)
        reduce.begin(1)
        reduce.end()
    else:
        for src, dst, i in zip((dvec, dvec_feat, dvec_ff), vec_outs, LATE):
            keep(src, dst, load_sem.at[i])
    for copy in stored:
        copy.wait()


def backward_all(fast, saved, weights, x):
    tokens, keys, feat = x.shape[0], saved.vision.shape[0], saved.vision.shape[1]
    count = len(ARRAY_ROWS)
    rows, ff = tokens // 2, 8 * weights[3].shape[3]
    hbm = pl.BlockSpec(memory_space=pl.ANY)
    dma = pltpu.SemaphoreType.DMA
    small = [(16, D), (16, feat), (8, ff)]
    out_shape = [jax.ShapeDtypeStruct((tokens, D), F32)]
    if fast:
        out_shape += [jax.ShapeDtypeStruct((k, n, D), LOW) for k, n in ARRAY_ROWS]
    else:
        out_shape += [jax.ShapeDtypeStruct(s, F32) for s in small]
        out_shape += [jax.ShapeDtypeStruct(w.shape, LOW) for w in weights]
    outs = pl.pallas_call(
        functools.partial(backward_kernel, fast),
        name="backward",
        out_shape=out_shape,
        in_specs=[hbm] * (len(K) + count),
        out_specs=[hbm] * len(out_shape),
        scratch_shapes=[pltpu.VMEM(saved[i].shape, saved[i].dtype) for i in LOADS]
        + [pltpu.VMEM((1, 4, 2, 32, D), LOW)]
        + [pltpu.VMEM(w.shape, LOW) for w in weights]
        + [pltpu.VMEM(s, F32) for s in small]
        + [pltpu.VMEM((tokens, D), LOW), pltpu.VMEM((ff // 768, tokens, 768), LOW)]
        + [
            pltpu.VMEM((2, tokens, 768), LOW),
            pltpu.VMEM((2, tokens, 768), LOW),
            pltpu.VMEM((2, keys, 2 * rows), LOW),
            dma((len(K),)),
            dma((count,)),
            dma((count,)),
            dma((2,)),
            dma((2,)),
            dma((2,)),
        ]
        + (reduce_scratch() if fast else []),
        compiler_params=pltpu.CompilerParams(
            vmem_limit_bytes=VMEM_BYTES,
            **(dict(collective_id=1, has_side_effects=True) if fast else {}),
        ),
    )(x, *saved, *weights)
    return outs[0], list(outs[1:])


def pack_rows(vectors):
    total = jnp.zeros((32, D), vectors[0].dtype)
    for first, last in ((0, VEC_ROWS), (VEC_ROWS, VEC_ROWS + 2), (VEC_ROWS + 2, VEC_ROWS + 3)):
        rows = jnp.stack(vectors[first:last])
        total = total + jnp.pad(rows, ((first, 32 - last), (0, D - rows.shape[1])))
    return total[None]


def local(
    fast,
    hidden,
    image_feats,
    caption_counts,
    text_lengths,
    out_grad,
    self_query,
    query_bias,
    self_key,
    self_value,
    value_bias,
    self_output,
    output_bias,
    first_gain,
    first_shift,
    cross_query,
    crossquery_bias,
    cross_key,
    cross_value,
    crossvalue_bias,
    cross_output,
    crossoutput_bias,
    second_gain,
    second_shift,
    vision_gain,
    vision_shift,
    expand_weight,
    expand_bias,
    contract_weight,
    contract_bias,
    third_gain,
    third_shift,
):
    low = jnp.bfloat16
    vectors = (
        query_bias,
        value_bias,
        output_bias,
        first_gain,
        first_shift,
        crossquery_bias,
        crossvalue_bias,
        crossoutput_bias,
        second_gain,
        second_shift,
        contract_bias,
        third_gain,
        third_shift,
        vision_gain,
        vision_shift,
        expand_bias,
    )
    own = [pack_rows(vectors), self_query, self_key, self_value, self_output]
    own += [cross_key, cross_value, cross_query, cross_output, expand_weight, contract_weight[None]]
    feat = image_feats.shape[-1]
    shards = D // self_query.shape[0]
    whole = ()
    if not fast:
        own = [own[0], jnp.stack(own[1:5]), jnp.stack(own[5:7]), jnp.stack(own[7:9]), own[9].T[None], own[10]]
        full = [lax.all_gather(s, FSDP, axis=1, tiled=False) for s in own]
        rows = full[0][0]
        each = [rows[:, i, : v.shape[0]].reshape(-1).astype(F32) for i, v in enumerate(vectors)]
        own = [f.reshape(f.shape[0], 4, 2, -1, D) for f in full]
        whole = (
            jnp.stack(each[:VEC_ROWS] + [jnp.zeros((D,), F32)] * (16 - VEC_ROWS)),
            jnp.stack(each[VEC_ROWS : VEC_ROWS + 2] + [jnp.zeros((feat,), F32)] * 6),
            jnp.broadcast_to(each[-1][None], (8, each[-1].shape[0])),
        )
    x = hidden.reshape(-1, D)
    saved, weights = forward_all(
        fast,
        caption_counts,
        text_lengths,
        x,
        image_feats,
        out_grad.reshape(-1, D),
        own,
        whole,
    )
    input_grad, summed = backward_all(fast, saved, weights, x)
    layer_out = saved.layer_out.reshape(hidden.shape)
    input_grad = input_grad.reshape(hidden.shape)
    if not fast:
        dvec, dvec_feat, dvec_ff = summed[:3]
        pieces = [dvec[i] for i in range(VEC_ROWS)]
        pieces += [dvec_feat[VEC_ROWS], dvec_feat[VEC_ROWS + 1], dvec_ff[0]]
        pieces = [v.astype(LOW).reshape(shards, -1) for v in pieces]
        pieces = [jnp.pad(v, ((0, 0), (0, D - v.shape[1]))) for v in pieces]
        packed = jnp.stack(pieces + [jnp.zeros((shards, D), LOW)] * (32 - len(pieces)), axis=1)
        grads = [packed[None]] + [g.reshape(g.shape[0], shards, -1, D) for g in summed[3:]]
        summed = [lax.psum_scatter(g, FSDP, scatter_dimension=1, tiled=False) for g in grads]
        summed = [lax.psum(g, DP) for g in summed]
    sums = [s.astype(F32) for s in summed]
    small = [sums[0][0, i, : v.shape[0]] for i, v in enumerate(vectors)]
    return (
        layer_out,
        input_grad,
        sums[1][0],
        small[0],
        sums[1][1],
        sums[1][2],
        small[1],
        sums[1][3],
        small[2],
        small[3],
        small[4],
        sums[3][0],
        small[5],
        sums[2][0],
        sums[2][1],
        small[6],
        sums[3][1],
        small[7],
        small[8],
        small[9],
        small[13],
        small[14],
        sums[4][0].T,
        small[15],
        sums[5][0],
        small[10],
        small[11],
        small[12],
    )


def solution(mesh):
    fast = mesh.shape[DP] == 4 and mesh.shape[FSDP] == 8
    tokens, pair = P((DP, FSDP), None, None), P((DP, FSDP), None)
    by_row, by_column, flat = P(FSDP, None), P(None, FSDP), P(FSDP)
    params = (
        (by_row, flat, by_row, by_row, flat, by_row, flat, flat, flat)
        + (by_row, flat, by_row, by_row, flat, by_row, flat)
        + (flat,) * 4
        + (by_column, flat, by_row, flat, flat, flat)
    )
    return jax.shard_map(
        functools.partial(local, fast),
        mesh=mesh,
        in_specs=(tokens, tokens, pair, P((DP, FSDP)), tokens) + params,
        out_specs=(tokens, tokens) + params,
        check_vma=False,
    )
```

```python
import functools
import typing

import jax
import jax.numpy as jnp
from jax import lax
from jax.experimental import pallas as pl
from jax.experimental.pallas import tpu as pltpu
from jax.sharding import PartitionSpec as P

D = 768
HEADS = 12
HDIM = 64
PATCH = 257
NQ = 32
SEQ = 64
EPS = 1e-06
MASKED = -1000000000.0


MESH = pl.DeviceIdType.MESH
DP, FSDP = "dp", "fsdp"
SHARD_LANES = 96


def place():
    dp, fs = lax.axis_index(DP), lax.axis_index(FSDP)
    return dp // 2, dp % 2, fs // 2, fs % 2


def at_device(y, c, z, x):
    return (2 * y + c, 2 * z + x)


def rows_at(start, size):
    return pl.ds(pl.multiple_of(start, 16), size)


def greet(peers):
    barrier = pltpu.get_barrier_semaphore()
    for peer in peers:
        pl.semaphore_signal(barrier, inc=1, device_id=peer, device_id_type=MESH)
    pl.semaphore_wait(barrier, len(peers))


class Piece:
    def __init__(self, array, four, size, which, start):
        self.array, self.four, self.size, self.which, self.start = array, four, size, which, start

    def shard(self, refs, y, c):
        return refs[self.array].at[self.which(y, c), rows_at(self.start(y, c), self.size)]

    def at(self, refs, y, c, z, x):
        return refs[self.array].at[self.which(y, c), z, x, rows_at(self.start(y, c), self.size)]

    def column(self, refs, y, c, x):
        return refs[self.array].at[self.which(y, c), :, x, rows_at(self.start(y, c), self.size)]

    def every(self, refs, y, c):
        return refs[self.array].at[self.which(y, c), :, :, rows_at(self.start(y, c), self.size)]


ARRAY_ROWS = ((1, 32), (4, 96), (2, 176), (2, 96), (1, 384), (1, 384))


def corner(array, start):
    return Piece(array, True, 48, lambda y, c: 0, lambda y, c: start + 48 * (2 * y + c))


def halved(array, start):
    return Piece(array, False, 48, lambda y, c: 0, lambda y, c: start + 48 * c)


GATHER_PIECES = (
    Piece(1, True, 32, lambda y, c: 2 * y + c, lambda y, c: 0),
    Piece(1, True, 32, lambda y, c: 2 * y + c, lambda y, c: 32),
    Piece(1, True, 32, lambda y, c: 2 * y + c, lambda y, c: 64),
    Piece(2, True, 48, lambda y, c: y, lambda y, c: 80 * c),
    Piece(2, True, 32, lambda y, c: y, lambda y, c: 80 * c + 48),
    Piece(2, False, 16, lambda y, c: c, lambda y, c: 160),
    Piece(3, True, 48, lambda y, c: y, lambda y, c: 48 * c),
    corner(4, 0),
    halved(4, 192),
    halved(4, 288),
    corner(5, 0),
    halved(5, 192),
    halved(5, 288),
)
GATHER_AHEAD = 2
GATHER_LAGS = (0, 1, 3, 4)
GATHER_SLOTS = len(GATHER_PIECES) + GATHER_LAGS[-1]


def remote(src, dst, send, recv, device):
    return pltpu.make_async_remote_copy(
        src_ref=src, dst_ref=dst, send_sem=send, recv_sem=recv, device_id=device, device_id_type=MESH
    )


class Gather:
    def __init__(self, full, sems):
        self.full = full
        self.here, self.vs, self.zs, self.xs, self.ys, self.cs = sems[:6]
        self.vs_s, self.zs_s, self.xs_s, self.ys_s, self.cs_s = sems[6:]
        y, c, z, x = self.me = place()
        self.zp = [lax.rem(z + i, 4) for i in (1, 2, 3)]
        self.zm = [lax.rem(z + 4 - i, 4) for i in (1, 2, 3)]
        self.to_z = [at_device(y, c, p, x) for p in self.zp]
        self.to_diag = [at_device(y, c, p, 1 - x) for p in self.zp]
        self.to_x, self.to_y = at_device(y, c, z, 1 - x), at_device(1 - y, c, z, x)
        self.to_c = at_device(y, 1 - c, z, x)
        self.sent, self.slot_at = [], 0
        greet(self.to_z + self.to_diag + [self.to_x, self.to_y, self.to_c])

    def go(self, *spec):
        copy = remote(*spec)
        copy.start()
        self.sent.append(copy)

    def arrived(self, dst, recv, send):
        remote(dst, dst, send, recv, self.to_x).wait_recv()

    def start(self, raw, staged, wide, sem):
        y, c, z, x = self.me
        self.own = (raw[0],) + tuple(staged) + (raw[10],)
        places = [(1, 0), (1, 1), (1, 2), (1, 3), (2, 0), (2, 1), (3, 0), (3, 1)]
        loads = [
            pltpu.make_async_copy(raw[1 + i], self.own[array].at[j], sem.at[i])
            for i, (array, j) in enumerate(places)
        ]
        loads.append(pltpu.make_async_copy(raw[9], wide, sem.at[8]))
        for copy in loads:
            copy.start()
        mine = self.full[0].at[0, z, x]
        for i, device in enumerate(self.to_z + self.to_diag + [self.to_x]):
            self.go(self.own[0].at[0], mine, self.vs_s.at[i], self.vs.at[i], device)
        for copy in loads[:4]:
            copy.wait()
        for k in range(GATHER_AHEAD):
            self.send(k)
        for copy in loads[4:]:
            copy.wait()
        self.own[4][0] = wide[...].T
        self.locals = [pltpu.make_async_copy(self.own[0].at[0], mine, self.here.at[0, 0])]
        for k, p in enumerate(GATHER_PIECES):
            for j in range(2 if p.four else 1):
                yy = y if j == 0 else 1 - y
                self.locals.append(
                    pltpu.make_async_copy(
                        p.shard(self.own, yy, c), p.at(self.full, yy, c, z, x), self.here.at[k + 1, j]
                    )
                )
        for copy in self.locals:
            copy.start()
        for copy in self.locals:
            copy.wait()

    def vectors(self):
        y, c, z, x = self.me
        places = [(m, x) for m in self.zm] + [(m, 1 - x) for m in self.zm] + [(z, 1 - x)]
        for i, (zz, xx) in enumerate(places):
            self.arrived(self.full[0].at[0, zz, xx], self.vs.at[i], self.vs_s.at[i])

    def send(self, k):
        y, c, z, x = self.me
        p = GATHER_PIECES[k]
        src, dst = p.shard(self.own, y, c), p.at(self.full, y, c, z, x)
        for i in range(3):
            self.go(src, dst, self.zs_s.at[k, i], self.zs.at[k, i], self.to_z[i])
        self.go(src, dst, self.xs_s.at[k, 0], self.xs.at[k, 0], self.to_x)

    def stage_x(self, k):
        y, c, z, x = self.me
        p = GATHER_PIECES[k]
        for i in range(3):
            got = p.at(self.full, y, c, self.zm[i], x)
            self.arrived(got, self.zs.at[k, i], self.zs_s.at[k, i])
            self.go(got, got, self.xs_s.at[k, i + 1], self.xs.at[k, i + 1], self.to_x)

    def stage_y(self, k):
        y, c, z, x = self.me
        p = GATHER_PIECES[k]
        self.arrived(p.at(self.full, y, c, z, 1 - x), self.xs.at[k, 0], self.xs_s.at[k, 0])
        for i in range(3):
            got = p.at(self.full, y, c, self.zm[i], 1 - x)
            self.arrived(got, self.xs.at[k, i + 1], self.xs_s.at[k, i + 1])
        if p.four:
            far = p.column(self.full, y, c, 1 - x)
            self.go(far, far, self.ys_s.at[k, 0], self.ys.at[k, 0], self.to_y)
            for i in range(3):
                near = p.at(self.full, y, c, self.zm[i], x)
                self.go(near, near, self.ys_s.at[k, i + 1], self.ys.at[k, i + 1], self.to_y)
        mine = p.every(self.full, y, c)
        self.go(mine, mine, self.cs_s.at[k, 0], self.cs.at[k, 0], self.to_c)

    def stage_c(self, k):
        y, c, z, x = self.me
        p = GATHER_PIECES[k]
        if p.four:
            got = p.column(self.full, 1 - y, c, 1 - x)
            self.arrived(got, self.ys.at[k, 0], self.ys_s.at[k, 0])
            for i in range(3):
                got = p.at(self.full, 1 - y, c, self.zm[i], x)
                self.arrived(got, self.ys.at[k, i + 1], self.ys_s.at[k, i + 1])
            mine = p.every(self.full, 1 - y, c)
            self.go(mine, mine, self.cs_s.at[k, 1], self.cs.at[k, 1], self.to_c)

    def finish(self, k):
        y, c, z, x = self.me
        p = GATHER_PIECES[k]
        self.arrived(p.every(self.full, y, 1 - c), self.cs.at[k, 0], self.cs_s.at[k, 0])
        if p.four:
            self.arrived(p.every(self.full, 1 - y, 1 - c), self.cs.at[k, 1], self.cs_s.at[k, 1])

    def advance(self, slots):
        total = len(GATHER_PIECES)
        while self.slot_at < min(slots, GATHER_SLOTS):
            t = self.slot_at
            if GATHER_AHEAD <= t + GATHER_AHEAD < total:
                self.send(t + GATHER_AHEAD)
            stages = (self.stage_x, self.stage_y, self.stage_c, self.finish)
            for lag, stage in zip(GATHER_LAGS, stages):
                if 0 <= t - lag < total:
                    stage(t - lag)
            self.slot_at += 1

    def need(self, k):
        self.advance(k + GATHER_LAGS[-1] + 1)

    def end(self):
        for copy in self.sent:
            copy.wait_send()


def gather_semaphores():
    total, dma = len(GATHER_PIECES), pltpu.SemaphoreType.DMA
    pairs = [dma((7,)), dma((total, 3)), dma((total, 4)), dma((total, 4)), dma((total, 2))]
    return [dma((total + 1, 2))] + pairs + pairs


LOW = jnp.bfloat16
F32 = jnp.float32
KEYS = 272
SCALE = HDIM**-0.5
NN = (((1,), (0,)), ((), ()))
NT = (((1,), (1,)), ((), ()))
TN = (((0,), (0,)), ((), ()))


def mm(a, b, dims=NN):
    return lax.dot_general(a, b, dims, preferred_element_type=F32)


def erf_of(v):
    v = jnp.clip(v, -3.832506856900711, 3.832506856900711)
    s = v * v
    top = jnp.full_like(s, 0.00022905065861350646)
    for k in (0.0034082910107109506, 0.050955695062380861, 0.18520832239976145, 1.128379143519084):
        top = top * s + k
    low = jnp.full_like(s, -1.1791602954361697e-7)
    for k in (0.000023547966471313185, 0.0010179625278914885, 0.014070470171167667, 0.11098505178285362, 0.49746925110067538, 1.0):
        low = low * s + k
    return v * top / low


def norm_parts(v):
    center = v - jnp.mean(v, axis=-1, keepdims=True)
    r = lax.rsqrt(jnp.mean(center * center, axis=-1, keepdims=True) + EPS)
    return center * r, r


def norm_back(dy, xhat, r, gain):
    gdy = gain * dy
    return r * (
        gdy
        - jnp.mean(gdy, axis=-1, keepdims=True)
        - xhat * jnp.mean(gdy * xhat, axis=-1, keepdims=True)
    )


def pair_lanes(v):
    lane = lax.broadcasted_iota(jnp.int32, v.shape, 1)
    zero = jnp.zeros_like(v)
    return jnp.concatenate([jnp.where(lane < HDIM, v, zero), jnp.where(lane < HDIM, zero, v)], axis=0)


def unpair(t):
    n = t.shape[1] // 2
    return jnp.concatenate([t[:HDIM, :n], t[HDIM:, n:]], axis=0).T


def self_mask(lengths, g):
    key = lax.broadcasted_iota(jnp.int32, (128, 256), 0)
    query = lax.broadcasted_iota(jnp.int32, (128, 256), 1) % 128
    late = key >= SEQ
    limit = jnp.where(late, lengths[2 * g + 1], lengths[2 * g]) + NQ
    slot = jnp.where(late, key - SEQ, key)
    return jnp.logical_and(late == (query >= SEQ), slot < limit)


def cross_mask(counts, rows, images):
    shape = (images * KEYS, 2 * rows)
    key = lax.broadcasted_iota(jnp.int32, shape, 0)
    caption = (lax.broadcasted_iota(jnp.int32, (1, 2 * rows), 1) % rows) // NQ
    shows = jnp.zeros_like(caption)
    total = 0
    for i in range(images):
        total = total + counts[0, i]
        shows = shows + (caption >= total).astype(jnp.int32)
    image = jnp.zeros_like(key)
    for i in range(1, images):
        image = image + (key >= i * KEYS).astype(jnp.int32)
    return jnp.logical_and(image == shows, key - image * KEYS < PATCH)


def softmax_down(s):
    e = jnp.exp(s - jnp.max(s, axis=0, keepdims=True))
    return e * (1.0 / jnp.sum(e, axis=0, keepdims=True))


VEC_ROWS = 13
(
    B_QUERY,
    B_VALUE,
    B_OUT,
    GAIN_1,
    SHIFT_1,
    B_CQUERY,
    B_CVALUE,
    B_COUT,
    GAIN_2,
    SHIFT_2,
    B_CONTRACT,
    GAIN_3,
    SHIFT_3,
) = range(VEC_ROWS)


def lanes_at(i, size=128):
    return pl.ds(pl.multiple_of(i * size, 128), size)


def forward_steps(r):
    tokens = r.x.shape[0]
    rows = tokens // 2
    half = tokens // 2
    images, feat = r.feats.shape[0], r.feats.shape[2]
    keys = images * KEYS
    pairs = D // 128

    def vec(i):
        return r.vec[i : i + 1, :]

    gain_v, shift_v = r.vec_feat[0:1, :], r.vec_feat[1:2, :]
    for image in range(images):

        def vision_step(i, carry):
            xhat, _ = norm_parts(r.feats[image, rows_at(i * 64, 64), :].astype(F32))
            to = rows_at(image * KEYS + i * 64, 64)
            r.vision[to, :] = (xhat * gain_v + shift_v).astype(LOW)
            r.xhat_v[to, :] = xhat.astype(LOW)
            return carry

        lax.fori_loop(0, PATCH // 64, vision_step, 0)
        xhat, _ = norm_parts(r.feats[image, PATCH - 1 : PATCH, :].astype(F32))
        only = lax.broadcasted_iota(jnp.int32, (16, feat), 0) == 0
        to = pl.ds(image * KEYS + PATCH - 1, 16)
        r.vision[to, :] = jnp.where(only, xhat * gain_v + shift_v, 0.0).astype(LOW)
        r.xhat_v[to, :] = jnp.where(only, xhat, 0.0).astype(LOW)
        r.step()
    r.shown[...] = jnp.where(cross_mask(r.counts, rows, images), 3e38, -3e38)
    r.save(K.vision, K.xhat_v)

    def project_to(dst, weight, bias):
        def step(i, carry):
            at = rows_at(i * half, half)
            out = mm(r.x[at, :], weight[...])
            if bias is not None:
                out = out + vec(bias)
            dst[at, :] = out.astype(LOW)
            return carry

        lax.fori_loop(0, 2, step, 0)

    def self_step(i, carry):
        lanes = lanes_at(i)
        for g in range(tokens // 128):
            at = pl.ds(g * 128, 128)
            s = mm(r.k[at, lanes], pair_lanes(r.q[at, lanes] * SCALE), NT)
            p = softmax_down(jnp.where(self_mask(r.lengths, g), s, MASKED)).astype(LOW)
            r.p_self[i, g] = p
            r.mixed[at, lanes] = unpair(mm(r.v[at, lanes], p, TN)).astype(LOW)
        return carry

    r.need(2)
    r.save_weights(1)
    project_to(r.q, r.w_self(0), B_QUERY)
    r.step()
    project_to(r.k, r.w_self(1), None)
    project_to(r.v, r.w_self(2), B_VALUE)
    r.step()
    lax.fori_loop(0, pairs // 2, self_step, 0)
    r.step()
    lax.fori_loop(pairs // 2, pairs, self_step, 0)
    r.save(K.q, K.k, K.v, K.p_self, K.mixed)
    r.step()

    def out_step(i, carry):
        at = rows_at(i * half, half)
        v = r.x[at, :].astype(F32) + (mm(r.mixed[at, :], r.w_self(3)[...]) + vec(B_OUT))
        xhat, scale = norm_parts(v)
        r.xhat1[at, :] = xhat
        r.r1[at, :] = jnp.broadcast_to(scale, (half, 128))
        r.joined[at, :] = xhat * vec(GAIN_1) + vec(SHIFT_1)
        return carry

    lax.fori_loop(0, 2, out_step, 0)
    for c in range(tokens // SEQ):
        r.cross_in[pl.ds(c * NQ, NQ), :] = r.joined[pl.ds(c * SEQ, NQ), :].astype(LOW)
    r.save(K.xhat1, K.r1, K.cross_in)
    r.need(5)
    r.save_weights(2)
    for image in range(images):
        at = pl.ds(image * KEYS, KEYS)
        r.ck[at, :] = mm(r.vision[at, :], r.w_ckey[...]).astype(LOW)
        r.cv[at, :] = (mm(r.vision[at, :], r.w_cvalue[...]) + vec(B_CVALUE)).astype(LOW)
        if image == 1:
            r.step()
    r.save(K.ck, K.cv)
    r.need(6)
    r.save_weights(3)
    r.cq[...] = (mm(r.cross_in[...], r.w_cross(0)[...]) + vec(B_CQUERY)).astype(LOW)

    def cross_step(i, carry):
        lanes = lanes_at(i)
        s = mm(r.ck[:, lanes], pair_lanes(r.cq[:, lanes] * SCALE), NT)
        p = softmax_down(jnp.minimum(s, r.shown[...])).astype(LOW)
        r.keep_cross(i, p)
        r.cmixed[:, lanes] = unpair(mm(r.cv[:, lanes], p, TN)).astype(LOW)
        return carry

    for first in range(0, pairs, 2):
        r.step()
        lax.fori_loop(first, first + 2, cross_step, 0)
    r.save(K.cq, K.cmixed)
    r.step()
    branch = mm(r.cmixed[...], r.w_cross(1)[...]) + vec(B_COUT)
    for c in range(tokens // SEQ):
        own, at = pl.ds(c * NQ, NQ), pl.ds(c * SEQ, NQ)
        xhat, scale = norm_parts(r.joined[at, :] + branch[c * NQ : (c + 1) * NQ, :])
        r.xhat2[own, :] = xhat
        r.r2[own, :] = jnp.broadcast_to(scale, (NQ, 128))
        r.joined[at, :] = xhat * vec(GAIN_2) + vec(SHIFT_2)
    r.joined_low[...] = r.joined[...].astype(LOW)
    r.save(K.xhat2, K.r2, K.joined_low)
    tile = 768
    tiles = r.active.shape[0]
    r.need(9)
    r.save_weights(4)

    def wide_step(n, carry):
        at = rows_at(n * tile, tile)
        r.before_slope(n)
        for m in range(2):
            part = pl.ds(m * half, half)
            wide = mm(r.joined_low[part, :], r.w_expand[at, :], NT) + r.vec_ff[0:1, lanes_at(n, tile)]
            cdf = 0.5 * (1.0 + erf_of(wide * 0.7071067811865476))
            slope = cdf + wide * (jnp.exp(-0.5 * wide * wide) * 0.3989422804014327)
            r.active[n, part, :] = (wide * cdf).astype(LOW)
            r.slope[n % 2, part, :] = slope.astype(LOW)
        r.after_slope(n)
        return carry

    for first in range(tiles):
        lax.fori_loop(first, first + 1, wide_step, 0)
        r.step()
    r.need(12)
    r.save_weights(5)
    gain3, shift3, bias3 = vec(GAIN_3), vec(SHIFT_3), vec(B_CONTRACT)
    zero = jnp.zeros((1, D), F32)
    dgain, dshift = zero, zero
    for m in range(2):
        part = pl.ds(m * half, half)

        def narrow_step(n, carry):
            return carry + mm(r.active[n, part, :], r.w_contract[rows_at(n * tile, tile), :])

        r.acc[...] = lax.fori_loop(0, tiles, narrow_step, jnp.zeros((half, D), F32))

        def last_step(i, carry):
            at = rows_at(m * half + i * 64, 64)
            xhat, scale = norm_parts(r.joined[at, :] + (r.acc[rows_at(i * 64, 64), :] + bias3))
            r.layer_out[at, :] = xhat * gain3 + shift3
            dy = r.out_grad[at, :].astype(F32)
            r.dthree[at, :] = norm_back(dy, xhat, scale, gain3)
            return (
                carry[0] + jnp.sum(dy * xhat, axis=0, keepdims=True),
                carry[1] + jnp.sum(dy, axis=0, keepdims=True),
            )

        dgain, dshift = lax.fori_loop(0, half // 64, last_step, (dgain, dshift))
    r.dvec3[...] = jnp.zeros_like(r.dvec3)
    r.dvec3[0:1, :] = dgain
    r.dvec3[1:2, :] = dshift
    r.save(K.dthree, K.layer_out, K.dvec3)


def spread(size, width, taken, offset):
    row = lax.broadcasted_iota(jnp.int32, (size, width), 0)
    lane = lax.broadcasted_iota(jnp.int32, (size, width), 1)
    return jnp.logical_and(lane == row + offset, row < taken).astype(F32).astype(LOW)


def build_vectors(rows, vec, vec_feat, vec_ff):
    feat, ff = vec_feat.shape[1], vec_ff.shape[1]
    one, two, three = D // 8, feat // 8, ff // 8
    total = jnp.zeros(vec.shape, F32)
    total_feat = jnp.zeros((16, feat), F32)
    for d in range(8):
        part = rows[0, d // 2, d % 2, 0:16, :]
        total = total + mm(part[:, :128], spread(128, D, one, one * d))
        total_feat = total_feat + mm(part[:, :256], spread(256, feat, two, two * d))
        vec_ff[0:1, d * three : (d + 1) * three] = part[15:16, :three].astype(F32)
    vec[...] = total
    vec_feat[0:2, :] = total_feat[VEC_ROWS : VEC_ROWS + 2]


def column_sum(v):
    return jnp.sum(v.astype(F32), axis=0, keepdims=True)


def weight_into(target, a, b, at=0, block=256):
    width = a.shape[1]
    for start in range(0, width, block):
        size = min(block, width - start)
        target[pl.ds(at + start, size), :] = mm(a[:, start : start + size], b[...], TN).astype(LOW)


def backward_ffn(r):
    tokens = r.dthree.shape[0]
    half = tokens // 2
    tile = 768
    tiles = r.w_contract.shape[0] // tile
    r.wait(K.dthree, WEIGHT_LOAD + 5)
    r.dn[...] = r.dthree[...].astype(LOW)
    r.dvec[B_CONTRACT : B_CONTRACT + 1, :] = column_sum(r.dn[...])

    def contract_step(n, carry):
        slot = r.ffn_tile(n)
        total = jnp.zeros((1, tile), F32)
        at = rows_at(n * tile, tile)
        for m in range(2):
            part = pl.ds(m * half, half)
            up = mm(r.dn[part, :], r.w_contract[at, :], NT)
            wide = (up * r.slope[slot, part, :].astype(F32)).astype(LOW)
            r.dwide[n, part, :] = wide
            total = total + column_sum(wide)
        r.dvec_ff[0:1, lanes_at(n, tile)] = total
        for j in range(3):
            lanes = slice(j * 256, (j + 1) * 256)
            to = rows_at(n * tile + j * 256, 256)
            r.w_contract[to, :] = mm(r.active[slot, :, lanes], r.dn[...], TN).astype(LOW)
        return carry

    lax.fori_loop(0, tiles, contract_step, 0)
    r.begin(3, 5)
    r.wait(K.joined_low, WEIGHT_LOAD + 4)

    def expand_step(n, carry):
        at = rows_at(n * tile, tile)
        for m in range(2):
            part = pl.ds(m * half, half)
            r.dthree[part, :] += mm(r.dwide[n, part, :], r.w_expand[at, :])
        for j in range(3):
            lanes = slice(j * 256, (j + 1) * 256)
            to = rows_at(n * tile + j * 256, 256)
            r.w_expand[to, :] = mm(r.dwide[n, :, lanes], r.joined_low[...], TN).astype(LOW)
        return carry

    for first in range(tiles):
        lax.fori_loop(first, first + 1, expand_step, 0)
        r.step()
    r.begin(3, 4)


def backward_cross(r):
    tokens = r.dthree.shape[0]
    rows = tokens // 2
    keys = r.ck.shape[0]
    r.wait(K.xhat2, K.r2, K.cmixed, WEIGHT_LOAD + 3)
    gain = r.vec[GAIN_2 : GAIN_2 + 1, :]
    dgain, dshift = jnp.zeros((1, D), F32), jnp.zeros((1, D), F32)
    for c in range(tokens // SEQ):
        own, at = pl.ds(c * NQ, NQ), pl.ds(c * SEQ, NQ)
        dy, xhat = r.dthree[at, :], r.xhat2[own, :]
        dgain = dgain + column_sum(dy * xhat)
        dshift = dshift + column_sum(dy)
        dtwo = norm_back(dy, xhat, r.r2[own, 0:1], gain)
        r.dthree[at, :] = dtwo
        r.dcb[own, :] = dtwo.astype(LOW)
    r.dvec[GAIN_2 : GAIN_2 + 1, :] = dgain
    r.dvec[SHIFT_2 : SHIFT_2 + 1, :] = dshift
    r.dvec[B_COUT : B_COUT + 1, :] = column_sum(r.dcb[...])
    r.dcm[...] = mm(r.dcb[...], r.w_cross(1)[...], NT).astype(LOW)
    weight_into(r.w_cross(1), r.cmixed[...], r.dcb)
    r.step()
    r.wait(K.ck, K.cv, K.cq)

    def step(i, carry):
        lanes = lanes_at(i)
        slot = r.cross_tile(i)
        low = r.p_cross[slot]
        p = low.astype(F32)
        up = pair_lanes(r.dcm[:, lanes])
        dp = mm(r.cv[:, lanes], up, NT)
        ds = (p * (dp - jnp.sum(p * dp, axis=0, keepdims=True))).astype(LOW)
        r.cv[:, lanes] = mm(low, up).astype(LOW)
        dq = unpair(mm(r.ck[:, lanes], ds, TN)) * SCALE
        r.ck[:, lanes] = (mm(ds, pair_lanes(r.cq[:, lanes])) * SCALE).astype(LOW)
        r.dcq[:, lanes] = dq.astype(LOW)
        return carry

    for first in range(0, D // 128, 2):
        lax.fori_loop(first, first + 2, step, 0)
        r.step()
    r.dvec[B_CVALUE : B_CVALUE + 1, :] = column_sum(r.cv[...])
    r.dvec[B_CQUERY : B_CQUERY + 1, :] = column_sum(r.dcq[...])
    r.wait(WEIGHT_LOAD + 2, K.vision, K.xhat_v, K.cross_in)
    feat = r.vision.shape[1]
    zero = jnp.zeros((1, feat), F32)

    def vision_step(i, carry):
        at = rows_at(i * KEYS, KEYS)
        up = mm(r.ck[at, :], r.w_ckey[...], NT) + mm(r.cv[at, :], r.w_cvalue[...], NT)
        return (
            carry[0] + column_sum(up * r.xhat_v[at, :].astype(F32)),
            carry[1] + column_sum(up),
        )

    carry = (zero, zero)
    for image in range(keys // KEYS):
        carry = vision_step(image, carry)
        if image == 1:
            r.step()
    dgain, dshift = carry
    r.dvec_feat[VEC_ROWS : VEC_ROWS + 1, :] = dgain
    r.dvec_feat[VEC_ROWS + 1 : VEC_ROWS + 2, :] = dshift
    r.step()
    for start, size in ((0, 512), (512, 512), (1024, 384)):
        columns = r.vision[:, start : start + size]
        r.w_ckey[pl.ds(start, size), :] = mm(columns, r.ck[...], TN).astype(LOW)
        r.w_cvalue[pl.ds(start, size), :] = mm(columns, r.cv[...], TN).astype(LOW)
        r.step()
    r.begin(2, 2)
    back = mm(r.dcq[...], r.w_cross(0)[...], NT)
    for c in range(tokens // SEQ):
        at = pl.ds(c * SEQ, NQ)
        r.dthree[at, :] += back[c * NQ : (c + 1) * NQ, :]
    weight_into(r.w_cross(0), r.cross_in[...], r.dcq)
    r.begin(2, 3)
    r.step()


def backward_self(r):
    tokens = r.dthree.shape[0]
    half = tokens // 2
    r.wait(K.xhat1, K.r1, K.mixed, WEIGHT_LOAD + 1)
    gain = r.vec[GAIN_1 : GAIN_1 + 1, :]
    zero = jnp.zeros((1, D), F32)

    def norm_step(i, carry):
        at = rows_at(i * 128, 128)
        dy, xhat = r.dthree[at, :], r.xhat1[at, :]
        done = norm_back(dy, xhat, r.r1[at, 0:1], gain)
        r.dthree[at, :] = done
        low = done.astype(LOW)
        r.dn[at, :] = low
        return (
            carry[0] + column_sum(dy * xhat),
            carry[1] + column_sum(dy),
            carry[2] + column_sum(low),
        )

    dgain, dshift, dbias = lax.fori_loop(0, tokens // 128, norm_step, (zero, zero, zero))
    r.dvec[GAIN_1 : GAIN_1 + 1, :] = dgain
    r.dvec[SHIFT_1 : SHIFT_1 + 1, :] = dshift
    r.dvec[B_OUT : B_OUT + 1, :] = dbias
    for m in range(2):
        part = pl.ds(m * half, half)
        r.dm[part, :] = mm(r.dn[part, :], r.w_self(3)[...], NT).astype(LOW)
    weight_into(r.w_self(3), r.mixed[...], r.dn)
    r.begin(1)
    r.step()
    r.wait(K.q, K.k, K.v, K.p_self)

    def step(i, carry):
        lanes = lanes_at(i)
        for g in range(tokens // 128):
            at = pl.ds(g * 128, 128)
            low = r.p_self[i, g]
            p = low.astype(F32)
            up = pair_lanes(r.dm[at, lanes])
            dp = mm(r.v[at, lanes], up, NT)
            ds = (p * (dp - jnp.sum(p * dp, axis=0, keepdims=True))).astype(LOW)
            dq = unpair(mm(r.k[at, lanes], ds, TN)) * SCALE
            dk = mm(ds, pair_lanes(r.q[at, lanes])) * SCALE
            r.v[at, lanes] = mm(low, up).astype(LOW)
            r.q[at, lanes] = dq.astype(LOW)
            r.k[at, lanes] = dk.astype(LOW)
        return carry

    for first in range(0, D // 128, 2):
        lax.fori_loop(first, first + 2, step, 0)
        r.step()
    r.dvec[B_QUERY : B_QUERY + 1, :] = column_sum(r.q[...])
    r.dvec[B_VALUE : B_VALUE + 1, :] = column_sum(r.v[...])
    r.wait(X_LOAD)
    for j, ref in enumerate((r.q, r.k, r.v)):
        for m in range(2):
            part = pl.ds(m * half, half)
            r.dthree[part, :] += mm(ref[part, :], r.w_self(j)[...], NT)
        weight_into(r.w_self(j), r.x[...], ref)
        if j == 1:
            r.begin(1)
        r.step()
    r.begin(1, 1)


SUM_PARTS = (
    (corner(5, 0), 0),
    (halved(5, 192), 2),
    (halved(5, 288), 3),
    (corner(4, 0), 1),
    (halved(4, 192), 4),
    (halved(4, 288), 5),
    (Piece(2, True, 48, lambda y, c: y, lambda y, c: 48 * c), 0),
    (Piece(2, False, 80, lambda y, c: c, lambda y, c: 96), 6),
    (Piece(3, True, 32, lambda y, c: y, lambda y, c: 32 * c), 7),
    (Piece(3, False, 32, lambda y, c: c, lambda y, c: 64), 8),
    (Piece(1, False, 48, lambda y, c: 3, lambda y, c: 48 * c), 2),
    (Piece(1, True, 48, lambda y, c: y, lambda y, c: 48 * c), 1),
    (Piece(1, False, 48, lambda y, c: 2, lambda y, c: 48 * c), 3),
    (Piece(0, False, 16, lambda y, c: 0, lambda y, c: 16 * c), 9),
)
SUM_PIECES = tuple(p for p, _ in SUM_PARTS)
LANDING = tuple(b for _, b in SUM_PARTS)
BUFFERS = max(LANDING) + 1
SUM_LAGS = (0, 2, 4, 6, 8, 9)


def next_user(k):
    for later in range(k + 1, len(LANDING)):
        if LANDING[later] == LANDING[k]:
            return later
    return None


def reuses(k):
    return LANDING[k] in LANDING[:k]


class Reduce:
    def __init__(self, grads, outs, refs):
        total = len(SUM_PIECES)
        self.grads, self.outs = grads, outs
        self.from_c, self.from_y, self.from_x, self.from_z = (
            refs[i * BUFFERS : (i + 1) * BUFFERS] for i in range(4)
        )
        refs = refs[4 * BUFFERS :]
        self.last, refs = refs[:total], refs[total:]
        self.done, self.credit, self.cs, self.ys, self.xs, self.zs, self.fs = refs[:7]
        self.cs_s, self.ys_s, self.xs_s, self.zs_s, self.fs_s = refs[7:]
        y, c, z, x = self.me = place()
        self.zp = [lax.rem(z + i, 4) for i in (1, 2, 3)]
        self.to_z = [at_device(y, c, p, x) for p in self.zp]
        self.back_z = [at_device(y, c, lax.rem(z + 4 - i, 4), x) for i in (1, 2, 3)]
        self.to_x, self.to_y = at_device(y, c, z, 1 - x), at_device(1 - y, c, z, x)
        self.to_c, self.to_d = at_device(y, 1 - c, z, x), at_device(1 - y, 1 - c, z, x)
        self.sent, self.stored, self.slot_at, self.begun = [], [], 0, 0
        self.z_sends = {}
        greet(self.to_z + [self.to_x, self.to_y, self.to_c, self.to_d])

    def go(self, *spec):
        copy = remote(*spec)
        copy.start()
        self.sent.append(copy)
        return copy

    def arrived(self, dst, recv, send):
        remote(dst, dst, send, recv, self.to_x).wait_recv()

    def sides(self, k):
        y = self.me[0]
        return (y, 1 - y) if SUM_PIECES[k].four else (y,)

    def owe(self, k, i, device):
        later = next_user(k)
        if later is not None:
            pl.semaphore_signal(
                self.credit.at[later, i], inc=1, device_id=device, device_id_type=MESH
            )

    def ask(self, k, i):
        if reuses(k):
            pl.semaphore_wait(self.credit.at[k, i], 1)

    def begin(self, count):
        c = self.me[1]
        for k in range(self.begun, self.begun + count):
            p = SUM_PIECES[k]
            self.ask(k, 0)
            for j, yy in enumerate(self.sides(k)):
                land = self.from_c[LANDING[k]].at[j]
                self.go(p.every(self.grads, yy, 1 - c), land, self.cs_s.at[k, j], self.cs.at[k, j], self.to_c)
        self.begun += count

    def stage_c(self, k):
        y, c, z, x = self.me
        p, buf = SUM_PIECES[k], self.from_c[LANDING[k]]
        sides = self.sides(k)
        for j in reversed(range(len(sides))):
            self.arrived(buf.at[j], self.cs.at[k, j], self.cs_s.at[k, j])
            for i in range(4):
                for l in range(2):
                    mine = p.at(self.grads, sides[j], c, i, l)
                    mine[...] = mine[...] + buf[j, i, l]
            if j == 1:
                self.ask(k, 1)
                mine = p.every(self.grads, sides[1], c)
                self.go(mine, self.from_y[LANDING[k]], self.ys_s.at[k], self.ys.at[k], self.to_y)
        self.owe(k, 0, self.to_c)

    def stage_y(self, k):
        y, c, z, x = self.me
        p = SUM_PIECES[k]
        if p.four:
            buf = self.from_y[LANDING[k]]
            self.arrived(buf, self.ys.at[k], self.ys_s.at[k])
            for i in range(4):
                for l in range(2):
                    mine = p.at(self.grads, y, c, i, l)
                    mine[...] = mine[...] + buf[i, l]
            self.owe(k, 1, self.to_y)
        self.ask(k, 2)
        far = p.column(self.grads, y, c, 1 - x)
        self.go(far, self.from_x[LANDING[k]], self.xs_s.at[k], self.xs.at[k], self.to_x)

    def stage_x(self, k):
        y, c, z, x = self.me
        p, buf = SUM_PIECES[k], self.from_x[LANDING[k]]
        self.arrived(buf, self.xs.at[k], self.xs_s.at[k])
        for i in range(4):
            buf[i] = buf[i] + p.at(self.grads, y, c, i, x)[...]
        land = self.from_z[LANDING[k]]
        self.z_sends[k] = []
        for i in range(3):
            self.ask(k, 3 + i)
            copy = remote(buf.at[self.zp[i]], land.at[i], self.zs_s.at[k, i], self.zs.at[k, i], self.to_z[i])
            copy.start()
            self.z_sends[k].append(copy)

    def stage_z(self, k):
        y, c, z, x = self.me
        p, buf, land, last = SUM_PIECES[k], self.from_x[LANDING[k]], self.from_z[LANDING[k]], self.last[k]
        for i in range(3):
            self.arrived(land.at[i], self.zs.at[k, i], self.zs_s.at[k, i])
        value = buf[z].astype(F32)
        for i in range(3):
            value = value + land[i].astype(F32)
        last[0] = value.astype(LOW)
        if p.four:
            out = p.shard(self.outs, y, c)
            for j, device in enumerate((self.to_y, self.to_c, self.to_d)):
                self.go(last.at[0], out, self.fs_s.at[k, j], self.fs.at[k, j], device)
            self.put(k, 0)
        else:
            self.go(last.at[0], last.at[1], self.fs_s.at[k, 0], self.fs.at[k, 0], self.to_y)
        for copy in self.z_sends[k]:
            copy.wait_send()
        self.owe(k, 2, self.to_x)
        for i in range(3):
            self.owe(k, 3 + i, self.back_z[i])

    def put(self, k, slot):
        y, c, z, x = self.me
        out = SUM_PIECES[k].shard(self.outs, y, c)
        copy = pltpu.make_async_copy(self.last[k].at[slot], out, self.done.at[k])
        copy.start()
        self.stored.append(copy)

    def stage_f(self, k):
        y, c, z, x = self.me
        p, last = SUM_PIECES[k], self.last[k]
        if not p.four:
            self.arrived(last.at[1], self.fs.at[k, 0], self.fs_s.at[k, 0])
            last[2] = last[0] + last[1]
            out = p.shard(self.outs, y, c)
            self.go(last.at[2], out, self.fs_s.at[k, 1], self.fs.at[k, 1], self.to_c)
            self.put(k, 2)

    def stage_g(self, k):
        y, c, z, x = self.me
        p = SUM_PIECES[k]
        if p.four:
            places = ((1 - y, c), (y, 1 - c), (1 - y, 1 - c))
            for j, (yy, cc) in enumerate(places):
                self.arrived(p.shard(self.outs, yy, cc), self.fs.at[k, j], self.fs_s.at[k, j])
        else:
            self.arrived(p.shard(self.outs, y, 1 - c), self.fs.at[k, 1], self.fs_s.at[k, 1])

    def advance(self, slots):
        total = len(SUM_PIECES)
        stages = (self.stage_c, self.stage_y, self.stage_x, self.stage_z, self.stage_f, self.stage_g)
        while self.slot_at < slots:
            if self.slot_at >= self.begun < total:
                return
            for lag, stage in zip(SUM_LAGS, stages):
                if 0 <= self.slot_at - lag < total:
                    stage(self.slot_at - lag)
            self.slot_at += 1

    def step(self):
        self.advance(self.slot_at + 1)

    def end(self):
        self.advance(len(SUM_PIECES) + SUM_LAGS[-1])
        for copy in self.sent:
            copy.wait_send()
        for copy in self.stored:
            copy.wait()


def reduce_scratch():
    total, dma = len(SUM_PIECES), pltpu.SemaphoreType.DMA
    first = [SUM_PIECES[LANDING.index(b)] for b in range(BUFFERS)]
    pairs = [dma((total, 2)), dma((total,)), dma((total,)), dma((total, 3)), dma((total, 3))]
    return (
        [pltpu.VMEM((2 if p.four else 1, 4, 2, p.size, D), LOW) for p in first]
        + [pltpu.VMEM((4, 2, p.size, D) if p.four else (1, 1, 16, 128), LOW) for p in first]
        + [pltpu.VMEM((4, p.size, D), LOW) for p in first]
        + [pltpu.VMEM((3, p.size, D), LOW) for p in first]
        + [pltpu.VMEM((1 if p.four else 3, p.size, D), LOW) for p in SUM_PIECES]
        + [dma((total,)), pltpu.SemaphoreType.REGULAR((total, 6))]
        + pairs
        + pairs
    )


def pack_vectors(rows, dvec, dvec_feat, dvec_ff):
    feat, ff = dvec_feat.shape[1], dvec_ff.shape[1]
    one, two, three = D // 8, feat // 8, ff // 8
    low, low_feat = dvec[...].astype(LOW), dvec_feat[...].astype(LOW)
    row = lax.broadcasted_iota(jnp.int32, (16, three), 0)
    for d in range(8):
        small = mm(low, spread(128, D, one, one * d), NT)
        wide = mm(low_feat, spread(256, feat, two, two * d), NT)
        block = jnp.concatenate([small + wide[:, :128], wide[:, 128:], jnp.zeros((16, three - 256), F32)], axis=1)
        block = jnp.where(row == 15, dvec_ff[0:1, d * three : (d + 1) * three], block)
        rows[0, d // 2, d % 2, 0:16, :three] = block.astype(LOW)
        rows[0, d // 2, d % 2, 0:16, three:] = jnp.zeros((16, D - three), LOW)
        rows[0, d // 2, d % 2, 16:32, :] = jnp.zeros((16, D), LOW)


class Refs:
    def __init__(self, **names):
        self.__dict__.update(names)


class Saved(typing.NamedTuple):
    vision: typing.Any
    xhat_v: typing.Any
    q: typing.Any
    k: typing.Any
    v: typing.Any
    p_self: typing.Any
    mixed: typing.Any
    xhat1: typing.Any
    r1: typing.Any
    cross_in: typing.Any
    ck: typing.Any
    cv: typing.Any
    cq: typing.Any
    cmixed: typing.Any
    xhat2: typing.Any
    r2: typing.Any
    joined_low: typing.Any
    dthree: typing.Any
    layer_out: typing.Any
    dvec3: typing.Any
    vec: typing.Any
    active: typing.Any
    slope: typing.Any
    p_cross: typing.Any


K = Saved(*range(len(Saved._fields)))
HELD = K.vec + 1
X_LOAD, WEIGHT_LOAD = 100, 200
RAW = 11
VMEM_BYTES = 63 * 1024 * 1024


def saved_shapes(tokens, images, feat, ff):
    rows, keys = tokens // 2, images * KEYS
    return Saved(
        vision=((keys, feat), LOW),
        xhat_v=((keys, feat), LOW),
        q=((tokens, D), LOW),
        k=((tokens, D), LOW),
        v=((tokens, D), LOW),
        p_self=((D // 128, tokens // 128, 128, 256), LOW),
        mixed=((tokens, D), LOW),
        xhat1=((tokens, D), F32),
        r1=((tokens, 128), F32),
        cross_in=((rows, D), LOW),
        ck=((keys, D), LOW),
        cv=((keys, D), LOW),
        cq=((rows, D), LOW),
        cmixed=((rows, D), LOW),
        xhat2=((rows, D), F32),
        r2=((rows, 128), F32),
        joined_low=((tokens, D), LOW),
        dthree=((tokens, D), F32),
        layer_out=((tokens, D), F32),
        dvec3=((8, D), F32),
        vec=((16, D), F32),
        active=((ff // 768, tokens, 768), LOW),
        slope=((ff // 768, tokens, 768), LOW),
        p_cross=((D // 128, keys, 2 * rows), LOW),
    )


def full_views(full):
    def flat(ref, j):
        return ref.at[j].reshape(8 * ref.shape[3], D)

    return dict(
        w_self=lambda j: flat(full[1], j),
        w_ckey=flat(full[2], 0),
        w_cvalue=flat(full[2], 1),
        w_cross=lambda j: flat(full[3], j),
        w_expand=flat(full[4], 0),
        w_contract=flat(full[5], 0),
    )


def forward_kernel(fast, *refs):
    count = len(ARRAY_ROWS)
    (counts, lengths, x, feats, out_grad), refs = refs[:5], refs[5:]
    inputs = RAW if fast else count
    own, refs = refs[:inputs], refs[inputs:]
    if not fast:
        vec_in, refs = refs[:3], refs[3:]
    outs, refs = Saved(*refs[: len(K)]), refs[len(K) :]
    weights, refs = refs[: count - 1], refs[count - 1 :]
    held, refs = refs[:HELD], refs[HELD:]
    full, refs = refs[:count], refs[count:]
    vec_feat, vec_ff, joined, acc, shown, active, slope, pbuf = refs[:8]
    save_sem, weight_sem, active_sem, slope_sem, p_sem = refs[8:13]
    kept = dict(zip(Saved._fields, held))
    vec = kept[Saved._fields[K.vec]]
    pairs, tiles = outs.p_cross.shape[0], outs.slope.shape[0]
    copies = []

    def begin(copy):
        copy.start()
        copies.append(copy)

    def save(*names):
        for i in names:
            begin(pltpu.make_async_copy(held[i], outs[i], save_sem.at[i]))

    def save_weights(i):
        begin(pltpu.make_async_copy(full[i], weights[i - 1], weight_sem.at[i]))

    def p_copy(i):
        return pltpu.make_async_copy(pbuf.at[i % 2], outs.p_cross.at[i], p_sem.at[i % 2])

    def slope_copy(n):
        return pltpu.make_async_copy(slope.at[n % 2], outs.slope.at[n], slope_sem.at[n % 2])

    def active_copy(n):
        return pltpu.make_async_copy(active.at[n], outs.active.at[n], active_sem.at[n])

    def keep_cross(i, p):
        @pl.when(i >= 2)
        def _():
            p_copy(i - 2).wait()

        pbuf[i % 2] = p
        p_copy(i).start()

    def before_slope(n):
        @pl.when(n >= 2)
        def _():
            slope_copy(n - 2).wait()

    def after_slope(n):
        slope_copy(n).start()
        active_copy(n).start()

    if fast:
        staged, wide, stage_sem, sems = refs[13:17], refs[17], refs[18], refs[19:]
        gather = Gather(full, sems)
        gather.start(own, staged, wide, stage_sem)
        gather.vectors()
        build_vectors(full[0], vec, vec_feat, vec_ff)
        need = gather.need

        def step():
            gather.advance(gather.slot_at + 1)
    else:
        loads = [pltpu.make_async_copy(own[i], full[i], weight_sem.at[i]) for i in range(count)]
        loads += [
            pltpu.make_async_copy(src, dst, p_sem.at[0])
            for src, dst in zip(vec_in, (vec, vec_feat, vec_ff))
        ]
        for copy in loads:
            copy.start()
            copy.wait()

        def need(k):
            pass

        def step():
            pass

    save(K.vec)
    r = Refs(
        counts=counts,
        lengths=lengths,
        x=x,
        feats=feats,
        out_grad=out_grad,
        **kept,
        **full_views(full),
        vec_feat=vec_feat,
        vec_ff=vec_ff,
        joined=joined,
        acc=acc,
        shown=shown,
        active=active,
        slope=slope,
        save=save,
        save_weights=save_weights,
        need=need,
        step=step,
        keep_cross=keep_cross,
        before_slope=before_slope,
        after_slope=after_slope,
    )
    forward_steps(r)
    for i in (pairs - 2, pairs - 1):
        p_copy(i).wait()
    for n in (tiles - 2, tiles - 1):
        slope_copy(n).wait()
    for n in range(tiles):
        active_copy(n).wait()
    for copy in copies:
        copy.wait()
    if fast:
        gather.end()


def stage_scratch(ff):
    shapes = [(k, rows, D) for k, rows in ARRAY_ROWS[1:5]]
    return [pltpu.VMEM(s, LOW) for s in shapes + [(D, ff // 8)]] + [pltpu.SemaphoreType.DMA((9,))]


def forward_all(fast, counts, lengths, x, feats, out_grad, own, vectors):
    tokens, images, feat = x.shape[0], feats.shape[0], feats.shape[2]
    count = len(ARRAY_ROWS)
    if fast:
        full = [(k, 4, 2, rows, D) for k, rows in ARRAY_ROWS]
    else:
        full = [w.shape for w in own]
    ff = 8 * full[4][3]
    rows, keys = tokens // 2, images * KEYS
    shapes = saved_shapes(tokens, images, feat, ff)
    vmem, smem = pl.BlockSpec(memory_space=pltpu.VMEM), pl.BlockSpec(memory_space=pltpu.SMEM)
    hbm = pl.BlockSpec(memory_space=pl.ANY)
    ins = [counts, lengths, x, feats, out_grad, *own]
    if not fast:
        ins += list(vectors)
    out_shape = [jax.ShapeDtypeStruct(*shape) for shape in shapes]
    out_shape += [jax.ShapeDtypeStruct(shape, LOW) for shape in full[1:]]
    dma = pltpu.SemaphoreType.DMA
    outs = pl.pallas_call(
        functools.partial(forward_kernel, fast),
        name="forward",
        out_shape=out_shape,
        in_specs=[smem, smem] + [vmem] * 3 + [hbm] * (len(ins) - 5),
        out_specs=[hbm] * len(out_shape),
        scratch_shapes=[pltpu.VMEM(*shape) for shape in shapes[:HELD]]
        + [pltpu.VMEM(shape, LOW) for shape in full]
        + [
            pltpu.VMEM((8, feat), F32),
            pltpu.VMEM((8, ff), F32),
            pltpu.VMEM((tokens, D), F32),
            pltpu.VMEM((tokens // 2, D), F32),
            pltpu.VMEM((keys, 2 * rows), F32),
            pltpu.VMEM((ff // 768, tokens, 768), LOW),
            pltpu.VMEM((2, tokens, 768), LOW),
            pltpu.VMEM((2, keys, 2 * rows), LOW),
            dma((HELD,)),
            dma((count,)),
            dma((ff // 768,)),
            dma((2,)),
            dma((2,)),
        ]
        + (stage_scratch(ff) + gather_semaphores() if fast else []),
        compiler_params=pltpu.CompilerParams(
            vmem_limit_bytes=VMEM_BYTES,
            **(dict(collective_id=0, has_side_effects=True) if fast else {}),
        ),
    )(*ins)
    return Saved(*outs[: len(K)]), list(outs[len(K) :])


LOADS = (K.dthree, K.joined_low, K.xhat2, K.r2, K.cmixed, K.ck, K.cv, K.cq, K.vision, K.xhat_v, K.cross_in)
LOADS += (K.xhat1, K.r1, K.p_self, K.vec, K.dvec3)
LATE = (K.mixed, K.q, K.k, K.v)


def backward_kernel(fast, *refs):
    count = len(ARRAY_ROWS)
    x_in, refs = refs[0], refs[1:]
    ins, refs = Saved(*refs[: len(K)]), refs[len(K) :]
    weights, refs = (None,) + tuple(refs[: count - 1]), refs[count - 1 :]
    input_grad, refs = refs[0], refs[1:]
    if fast:
        outs, refs = refs[:count], refs[count:]
    else:
        vec_outs, outs, refs = refs[:3], (None,) + tuple(refs[3 : count + 2]), refs[count + 2 :]
    held, refs = dict(zip(LOADS, refs)), refs[len(LOADS) :]
    full, refs = refs[:count], refs[count:]
    dvec, dvec_feat, dvec_ff, dn, dwide, abuf, sbuf, pbuf = refs[:8]
    load_sem, w_sem, g_sem, abuf_sem, sbuf_sem, pbuf_sem = refs[8:14]
    x, dm = abuf.at[0], abuf.at[1]
    half = dn.shape[0] // 2
    dcb, dcm, dcq = sbuf.at[0, pl.ds(0, half)], sbuf.at[0, pl.ds(half, half)], sbuf.at[1, pl.ds(0, half)]
    for i, name in enumerate(LATE):
        held[name] = dwide.at[i]
    loads = {i: pltpu.make_async_copy(ins[i], held[i], load_sem.at[i]) for i in LOADS + LATE}
    loads[X_LOAD] = pltpu.make_async_copy(x_in, x, load_sem.at[K.layer_out])
    for i in range(1, count):
        loads[WEIGHT_LOAD + i] = pltpu.make_async_copy(weights[i], full[i], w_sem.at[i])

    def tile_copies(n, slot):
        return (
            pltpu.make_async_copy(ins.active.at[n], abuf.at[slot], abuf_sem.at[slot]),
            pltpu.make_async_copy(ins.slope.at[n], sbuf.at[slot], sbuf_sem.at[slot]),
        )

    def pair_copy(i, slot):
        return pltpu.make_async_copy(ins.p_cross.at[i], pbuf.at[slot], pbuf_sem.at[slot])

    for i in (K.dthree, WEIGHT_LOAD + 5):
        loads[i].start()
    for copy in tile_copies(0, 0):
        copy.start()
    for i in (K.joined_low, WEIGHT_LOAD + 4) + LOADS[2:5] + (WEIGHT_LOAD + 3,) + LOADS[5:8]:
        loads[i].start()
    pair_copy(0, 0).start()
    for i in (WEIGHT_LOAD + 2,) + LOADS[8:] + (WEIGHT_LOAD + 1,):
        loads[i].start()

    def wait(*names):
        for i in names:
            loads[i].wait()

    def ffn_tile(n):
        @pl.when(n + 1 < ins.active.shape[0])
        def _():
            for copy in tile_copies(n + 1, (n + 1) % 2):
                copy.start()

        for copy in tile_copies(n, n % 2):
            copy.wait()
        return n % 2

    def cross_tile(i):
        @pl.when(i + 1 < ins.p_cross.shape[0])
        def _():
            pair_copy(i + 1, (i + 1) % 2).start()

        pair_copy(i, i % 2).wait()
        return i % 2

    stored = []

    def keep(src, dst, sem):
        copy = pltpu.make_async_copy(src, dst, sem)
        copy.start()
        stored.append(copy)

    if fast:
        reduce = Reduce(full, outs, refs[14:])
        step = reduce.step

        def begin(parts, *arrays):
            reduce.begin(parts)
    else:

        def step():
            pass

        def begin(parts, *arrays):
            for i in arrays:
                keep(full[i], outs[i], g_sem.at[i])

    r = Refs(
        **{Saved._fields[i]: ref for i, ref in held.items()},
        **full_views(full),
        x=x,
        dvec=dvec,
        dvec_feat=dvec_feat,
        dvec_ff=dvec_ff,
        dn=dn,
        dwide=dwide,
        dm=dm,
        dcb=dcb,
        dcm=dcm,
        dcq=dcq,
        active=abuf,
        slope=sbuf,
        p_cross=pbuf,
        wait=wait,
        begin=begin,
        step=step,
        ffn_tile=ffn_tile,
        cross_tile=cross_tile,
    )
    dvec[...] = jnp.zeros_like(dvec)
    dvec_feat[...] = jnp.zeros_like(dvec_feat)
    wait(K.vec, K.dvec3)
    dvec[GAIN_3 : GAIN_3 + 2, :] = held[K.dvec3][0:2, :]
    backward_ffn(r)
    for i in LATE + (X_LOAD,):
        loads[i].start()
    backward_cross(r)
    backward_self(r)
    keep(held[K.dthree], input_grad, g_sem.at[0])
    if fast:
        pack_vectors(full[0], dvec, dvec_feat, dvec_ff)
        reduce.begin(1)
        reduce.end()
    else:
        for src, dst, i in zip((dvec, dvec_feat, dvec_ff), vec_outs, LATE):
            keep(src, dst, load_sem.at[i])
    for copy in stored:
        copy.wait()


def backward_all(fast, saved, weights, x):
    tokens, keys, feat = x.shape[0], saved.vision.shape[0], saved.vision.shape[1]
    count = len(ARRAY_ROWS)
    rows, ff = tokens // 2, 8 * weights[3].shape[3]
    hbm = pl.BlockSpec(memory_space=pl.ANY)
    dma = pltpu.SemaphoreType.DMA
    small = [(16, D), (16, feat), (8, ff)]
    out_shape = [jax.ShapeDtypeStruct((tokens, D), F32)]
    if fast:
        out_shape += [jax.ShapeDtypeStruct((k, n, D), LOW) for k, n in ARRAY_ROWS]
    else:
        out_shape += [jax.ShapeDtypeStruct(s, F32) for s in small]
        out_shape += [jax.ShapeDtypeStruct(w.shape, LOW) for w in weights]
    outs = pl.pallas_call(
        functools.partial(backward_kernel, fast),
        name="backward",
        out_shape=out_shape,
        in_specs=[hbm] * (len(K) + count),
        out_specs=[hbm] * len(out_shape),
        scratch_shapes=[pltpu.VMEM(saved[i].shape, saved[i].dtype) for i in LOADS]
        + [pltpu.VMEM((1, 4, 2, 32, D), LOW)]
        + [pltpu.VMEM(w.shape, LOW) for w in weights]
        + [pltpu.VMEM(s, F32) for s in small]
        + [pltpu.VMEM((tokens, D), LOW), pltpu.VMEM((ff // 768, tokens, 768), LOW)]
        + [
            pltpu.VMEM((2, tokens, 768), LOW),
            pltpu.VMEM((2, tokens, 768), LOW),
            pltpu.VMEM((2, keys, 2 * rows), LOW),
            dma((len(K),)),
            dma((count,)),
            dma((count,)),
            dma((2,)),
            dma((2,)),
            dma((2,)),
        ]
        + (reduce_scratch() if fast else []),
        compiler_params=pltpu.CompilerParams(
            vmem_limit_bytes=VMEM_BYTES,
            **(dict(collective_id=1, has_side_effects=True) if fast else {}),
        ),
    )(x, *saved, *weights)
    return outs[0], list(outs[1:])


def pack_rows(vectors):
    total = jnp.zeros((32, D), vectors[0].dtype)
    for first, last in ((0, VEC_ROWS), (VEC_ROWS, VEC_ROWS + 2), (VEC_ROWS + 2, VEC_ROWS + 3)):
        rows = jnp.stack(vectors[first:last])
        total = total + jnp.pad(rows, ((first, 32 - last), (0, D - rows.shape[1])))
    return total[None]


def local(
    fast,
    hidden,
    image_feats,
    caption_counts,
    text_lengths,
    out_grad,
    self_query,
    query_bias,
    self_key,
    self_value,
    value_bias,
    self_output,
    output_bias,
    first_gain,
    first_shift,
    cross_query,
    crossquery_bias,
    cross_key,
    cross_value,
    crossvalue_bias,
    cross_output,
    crossoutput_bias,
    second_gain,
    second_shift,
    vision_gain,
    vision_shift,
    expand_weight,
    expand_bias,
    contract_weight,
    contract_bias,
    third_gain,
    third_shift,
):
    low = jnp.bfloat16
    vectors = (
        query_bias,
        value_bias,
        output_bias,
        first_gain,
        first_shift,
        crossquery_bias,
        crossvalue_bias,
        crossoutput_bias,
        second_gain,
        second_shift,
        contract_bias,
        third_gain,
        third_shift,
        vision_gain,
        vision_shift,
        expand_bias,
    )
    own = [pack_rows(vectors), self_query, self_key, self_value, self_output]
    own += [cross_key, cross_value, cross_query, cross_output, expand_weight, contract_weight[None]]
    feat = image_feats.shape[-1]
    shards = D // self_query.shape[0]
    whole = ()
    if not fast:
        own = [own[0], jnp.stack(own[1:5]), jnp.stack(own[5:7]), jnp.stack(own[7:9]), own[9].T[None], own[10]]
        full = [lax.all_gather(s, FSDP, axis=1, tiled=False) for s in own]
        rows = full[0][0]
        each = [rows[:, i, : v.shape[0]].reshape(-1).astype(F32) for i, v in enumerate(vectors)]
        own = [f.reshape(f.shape[0], 4, 2, -1, D) for f in full]
        whole = (
            jnp.stack(each[:VEC_ROWS] + [jnp.zeros((D,), F32)] * (16 - VEC_ROWS)),
            jnp.stack(each[VEC_ROWS : VEC_ROWS + 2] + [jnp.zeros((feat,), F32)] * 6),
            jnp.broadcast_to(each[-1][None], (8, each[-1].shape[0])),
        )
    x = hidden.reshape(-1, D)
    saved, weights = forward_all(
        fast,
        caption_counts,
        text_lengths,
        x,
        image_feats,
        out_grad.reshape(-1, D),
        own,
        whole,
    )
    input_grad, summed = backward_all(fast, saved, weights, x)
    layer_out = saved.layer_out.reshape(hidden.shape)
    input_grad = input_grad.reshape(hidden.shape)
    if not fast:
        dvec, dvec_feat, dvec_ff = summed[:3]
        pieces = [dvec[i] for i in range(VEC_ROWS)]
        pieces += [dvec_feat[VEC_ROWS], dvec_feat[VEC_ROWS + 1], dvec_ff[0]]
        pieces = [v.astype(LOW).reshape(shards, -1) for v in pieces]
        pieces = [jnp.pad(v, ((0, 0), (0, D - v.shape[1]))) for v in pieces]
        packed = jnp.stack(pieces + [jnp.zeros((shards, D), LOW)] * (32 - len(pieces)), axis=1)
        grads = [packed[None]] + [g.reshape(g.shape[0], shards, -1, D) for g in summed[3:]]
        summed = [lax.psum_scatter(g, FSDP, scatter_dimension=1, tiled=False) for g in grads]
        summed = [lax.psum(g, DP) for g in summed]
    sums = [s.astype(F32) for s in summed]
    small = [sums[0][0, i, : v.shape[0]] for i, v in enumerate(vectors)]
    return (
        layer_out,
        input_grad,
        sums[1][0],
        small[0],
        sums[1][1],
        sums[1][2],
        small[1],
        sums[1][3],
        small[2],
        small[3],
        small[4],
        sums[3][0],
        small[5],
        sums[2][0],
        sums[2][1],
        small[6],
        sums[3][1],
        small[7],
        small[8],
        small[9],
        small[13],
        small[14],
        sums[4][0].T,
        small[15],
        sums[5][0],
        small[10],
        small[11],
        small[12],
    )


def solution(mesh):
    fast = mesh.shape[DP] == 4 and mesh.shape[FSDP] == 8
    tokens, pair = P((DP, FSDP), None, None), P((DP, FSDP), None)
    by_row, by_column, flat = P(FSDP, None), P(None, FSDP), P(FSDP)
    params = (
        (by_row, flat, by_row, by_row, flat, by_row, flat, flat, flat)
        + (by_row, flat, by_row, by_row, flat, by_row, flat)
        + (flat,) * 4
        + (by_column, flat, by_row, flat, flat, flat)
    )
    return jax.shard_map(
        functools.partial(local, fast),
        mesh=mesh,
        in_specs=(tokens, tokens, pair, P((DP, FSDP)), tokens) + params,
        out_specs=(tokens, tokens) + params,
        check_vma=False,
    )
```
